512 devices in a mesh: row: 64 (over y_lo, z, core), col: 8 (over x, y_hi).
Axes of the slice: x: 4, y: 8 (y_hi: 2, y_lo: 4; y = y_hi * 4 + y_lo), z: 8, core: 2. Of those that a mesh axis runs over, the one named last changes fastest.
Arguments:
- tokens: bfloat16 [1024, 6144], P('row', 'col'), may hold values from -6 to 6
- in_weight: bfloat16 [96, 384], replicated, may hold values from -0.625 to 0.625
- conv_weight: float32 [3, 3, 192], replicated, may hold values from -2 to 2
- conv_bias: float32 [192], replicated, may hold values from -3 to 3
- scan_weight: bfloat16 [4, 192, 35], replicated, may hold values from -0.4375 to 0.4375
- step_bias: float32 [4, 3], replicated, may hold values from -5 to -1.5
- log_decay: float32 [4, 3], replicated, may hold values from -1.5 to 1
- skip_gain: float32 [4, 192], replicated, may hold values from 0.5 to 1.5
- norm_gain: float32 [192], replicated, may hold values from 0.5 to 1.5
- norm_bias: float32 [192], replicated, may hold values from -2 to 2
- out_weight: bfloat16 [192, 96], replicated, may hold values from -0.4375 to 0.4375
- cotangent: bfloat16 [1024, 6144], P('row', 'col'), may hold values from -6 to 6
Outputs:
- output: bfloat16 [1024, 6144], P('row', 'col')
- grad_tokens: bfloat16 [1024, 6144], P('row', 'col')
- grad_in_weight: float32 [96, 384], replicated
- grad_conv_weight: float32 [3, 3, 192], replicated
- grad_conv_bias: float32 [192], replicated
- grad_scan_weight: float32 [4, 192, 35], replicated
- grad_step_bias: float32 [4, 3], replicated
- grad_log_decay: float32 [4, 3], replicated
- grad_skip_gain: float32 [4, 192], replicated
- grad_norm_gain: float32 [192], replicated
- grad_norm_bias: float32 [192], replicated
- grad_out_weight: float32 [192, 96], replicated
The draws below stay inside these ranges and needn't reach their ends.
All inputs are finite; a program needn't handle non-finite values.
Results may differ from the reference program's by a relative error of at most 0.022.
Values may be sent and summed in bfloat16 or wider, within the bound.
No kernel may reach another device: no remote copies, remote signals or barrier semaphores. Data moves between devices by JAX's collectives and lax.ppermute only.
A program may use at most 128 MiB of HBM per device.

```python
import jax
import jax.numpy as jnp
from jax import lax

D = 96
DI = 192
NS = 16
QC = 64
HEADS = 3
H = 1024
W = 64


def level_of(key, extent, cuts, least, top_value):
    def one(dim, shards_of):
        heights = jax.random.uniform(jax.random.fold_in(jax.random.fold_in(key, 6), dim), (shards_of,), jnp.float32, least / len(cuts), top_value / len(cuts))
        return jnp.repeat(jnp.exp(heights), extent[dim] // shards_of).reshape((-1,) + (1,) * (len(extent) - dim - 1))

    loudness = one(*cuts[0])
    for cut in cuts[1:]:
        loudness = loudness * one(*cut)
    return loudness


def noise(stream_key, shape, scale, bound, split=(), held_as=jnp.bfloat16):
    entries = jax.random.normal(stream_key, shape, jnp.float32) * scale
    if len(split) > 0:
        entries = level_of(stream_key, shape, split, -0.22, 0.18) * entries
    return jnp.clip(entries, min=-bound, max=bound).astype(held_as)


def setup_inputs(seed: int = 0) -> dict:
    streams_of = jax.random.split(jax.random.key(seed), 13)
    return {
        "tokens": noise(streams_of[0], (H, W * D), 1.0, 6.0, ((0, 64), (1, 8))),
        "in_weight": noise(streams_of[1], (D, 2 * DI), D ** -0.5, 0.625),
        "conv_weight": noise(streams_of[2], (3, 3, DI), 9 ** -0.5, 2.0, (), jnp.float32),
        "conv_bias": noise(streams_of[3], (DI,), 0.5, 3.0, (), jnp.float32),
        "scan_weight": noise(streams_of[4], (4, DI, HEADS + 2 * NS), DI ** -0.5, 0.4375),
        "step_bias": jnp.clip(jax.random.uniform(streams_of[5], (4, HEADS), jnp.float32, -5.0, -1.5), -5.0, -1.5),
        "log_decay": jnp.clip(jax.random.uniform(streams_of[6], (4, HEADS), jnp.float32, -1.5, 1.0), -1.5, 1.0),
        "skip_gain": jnp.clip(jax.random.uniform(streams_of[7], (4, DI), jnp.float32, 0.5, 1.5), 0.5, 1.5),
        "norm_gain": jnp.clip(1.0 + 0.1 * jax.random.normal(streams_of[8], (DI,), jnp.float32), 0.5, 1.5),
        "norm_bias": noise(streams_of[9], (DI,), 0.3, 2.0, (), jnp.float32),
        "out_weight": noise(streams_of[10], (DI, D), DI ** -0.5, 0.4375),
        "cotangent": noise(streams_of[11], (H, W * D), 1.0, 6.0, ((0, 64), (1, 8))),
    }


highest = lax.Precision.HIGHEST

def to_lines(planes, direction):
    if direction == 1:
        return jnp.flip(planes, 1)
    if direction == 2:
        return jnp.swapaxes(planes, 0, 1)
    if direction == 3:
        return jnp.flip(jnp.swapaxes(planes, 0, 1), 1)
    return planes

def from_lines(planes, direction):
    if direction == 1:
        return jnp.flip(planes, 1)
    if direction == 2:
        return jnp.swapaxes(planes, 0, 1)
    if direction == 3:
        return jnp.swapaxes(jnp.flip(planes, 1), 0, 1)
    return planes

def segment(values, step_size, in_gate, out_gate, decay_rate, window_cap):
    line_count, length, inner_width = values.shape
    head_count = step_size.shape[-1]
    head_dim = inner_width // head_count
    states = in_gate.shape[-1]
    window = min(window_cap, length)
    pieces = length // window
    log_step = step_size * decay_rate
    scaled = (values.reshape(line_count, length, head_count, head_dim) * step_size[..., None]).reshape(line_count, pieces, window, head_count, head_dim)
    log_inner = jnp.cumsum(log_step.reshape(line_count, pieces, window, head_count), axis=2)
    keys_block = in_gate.reshape(line_count, pieces, window, states)
    query_block = out_gate.reshape(line_count, pieces, window, states)
    scores = jnp.einsum('mkqn,mksn->mkqs', query_block, keys_block, precision=highest)
    spread = log_inner[:, :, :, None, :] - log_inner[:, :, None, :, :]
    causal = (jnp.arange(window)[:, None] >= jnp.arange(window)[None, :])[None, None, :, :, None]
    decay_table = jnp.where(causal, jnp.exp(jnp.where(causal, spread, 0.0)), 0.0)
    weights = scores[..., None] * decay_table
    inside = jnp.einsum('mkqsh,mkshp->mkqhp', weights, scaled, precision=highest)
    to_end = jnp.exp(log_inner[:, :, -1:, :] - log_inner)
    block_state = jnp.einsum('mksh,mkshp,mksn->mkhpn', to_end, scaled, keys_block, precision=highest)
    block_log = log_inner[:, :, -1, :]

    def advance(carry_state, step_items):
        contrib, piece_log = step_items
        return (jnp.exp(piece_log)[..., None, None] * carry_state + contrib, carry_state)
    zero_state = jnp.zeros((line_count, head_count, head_dim, states), jnp.float32)
    end_state, incoming = lax.scan(advance, zero_state, (jnp.moveaxis(block_state, 1, 0), jnp.moveaxis(block_log, 1, 0)))
    incoming = jnp.moveaxis(incoming, 0, 1)
    across = jnp.einsum('mkqn,mkqh,mkhpn->mkqhp', query_block, jnp.exp(log_inner), incoming, precision=highest)
    output = (inside + across).reshape(line_count, length, inner_width)
    log_full = jnp.cumsum(log_step, axis=1)
    return (output, end_state, log_full)

def line_outputs(values, raw_proj, step_shift, log_rate, direction):
    line_values = to_lines(values, direction)
    line_raw = to_lines(raw_proj, direction)
    line_count, length, inner_width = line_values.shape
    proj_width = line_raw.shape[-1]
    head_count = step_shift.shape[0]
    states = (proj_width - head_count) // 2
    group_size = 16

    def one_group(group_items):
        group_values, group_raw = group_items
        step_size = jax.nn.softplus(group_raw[..., :head_count] + step_shift)
        return segment(group_values, step_size, group_raw[..., head_count:head_count + states], group_raw[..., head_count + states:], -jnp.exp(log_rate), QC)[0]
    grouped = lax.map(jax.checkpoint(one_group), (line_values.reshape(line_count // group_size, group_size, length, inner_width), line_raw.reshape(line_count // group_size, group_size, length, proj_width)))
    return from_lines(grouped.reshape(line_count, length, inner_width), direction)

def scan_all(values, raw_all, step_bias, log_decay, skip_gain):
    summed = jnp.zeros_like(values)
    for direction in range(4):
        summed = summed + line_outputs(values, raw_all[direction], step_bias[direction], log_decay[direction], direction) + skip_gain[direction] * values
    return summed

def depthwise(padded, kernel, height, width):
    accumulated = jnp.zeros((height, width, kernel.shape[-1]), jnp.float32)
    for offset_row in range(3):
        for offset_col in range(3):
            accumulated = accumulated + kernel[offset_row, offset_col] * padded[offset_row:offset_row + height, offset_col:offset_col + width]
    return accumulated

def flipped(padded_grad, kernel, height, width):
    accumulated = jnp.zeros((height, width, kernel.shape[-1]), jnp.float32)
    for offset_row in range(3):
        for offset_col in range(3):
            accumulated = accumulated + kernel[offset_row, offset_col] * padded_grad[2 - offset_row:2 - offset_row + height, 2 - offset_col:2 - offset_col + width]
    return accumulated

def kernel_grads(grad_wide, padded, height, width):
    kernel_rows = []
    for offset_row in range(3):
        for offset_col in range(3):
            kernel_rows.append(lax.optimization_barrier(jnp.sum(grad_wide * padded[offset_row:offset_row + height, offset_col:offset_col + width], axis=(0, 1))))
    return (jnp.stack(kernel_rows).reshape(3, 3, -1), lax.optimization_barrier(jnp.sum(grad_wide, axis=(0, 1))))

def post_norm(summed, gate_wide, norm_gain, norm_bias):
    center = summed - lax.optimization_barrier(jnp.mean(summed, axis=-1, keepdims=True))
    spread = lax.optimization_barrier(jnp.mean(center * center, axis=-1, keepdims=True))
    normed = center * lax.rsqrt(spread + 1e-05) * norm_gain + norm_bias
    return normed * gate_wide * jax.nn.sigmoid(gate_wide)

def reference(tokens, in_weight, conv_weight, conv_bias, scan_weight, step_bias, log_decay, skip_gain, norm_gain, norm_bias, out_weight, cotangent):
    height = tokens.shape[0]
    width = tokens.shape[1] // D
    block_in = tokens.reshape(height, width, D).astype(jnp.float32)
    projected = jnp.einsum('rcd,de->rce', block_in, in_weight.astype(jnp.float32))
    branch = projected[..., :DI].astype(jnp.bfloat16)
    gate_in = projected[..., DI:].astype(jnp.bfloat16)
    padded = jnp.pad(branch, ((1, 1), (1, 1), (0, 0)))
    before = depthwise(padded, conv_weight, height, width) + conv_bias
    sigmoid_pre = jax.nn.sigmoid(before)
    activated = (before * sigmoid_pre).astype(jnp.bfloat16)
    wide_act = lax.optimization_barrier(activated).astype(jnp.float32)
    scan_wide = scan_weight.astype(jnp.float32)
    raw_all = jnp.einsum('rci,kij->krcj', wide_act, scan_wide)
    summed, pull_scan = jax.vjp(scan_all, wide_act, raw_all, step_bias, log_decay, skip_gain)
    gate_wide = lax.optimization_barrier(gate_in).astype(jnp.float32)
    gated_out, pull_post = jax.vjp(post_norm, summed, gate_wide, norm_gain, norm_bias)
    gated_low = gated_out.astype(jnp.bfloat16)
    gated_wide = lax.optimization_barrier(gated_low).astype(jnp.float32)
    out_wide = out_weight.astype(jnp.float32)
    output = jnp.einsum('rci,id->rcd', gated_wide, out_wide).astype(jnp.bfloat16)
    back_in = cotangent.reshape(height, width, D).astype(jnp.float32)
    grad_gated = jnp.einsum('rcd,id->rci', back_in, out_wide)
    grad_out = jnp.einsum('rci,rcd->id', gated_wide, back_in)
    grad_sum, grad_gate, grad_gain, grad_shift = pull_post(grad_gated)
    grad_low = grad_sum.astype(jnp.bfloat16)
    grad_wide = lax.optimization_barrier(grad_low).astype(jnp.float32)
    grad_values, grad_raw, grad_bias, grad_rate, grad_skip = pull_scan(grad_wide)
    raw_low = lax.optimization_barrier(grad_raw.astype(jnp.bfloat16)).astype(jnp.float32)
    grad_act = grad_values + jnp.einsum('krcj,kij->rci', raw_low, scan_wide)
    grad_scan = jnp.einsum('rci,krcj->kij', wide_act, raw_low)
    grad_before = (grad_act * sigmoid_pre * (1.0 + before * (1.0 - sigmoid_pre))).astype(jnp.bfloat16)
    before_wide = lax.optimization_barrier(grad_before).astype(jnp.float32)
    grad_padded = jnp.pad(grad_before, ((1, 1), (1, 1), (0, 0)))
    grad_branch = flipped(grad_padded, conv_weight, height, width)
    grad_kernel, grad_cbias = kernel_grads(before_wide, padded, height, width)
    grad_mixed = jnp.concatenate([grad_branch, grad_gate], axis=-1).astype(jnp.bfloat16)
    mixed_wide = lax.optimization_barrier(grad_mixed).astype(jnp.float32)
    grad_tokens = jnp.einsum('rce,de->rcd', mixed_wide, in_weight.astype(jnp.float32)).astype(jnp.bfloat16)
    grad_in = jnp.einsum('rcd,rce->de', block_in, mixed_wide)
    scale = float(height * width) ** (-0.5)
    return (output.reshape(height, width * D), grad_tokens.reshape(height, width * D), grad_in * scale, grad_kernel * scale, grad_cbias * scale, grad_scan * scale, grad_bias * scale, grad_rate * scale, grad_skip * scale, grad_gain * scale, grad_shift * scale, grad_out * scale)
```

```python
from functools import partial

import jax
import jax.numpy as jnp
from jax import lax
from jax.experimental import pallas as pl
from jax.experimental.pallas import tpu as pltpu
from jax.sharding import PartitionSpec as P

D = 96
DI = 192
NS = 16
HEADS = 3
R = 16
C = 8
T = R * C
PITCH = 16

F32 = jnp.float32
BF = jnp.bfloat16
HI = lax.Precision.HIGHEST
FAR = -1e30


def dot(a, b, ca=1, cb=0, precision=None):
    return lax.dot_general(
        a, b, (((ca,), (cb,)), ((), ())), precision=precision, preferred_element_type=F32
    )


def iota(shape, dim):
    return lax.broadcasted_iota(jnp.int32, shape, dim)


def mask(k):
    t, s = (iota((T, T), 0), iota((T, T), 1))
    rt, ct, rs, cs = (t >> 3, t & 7, s >> 3, s & 7)
    if k == 0:
        return (rt == rs) & (cs <= ct)
    if k == 1:
        return (rt == rs) & (cs >= ct)
    if k == 2:
        return (ct == cs) & (rs <= rt)
    return (ct == cs) & (rs >= rt)


def same_line(vertical):
    t, s = (iota((T, T), 0), iota((T, T), 1))
    return (t & 7) == (s & 7) if vertical else (t >> 3) == (s >> 3)


def pick_lanes(parts):
    lane = iota((T, T), 1) // 3
    out = parts[3]
    for k in range(3):
        out = jnp.where(lane == k, parts[k], out)
    return out


def as_f32(m):
    return jnp.where(m, 1.0, 0.0).astype(F32)


def lines_of(k):
    return R if k < 2 else C


def half_of(k):
    return lines_of(k) * 8


def spread_states(bc, k):
    lines, half = (lines_of(k), half_of(k))
    i, j = (iota((T, 2 * half), 0), iota((T, 2 * half), 1))
    n = 2 * (j & 7) + j // half
    wide = dot(bc, as_f32(i == 16 * k + n), precision=HI)
    return jnp.where(on_line(k), wide, 0.0)


def on_line(k):
    lines, half = (lines_of(k), half_of(k))
    t, j = (iota((T, 2 * half), 0), iota((T, 2 * half), 1))
    line = t >> 3 if k < 2 else t & 7
    return ((j >> 3) & (lines - 1)) == line


def gather_states(wide, k):
    half = half_of(k)
    j, i = (iota((2 * half, T), 0), iota((2 * half, T), 1))
    n = 2 * (j & 7) + j // half
    return dot(jnp.where(on_line(k), wide, 0.0), as_f32(i == 16 * k + n), precision=HI)


def by_head(values, k):
    lane = iota((T, DI), 1)
    a, b, c = (values[:, 3 * k + h : 3 * k + h + 1] for h in range(HEADS))
    return jnp.where(lane < 64, a, jnp.where(lane < 128, b, c))


def head_sum(wide, k):
    c, j = (iota((DI, T), 0), iota((DI, T), 1))
    return dot(wide, as_f32(j == 3 * k + c // 64), precision=HI)


def per_head(f):
    lane = iota((T, DI), 1)
    a, b, c = (f(h) for h in range(HEADS))
    return jnp.where(lane < 64, a, jnp.where(lane < 128, b, c))


def write_message(ref, states, totals, k_first):
    half = half_of(k_first)
    for d in range(2):
        s = states[d]
        for h in range(HEADS):
            ref[:, d * 3 + h, :] = jnp.concatenate(
                [s[:half, 64 * h : 64 * h + 64], s[half:, 64 * h : 64 * h + 64]], axis=1
            )
    j, t = (iota((half, T), 0), iota((half, T), 1))
    sel = as_f32(t == ((j >> 3) if k_first == 2 else (j >> 3) * 8))
    if k_first == 2:
        i, o = (iota((T, T), 0), iota((T, T), 1))
        totals = dot(totals, as_f32(i == o + 6), precision=HI)
    ref[:, 6, :] = dot(sel, totals, precision=HI)
    ref[:, 7, :] = jnp.zeros((half, T), F32)


def read_message(ref, d):
    x = [ref[:, d * 3 + h, :] for h in range(HEADS)]
    top = jnp.concatenate([v[:, :64] for v in x], axis=1)
    bottom = jnp.concatenate([v[:, 64:] for v in x], axis=1)
    return jnp.concatenate([top, bottom], axis=0)


def chain_kernel(backward, got_ref, out_ref):
    n, m = (got_ref.shape[0], got_ref.shape[1])
    sub = iota((m, 8, 128), 1)
    lane = iota((m, 8, 128), 2)
    ahead = sub < 3 if not backward else sub >= 3

    def factor(i):
        row = jnp.broadcast_to(got_ref[i, :, 6:7, :], (m, 8, 128))
        return jnp.sum(jnp.where(lane == sub, row, 0.0), axis=2, keepdims=True)

    up = jnp.zeros((m, 8, 128), F32)
    for i in range(n):
        out_ref[i] = up
        if i < n - 1:
            up = factor(i) * up + got_ref[i]
    down = jnp.zeros((m, 8, 128), F32)
    for i in range(n - 1, -1, -1):
        out_ref[i] = jnp.where(ahead, out_ref[i], down)
        if i > 0:
            down = factor(i) * down + got_ref[i]


def sigmoid(x):
    return jax.nn.sigmoid(x)


def softplus(x):
    return jnp.maximum(x, 0.0) + jnp.log1p(jnp.exp(-jnp.abs(x)))


def conv_in(tok_ref, wbr_ref):
    branch = dot(tok_ref[...], wbr_ref[...]).astype(BF).astype(F32)
    return branch.reshape(R + 2, PITCH, DI)


def first_kernel(
    tok_ref, wbr_ref, cw_ref, cb_ref, wd_ref, wbc_ref, sb_ref, ld_ref,
    before_ref, act_ref, rawd_ref, bc_ref, step_ref, log_ref, tot_ref, mv_ref, mh_ref,
):
    padded = conv_in(tok_ref, wbr_ref)
    total = jnp.zeros((R, C, DI), F32)
    for b in range(3):
        shifted = padded[:, b : b + C, :]
        for a in range(3):
            total = total + cw_ref[3 * a + b : 3 * a + b + 1, :] * shifted[a : a + R]
    before = total.reshape(T, DI) + cb_ref[...]
    act = (before * sigmoid(before)).astype(BF)
    before_ref[...] = before
    act_ref[...] = act
    raw_d = dot(act, wd_ref[...])
    bc = dot(act, wbc_ref[...])
    step = softplus(raw_d + sb_ref[...])
    log_step = step * -jnp.exp(ld_ref[...])
    log = pick_lanes([dot(as_f32(mask(k)), log_step, precision=HI) for k in range(4)])
    rows, cols = (dot(as_f32(same_line(v)), log_step, precision=HI) for v in (False, True))
    tot = pick_lanes([rows, rows, cols, cols])
    rawd_ref[...] = raw_d
    bc_ref[...] = bc
    step_ref[...] = step
    log_ref[...] = log
    tot_ref[...] = tot
    weight = jnp.exp(tot - log) * step
    wide = act.astype(F32)
    states = [
        dot(spread_states(bc, k), by_head(weight, k) * wide, 0, 0, HI) for k in range(4)
    ]
    factor = jnp.exp(tot)
    write_message(mv_ref, states[2:], factor, 2)
    write_message(mh_ref, states[:2], factor, 0)


def tables(k, bc, out_gate):
    lane = iota((T, T), 1) >> 4
    return dot(jnp.where(lane == k, out_gate, 0.0), bc, 1, 1, HI)


def decay(k, h, log, log_t):
    i = 3 * k + h
    return jnp.exp(jnp.where(mask(k), log[:, i : i + 1] - log_t[i : i + 1, :], FAR))


def shifted_gate(bc):
    return pltpu.roll(bc, 64, 1)


def local_kernel(act_ref, bc_ref, step_ref, log_ref, y_ref):
    bc = bc_ref[...]
    out_gate = shifted_gate(bc)
    log = log_ref[...]
    log_t, step_t = (log.T, step_ref[...].T)
    weights = [jnp.zeros((T, T), F32)] * HEADS
    for k in range(4):
        scores = tables(k, bc, out_gate)
        for h in range(HEADS):
            i = 3 * k + h
            weights[h] = weights[h] + scores * (
                decay(k, h, log, log_t) * step_t[i : i + 1, :]
            )
    wide = act_ref[...].astype(F32)
    y_ref[...] = per_head(lambda h: dot(weights[h], wide, precision=HI))


def carry(k, out_gate, exp_log, state):
    return by_head(exp_log, k) * dot(spread_states(out_gate, k), state, precision=HI)


def norm_kernel(
    y_ref, act_ref, bc_ref, log_ref, tot_ref, sv_ref, sh_ref, skip_ref, tok_ref, wg_ref, gain_ref,
    nb_ref, ow_ref, cot_ref,
    out_ref, g_ref, dgate_ref, gated_ref, norms_ref, mv_ref, mh_ref,
):
    bc = bc_ref[...]
    out_gate = shifted_gate(bc)
    exp_log = jnp.exp(log_ref[...])
    summed = y_ref[...] + skip_ref[...] * act_ref[...].astype(F32)
    for k in range(4):
        state = read_message(sh_ref if k < 2 else sv_ref, k % 2)
        summed = summed + carry(k, out_gate, exp_log, state)
    gate = dot(tok_ref[...], wg_ref[...]).astype(BF).astype(F32)
    sig = sigmoid(gate)
    center = summed - jnp.mean(summed, axis=1, keepdims=True)
    inv = lax.rsqrt(jnp.mean(center * center, axis=1, keepdims=True) + 1e-5)
    unit = center * inv
    normed = unit * gain_ref[...] + nb_ref[...]
    gated = (normed * gate * sig).astype(BF)
    gated_ref[...] = gated
    out_ref[...] = dot(gated, ow_ref[...]).astype(BF)
    grad = dot(cot_ref[...], ow_ref[...], 1, 1)
    dnormed = grad * gate * sig
    dgate_ref[...] = (grad * normed * (sig * (1.0 + gate * (1.0 - sig)))).astype(BF)
    norms_ref[0:1, :] = jnp.sum(dnormed * unit, axis=0, keepdims=True)
    norms_ref[1:2, :] = jnp.sum(dnormed, axis=0, keepdims=True)
    dunit = dnormed * gain_ref[...]
    g = inv * (
        dunit
        - jnp.mean(dunit, axis=1, keepdims=True)
        - unit * jnp.mean(dunit * unit, axis=1, keepdims=True)
    )
    g = g.astype(BF)
    g_ref[...] = g
    g = g.astype(F32)
    states = [
        dot(spread_states(out_gate, k), by_head(exp_log, k) * g, 0, 0, HI) for k in range(4)
    ]
    factor = jnp.exp(tot_ref[...])
    write_message(mv_ref, states[2:], factor, 2)
    write_message(mh_ref, states[:2], factor, 0)


def back_kernel(
    act_ref, bc_ref, step_ref, log_ref, g_ref, sv_ref, sh_ref,
    dact_ref, dbc_ref, dstep_ref, dlog_ref,
):
    bc = bc_ref[...]
    out_gate = shifted_gate(bc)
    log = log_ref[...]
    step = step_ref[...]
    log_t, step_t = (log.T, step.T)
    exp_log = jnp.exp(log)
    act = act_ref[...]
    g = g_ref[...]
    gw = g.astype(F32)
    lane = iota((T, DI), 1) // 64
    lane16 = iota((T, T), 1) >> 4
    lane1 = iota((T, T), 1)
    pair = [dot(jnp.where(lane == h, g, jnp.zeros_like(g)), act, 1, 1) for h in range(HEADS)]
    weights = [jnp.zeros((T, T), F32)] * HEADS
    d_in = jnp.zeros((T, T), F32)
    d_out = jnp.zeros((T, T), F32)
    row_sums = jnp.zeros((T, T), F32)
    step_rows = []
    for k in range(4):
        scores = tables(k, bc, out_gate)
        d_scores = jnp.zeros((T, T), F32)
        for h in range(HEADS):
            i = 3 * k + h
            dec = decay(k, h, log, log_t)
            dec_step = dec * step_t[i : i + 1, :]
            weights[h] = weights[h] + scores * dec_step
            d_scores = d_scores + pair[h] * dec_step
            d_step = pair[h] * dec * scores
            step_rows.append(jnp.sum(d_step, axis=0, keepdims=True))
            rows = jnp.sum(d_step * step_t[i : i + 1, :], axis=1, keepdims=True)
            row_sums = jnp.where(lane1 == i, rows, row_sums)
        d_out = d_out + dot(d_scores, jnp.where(lane16 == k, bc, 0.0), precision=HI)
        d_in = d_in + dot(d_scores, jnp.where(lane16 == k, out_gate, 0.0), 0, 0, HI)
        state = read_message(sh_ref if k < 2 else sv_ref, k % 2)
        expg = by_head(exp_log, k) * gw
        carried = dot(spread_states(out_gate, k), state, precision=HI)
        row_sums = row_sums + head_sum(carried * expg, k)
        d_out = d_out + gather_states(dot(expg, state, 1, 1, HI), k)
    d_step = jnp.concatenate(step_rows + [jnp.zeros((T - 12, T), F32)], axis=0).T
    dact_ref[...] = per_head(lambda h: dot(weights[h], gw, 0, 0, HI))
    dbc_ref[...] = d_in + pltpu.roll(d_out, 64, 1)
    dstep_ref[...] = d_step
    dlog_ref[...] = row_sums - step * d_step


def gate_grads_kernel(tok_ref, dgate_ref, gated_ref, cot_ref, gin_ref, gout_ref):
    gin_ref[...] = dot(tok_ref[...], dgate_ref[...], 0, 0)
    gout_ref[...] = dot(cot_ref[...], gated_ref[...], 0, 0)


def last_kernel(
    tok_ref, wbr_ref, cw_ref, before_ref, act_ref, rawd_ref, bc_ref, step_ref, log_ref, tot_ref, g_ref,
    sv_ref, sh_ref, lv_ref, lh_ref, dact_ref, dbc_ref, dstep_ref, dlog_ref, skip_ref, wd_ref, wbc_ref,
    sb_ref, ld_ref, gin_gate_ref, gout_ref, norms_ref,
    gb_ref, pack_ref,
):
    step, log, tot, bc = (step_ref[...], log_ref[...], tot_ref[...], bc_ref[...])
    act = act_ref[...]
    wide = act.astype(F32)
    g = g_ref[...].astype(F32)
    d_act = dact_ref[...] + skip_ref[...] * g
    d_bc = dbc_ref[...]
    to_end = jnp.exp(tot - log)
    weight = to_end * step
    through = jnp.exp(tot)
    inner = jnp.zeros((T, T), F32)
    cross = jnp.zeros((T, T), F32)
    for k in range(4):
        later = read_message(lh_ref if k < 2 else lv_ref, k % 2)
        earlier = read_message(sh_ref if k < 2 else sv_ref, k % 2)
        reach = dot(spread_states(bc, k), later, precision=HI)
        wk = by_head(weight, k)
        d_act = d_act + wk * reach
        inner = inner + head_sum(wide * reach, k)
        d_bc = d_bc + gather_states(dot(wk * wide, later, 1, 1, HI), k)
        cross = cross + dot(as_f32(on_line(k)), head_sum(later * earlier, k), precision=HI)
    d_step = dstep_ref[...] + to_end * inner
    left = weight * inner
    d_log = dlog_ref[...]
    parts = []
    for k in range(4):
        m = as_f32(mask(k))
        rest = as_f32(same_line(k >= 2)) - m.T
        parts.append(dot(m, d_log, 0, 0, HI) + dot(rest, left, precision=HI))
    d_log_step = pick_lanes(parts) + cross * through
    rate = -jnp.exp(ld_ref[...])
    d_rate = jnp.sum(d_log_step * step, axis=0, keepdims=True) * rate
    d_raw = (d_step + rate * d_log_step) * sigmoid(rawd_ref[...] + sb_ref[...])
    live = iota((T, T), 1) < 12
    d_raw = jnp.where(live, d_raw, 0.0)
    d_bias = jnp.sum(d_raw, axis=0, keepdims=True)
    d_raw = d_raw.astype(BF)
    d_bc = d_bc.astype(BF)
    d_act = d_act + dot(d_raw, wd_ref[...], 1, 1) + dot(d_bc, wbc_ref[...], 1, 1)
    before = before_ref[...]
    sig = sigmoid(before)
    gb = (d_act * sig * (1.0 + before * (1.0 - sig))).astype(BF)
    gb_ref[...] = gb
    gbw = gb.astype(F32)
    padded = conv_in(tok_ref, wbr_ref)
    tok = tok_ref[...].astype(F32).reshape(R + 2, PITCH, D)
    gin = jnp.zeros((D, DI), F32)
    conv_rows = [None] * 9
    for b in range(3):
        near = padded[:, b : b + C, :]
        near_tok = tok[:, b : b + C, :]
        for a in range(3):
            i = 3 * a + b
            conv_rows[i] = jnp.sum(gbw * near[a : a + R].reshape(T, DI), axis=0, keepdims=True)
            gin = gin + cw_ref[i : i + 1, :] * dot(
                near_tok[a : a + R].reshape(T, D).astype(BF), gb, 0, 0
            )
    wide_row = lambda x: jnp.concatenate([x, jnp.zeros((1, DI - T), F32)], axis=1)
    small = jnp.concatenate(
        conv_rows
        + [
            jnp.sum(gbw, axis=0, keepdims=True),
            jnp.sum(g * wide, axis=0, keepdims=True),
            norms_ref[0:1, :],
            norms_ref[1:2, :],
            wide_row(d_bias),
            wide_row(jnp.where(live[:1], d_rate, 0.0)),
            jnp.zeros((1, DI), F32),
        ],
        axis=0,
    )
    both = [
        gin, gin_gate_ref[...], gout_ref[...], small, dot(d_bc, act, 0, 0),
        dot(d_raw, act, 0, 0)[:16],
    ]
    full = jnp.concatenate(both, axis=0)
    pack_ref[0:448, :] = full[:, :128]
    pack_ref[448:672, :] = jnp.concatenate([full[:224, 128:], full[224:, 128:]], axis=1)


def out_kernel(gb_ref, cw_ref, dgate_ref, wbr_ref, wg_ref, out_ref):
    padded = gb_ref[...].astype(F32).reshape(R + 2, PITCH, DI)
    total = jnp.zeros((R, C, DI), F32)
    for b in range(3):
        shifted = padded[:, 2 - b : 2 - b + C, :]
        for a in range(3):
            total = total + cw_ref[3 * a + b : 3 * a + b + 1, :] * shifted[2 - a : 2 - a + R]
    d_branch = total.reshape(T, DI).astype(BF)
    out_ref[...] = (
        dot(d_branch, wbr_ref[...], 1, 1) + dot(dgate_ref[...], wg_ref[...], 1, 1)
    ).astype(BF)


def call(kernel, outs, *args, flops=10**8):
    whole = pl.BlockSpec(memory_space=pltpu.VMEM)
    return pl.pallas_call(
        kernel,
        out_shape=[jax.ShapeDtypeStruct(s, t) for s, t in outs],
        in_specs=[whole] * len(args),
        out_specs=[whole] * len(outs),
        compiler_params=pltpu.CompilerParams(vmem_limit_bytes=40 * 2**20),
        cost_estimate=pl.CostEstimate(flops=flops, bytes_accessed=10**6, transcendentals=0),
    )(*args)


def shift_over(x, axes, steps):
    sizes = [lax.axis_size(a) for a in axes]
    pairs = []
    if len(axes) == 1:
        for i in range(sizes[0]):
            if 0 <= i + steps[0] < sizes[0]:
                pairs.append((i + steps[0], i))
        return lax.ppermute(x, axes[0], pairs)
    for i in range(sizes[0]):
        for j in range(sizes[1]):
            a, b = (i + steps[0], j + steps[1])
            if 0 <= a < sizes[0] and 0 <= b < sizes[1]:
                pairs.append((a * sizes[1] + b, i * sizes[1] + j))
    return lax.ppermute(x, axes, pairs)


def with_rim(x):
    both = ("row", "col")
    up = shift_over(x[-1:], ("row",), (-1,))
    down = shift_over(x[:1], ("row",), (1,))
    left = shift_over(x[:, -1:], ("col",), (-1,))
    right = shift_over(x[:, :1], ("col",), (1,))
    corner = {
        (i, j): shift_over(
            x[-1:, -1:] if (i, j) == (-1, -1)
            else x[-1:, :1] if (i, j) == (-1, 1)
            else x[:1, -1:] if (i, j) == (1, -1)
            else x[:1, :1],
            both,
            (i, j),
        )
        for i in (-1, 1)
        for j in (-1, 1)
    }
    top = jnp.concatenate([corner[-1, -1], up, corner[-1, 1]], axis=1)
    mid = jnp.concatenate([left, x, right], axis=1)
    low = jnp.concatenate([corner[1, -1], down, corner[1, 1]], axis=1)
    full = jnp.concatenate([top, mid, low], axis=0)
    full = jnp.pad(full, ((0, 0), (0, PITCH - C - 2), (0, 0)))
    return full.reshape((R + 2) * PITCH, x.shape[-1])


def exchange(message, axis, backward):
    size = lax.axis_size(axis)
    got = lax.all_to_all(message, axis, 0, 0, tiled=True)
    shape = (size, message.shape[0] // size, 8, 128)
    (states,) = call(partial(chain_kernel, backward), [(shape, F32)], got.reshape(shape), flops=10**7)
    return lax.all_to_all(states.reshape(message.shape), axis, 0, 0, tiled=True)


def local(
    tokens, in_weight, conv_weight, conv_bias, scan_weight, step_bias, log_decay, skip_gain, norm_gain,
    norm_bias, out_weight, cotangent,
):
    own = tokens.reshape(T, D)
    halo = with_rim(tokens.reshape(R, C, D))
    cot = cotangent.reshape(T, D)
    w_branch, w_gate = (in_weight[:, :DI], in_weight[:, DI:])
    taps = jnp.pad(conv_weight.reshape(9, DI), ((0, 7), (0, 0)))
    by_channel = jnp.moveaxis(scan_weight, 1, 0)
    w_step = jnp.pad(by_channel[:, :, :HEADS].reshape(DI, 12), ((0, 0), (0, 116)))
    w_bc = jnp.concatenate(
        [
            by_channel[:, :, HEADS : HEADS + NS].reshape(DI, 64),
            by_channel[:, :, HEADS + NS :].reshape(DI, 64),
        ],
        axis=1,
    )
    row = lambda x: x.reshape(1, -1)
    bias = jnp.pad(row(step_bias), ((0, 0), (0, 116)))
    rate = jnp.pad(row(log_decay), ((0, 0), (0, 116)))
    skip = row(jnp.sum(skip_gain, axis=0))
    square = ((T, T), F32)
    wide = ((T, DI), F32)
    low = ((T, DI), BF)
    msg_v, msg_h = (((64, 8, 128), F32), ((128, 8, 128), F32))

    before, act, raw_d, bc, step, log, tot, mv, mh = call(
        first_kernel, [wide, low, square, square, square, square, square, msg_v, msg_h],
        halo, w_branch, taps, row(conv_bias), w_step, w_bc, bias, rate,
    )
    sv = exchange(mv, "row", False)
    sh = exchange(mh, "col", False)
    (y,) = call(local_kernel, [wide], act, bc, step, log)
    out, g, d_gate, gated, norms, mv, mh = call(
        norm_kernel, [((T, D), BF), low, low, low, ((8, DI), F32), msg_v, msg_h],
        y, act, bc, log, tot, sv, sh, skip, own, w_gate, row(norm_gain), row(norm_bias), out_weight, cot,
    )
    lv = exchange(mv, "row", True)
    lh = exchange(mh, "col", True)
    d_act, d_bc, d_step, d_log = call(
        back_kernel, [wide, square, square, square], act, bc, step, log, g, sv, sh
    )
    gin_gate, gout = call(
        gate_grads_kernel, [((D, DI), F32), ((D, DI), F32)], own, d_gate, gated, cot, flops=10**7
    )
    gb, pack = call(
        last_kernel, [low, ((672, 128), F32)],
        halo, w_branch, taps, before, act, raw_d, bc, step, log, tot, g, sv, sh, lv, lh, d_act, d_bc, d_step,
        d_log, skip, w_step, w_bc, bias, rate, gin_gate, gout, norms,
    )
    total = lax.psum(pack, ("row", "col"))
    gb_halo = with_rim(gb.reshape(R, C, DI))
    (d_tokens,) = call(out_kernel, [((T, D), BF)], gb_halo, taps, d_gate, w_branch, w_gate)
    scale = float(T * lax.axis_size("row") * lax.axis_size("col")) ** (-0.5)
    total = total * scale
    full = jnp.concatenate(
        [total[:448], jnp.concatenate([total[448:, :64], total[448:, 64:]], axis=0)], axis=1
    )
    small = full[288:304]
    g_bc = full[304:432].reshape(2, 4, NS, DI)
    g_step = full[432:444].reshape(4, HEADS, DI)
    g_scan = jnp.concatenate([g_step, g_bc[0], g_bc[1]], axis=1)
    return (
        out.reshape(R, C * D),
        d_tokens.reshape(R, C * D),
        jnp.concatenate([full[:96], full[96:192]], axis=1),
        small[:9].reshape(3, 3, DI),
        small[9],
        jnp.swapaxes(g_scan, 1, 2),
        small[13, :12].reshape(4, HEADS),
        small[14, :12].reshape(4, HEADS),
        jnp.broadcast_to(small[10], (4, DI)),
        small[11],
        small[12],
        full[192:288].T,
    )


def solution(mesh):
    in_specs = (P("row", "col"), P(), P(), P(), P(), P(), P(), P(), P(), P(), P(), P("row", "col"))
    out_specs = (P("row", "col"), P("row", "col"), P(), P(), P(), P(), P(), P(), P(), P(), P(), P())
    return jax.shard_map(local, mesh=mesh, in_specs=in_specs, out_specs=out_specs, check_vma=False)
```

```python
from functools import partial

import jax
import jax.numpy as jnp
from jax import lax
from jax.experimental import pallas as pl
from jax.experimental.pallas import tpu as pltpu
from jax.sharding import PartitionSpec as P

D = 96
DI = 192
NS = 16
HEADS = 3
R = 16
C = 8
T = R * C
PITCH = 16
SPAN = 80

F32 = jnp.float32
BF = jnp.bfloat16
HI = lax.Precision.HIGHEST
FAR = -1e30


def dot(a, b, ca=1, cb=0, precision=None):
    return lax.dot_general(
        a, b, (((ca,), (cb,)), ((), ())), precision=precision, preferred_element_type=F32
    )


def iota(shape, dim):
    return lax.broadcasted_iota(jnp.int32, shape, dim)


def mask(k):
    t, s = (iota((T, T), 0), iota((T, T), 1))
    rt, ct, rs, cs = (t >> 3, t & 7, s >> 3, s & 7)
    if k == 0:
        return (rt == rs) & (cs <= ct)
    if k == 1:
        return (rt == rs) & (cs >= ct)
    if k == 2:
        return (ct == cs) & (rs <= rt)
    return (ct == cs) & (rs >= rt)


def same_line(vertical):
    t, s = (iota((T, T), 0), iota((T, T), 1))
    return (t & 7) == (s & 7) if vertical else (t >> 3) == (s >> 3)


def pick_lanes(parts):
    lane = iota((T, T), 1) // 3
    out = parts[3]
    for k in range(3):
        out = jnp.where(lane == k, parts[k], out)
    return out


def as_f32(m):
    return jnp.where(m, 1.0, 0.0).astype(F32)


def states_of(k):
    return 256 if k < 2 else 128


def line_and_entry(j, k):
    if k < 2:
        return (j >> 4, j & 15)
    return ((j >> 3) & 7, 2 * (j & 7) + (j >> 6))


def on_line(k):
    t, j = (iota((T, states_of(k)), 0), iota((T, states_of(k)), 1))
    return line_and_entry(j, k)[0] == (t >> 3 if k < 2 else t & 7)


def spread_states(bc, k):
    i, j = (iota((T, states_of(k)), 0), iota((T, states_of(k)), 1))
    wide = dot(bc, as_f32(i == 16 * k + line_and_entry(j, k)[1]), precision=HI)
    return jnp.where(on_line(k), wide, 0.0)


def gather_states(wide, k):
    j, i = (iota((states_of(k), T), 0), iota((states_of(k), T), 1))
    entry = line_and_entry(j, k)[1]
    return dot(jnp.where(on_line(k), wide, 0.0), as_f32(i == 16 * k + entry), precision=HI)


def by_head(values, k):
    lane = iota((T, DI), 1)
    a, b, c = (values[:, 3 * k + h : 3 * k + h + 1] for h in range(HEADS))
    return jnp.where(lane < 64, a, jnp.where(lane < 128, b, c))


def head_sum(wide, k):
    c, j = (iota((DI, T), 0), iota((DI, T), 1))
    return dot(wide, as_f32(j == 3 * k + c // 64), precision=HI)


def per_head(f):
    lane = iota((T, DI), 1)
    a, b, c = (f(h) for h in range(HEADS))
    return jnp.where(lane < 64, a, jnp.where(lane < 128, b, c))


def write_message(ref, states, totals):
    for d in range(2):
        s = states[d]
        for h in range(HEADS):
            ref[:, d * 3 + h, :] = jnp.concatenate(
                [s[:64, 64 * h : 64 * h + 64], s[64:, 64 * h : 64 * h + 64]], axis=1
            )
    j, t = (iota((64, T), 0), iota((64, T), 1))
    i, o = (iota((T, T), 0), iota((T, T), 1))
    totals = dot(totals, as_f32(i == o + 6), precision=HI)
    ref[:, 6, :] = dot(as_f32(t == (j >> 3)), totals, precision=HI)
    ref[:, 7, :] = jnp.zeros((64, T), F32)


def read_message(ref, d):
    x = [ref[:, d * 3 + h, :] for h in range(HEADS)]
    top = jnp.concatenate([v[:, :64] for v in x], axis=1)
    bottom = jnp.concatenate([v[:, 64:] for v in x], axis=1)
    return jnp.concatenate([top, bottom], axis=0)


def chain_kernel(backward, got_ref, out_ref):
    n, m = (got_ref.shape[0], got_ref.shape[1])
    sub = iota((m, 8, 128), 1)
    lane = iota((m, 8, 128), 2)
    ahead = sub < 3 if not backward else sub >= 3

    def factor(i):
        row = jnp.broadcast_to(got_ref[i, :, 6:7, :], (m, 8, 128))
        return jnp.sum(jnp.where(lane == sub, row, 0.0), axis=2, keepdims=True)

    up = jnp.zeros((m, 8, 128), F32)
    for i in range(n):
        out_ref[i] = up
        if i < n - 1:
            up = factor(i) * up + got_ref[i]
    down = jnp.zeros((m, 8, 128), F32)
    for i in range(n - 1, -1, -1):
        out_ref[i] = jnp.where(ahead, out_ref[i], down)
        if i > 0:
            down = factor(i) * down + got_ref[i]


def state_in(k, rows, columns):
    return rows[k][...] if k < 2 else read_message(columns, k - 2)


def sigmoid(x):
    return jax.nn.sigmoid(x)


def softplus(x):
    return jnp.maximum(x, 0.0) + jnp.log1p(jnp.exp(-jnp.abs(x)))


def conv_in(tok_ref, wbr_ref):
    branch = dot(tok_ref[...], wbr_ref[...]).astype(BF).astype(F32)
    return branch.reshape(R + 2, PITCH, DI)


def first_kernel(
    tok_ref, wbr_ref, cw_ref, cb_ref, wd_ref, wbc_ref, sb_ref, ld_ref,
    before_ref, act_ref, rawd_ref, bc_ref, step_ref, log_ref, tot_ref, mv_ref,
):
    padded = conv_in(tok_ref, wbr_ref)
    total = jnp.zeros((R, C, DI), F32)
    for b in range(3):
        shifted = padded[:, b : b + C, :]
        for a in range(3):
            total = total + cw_ref[3 * a + b : 3 * a + b + 1, :] * shifted[a : a + R]
    before = total.reshape(T, DI) + cb_ref[...]
    act = (before * sigmoid(before)).astype(BF)
    before_ref[...] = before
    act_ref[...] = act
    raw_d = dot(act, wd_ref[...])
    bc = dot(act, wbc_ref[...])
    step = softplus(raw_d + sb_ref[...])
    log_step = step * -jnp.exp(ld_ref[...])
    log = pick_lanes([dot(as_f32(mask(k)), log_step, precision=HI) for k in range(4)])
    rows, cols = (dot(as_f32(same_line(v)), log_step, precision=HI) for v in (False, True))
    tot = pick_lanes([rows, rows, cols, cols])
    rawd_ref[...] = raw_d
    bc_ref[...] = bc
    step_ref[...] = step
    log_ref[...] = log
    tot_ref[...] = tot
    weight = jnp.exp(tot - log) * step
    wide = act.astype(F32)
    states = [
        dot(spread_states(bc, k), by_head(weight, k) * wide, 0, 0, HI) for k in (2, 3)
    ]
    write_message(mv_ref, states, jnp.exp(tot))


def row_scan_kernel(
    me_ref, tok_ref, wbr_ref, cw_ref, cb_ref, wd_ref, wbc_ref, sb_ref, ld_ref,
    s0_ref, s1_ref, later_ref, gate_ref, pad_ref,
):
    branch = dot(tok_ref[...], wbr_ref[...]).astype(BF).astype(F32)
    pad_ref[...] = branch.reshape(R + 2, SPAN, DI)
    low = me_ref[0] * C
    high = low + C
    t, u = (iota((T, T), 0), iota((T, T), 1))
    same = (t >> 6) == (u >> 6)
    t, u = (t & 63, u & 63)
    reach = [
        same & (u > t) & (u < low),
        same & (u < t) & (u >= high),
        same & (u <= t) & (u >= high),
        same & (u >= t) & (u < low),
    ]
    reach = jnp.concatenate([as_f32(m) for m in reach], axis=0)
    before, after = (t < low, t >= high)
    first = iota((T, T), 1) < 3
    valid_in = jnp.where(first, as_f32(before), as_f32(after))
    valid_out = jnp.where(first, as_f32(after), as_f32(before))
    tj, j = (iota((T, 32), 0), iota((T, 32), 1))
    line = (tj >> 6) == (j >> 4)
    i, ji = (iota((T, 32), 0), iota((T, 32), 1))
    rate = -jnp.exp(ld_ref[...])
    for group in range(R // 2):
        total = jnp.zeros((2, 64, DI), F32)
        for b in range(3):
            shifted = pad_ref[2 * group : 2 * group + 4, b : b + 64, :]
            for a in range(3):
                total = total + cw_ref[3 * a + b : 3 * a + b + 1, :] * shifted[a : a + 2]
        wide = total.reshape(T, DI) + cb_ref[...]
        act = (wide * sigmoid(wide)).astype(BF)
        wide = act.astype(F32)
        step = softplus(dot(act, wd_ref[...]) + sb_ref[...])
        bc = dot(act, wbc_ref[...])
        x = dot(reach, step * rate, precision=HI)
        w_in = jnp.exp(jnp.where(first, x[:T], x[T : 2 * T])) * step * valid_in
        later_ref[group * T : group * T + T, :] = (
            jnp.exp(jnp.where(first, x[2 * T : 3 * T], x[3 * T :])) * valid_out
        )
        gate_ref[group * T : group * T + T, :] = shifted_gate(bc)
        for k, ref in enumerate((s0_ref, s1_ref)):
            entry = as_f32(i == 16 * k + (ji & 15))
            spread = jnp.where(line, dot(bc, entry, precision=HI), 0.0)
            ref[32 * group : 32 * group + 32, :] = dot(spread, by_head(w_in, k) * wide, 0, 0, HI)


def row_back_kernel(g_ref, later_ref, gate_ref, l0_ref, l1_ref):
    tj, j = (iota((T, 32), 0), iota((T, 32), 1))
    line = (tj >> 6) == (j >> 4)
    for group in range(R // 2):
        part = slice(group * T, group * T + T)
        g = g_ref[part, :].astype(F32)
        later = later_ref[part, :]
        gate = gate_ref[part, :]
        for k, ref in enumerate((l0_ref, l1_ref)):
            entry = as_f32(tj == 16 * k + (j & 15))
            spread = jnp.where(line, dot(gate, entry, precision=HI), 0.0)
            ref[32 * group : 32 * group + 32, :] = dot(spread, by_head(later, k) * g, 0, 0, HI)


def tables(k, bc, out_gate):
    lane = iota((T, T), 1) >> 4
    return dot(jnp.where(lane == k, out_gate, 0.0), bc, 1, 1, HI)


def decay(k, h, log, log_t):
    i = 3 * k + h
    return jnp.exp(jnp.where(mask(k), log[:, i : i + 1] - log_t[i : i + 1, :], FAR))


def shifted_gate(bc):
    return pltpu.roll(bc, 64, 1)


def local_kernel(act_ref, bc_ref, step_ref, log_ref, y_ref):
    bc = bc_ref[...]
    out_gate = shifted_gate(bc)
    log = log_ref[...]
    log_t, step_t = (log.T, step_ref[...].T)
    weights = [jnp.zeros((T, T), F32)] * HEADS
    for k in range(4):
        scores = tables(k, bc, out_gate)
        for h in range(HEADS):
            i = 3 * k + h
            weights[h] = weights[h] + scores * (
                decay(k, h, log, log_t) * step_t[i : i + 1, :]
            )
    wide = act_ref[...].astype(F32)
    y_ref[...] = per_head(lambda h: dot(weights[h], wide, precision=HI))


def carry(k, out_gate, exp_log, state):
    return by_head(exp_log, k) * dot(spread_states(out_gate, k), state, precision=HI)


def norm_kernel(
    y_ref, act_ref, bc_ref, log_ref, tot_ref, sv_ref, s0_ref, s1_ref, skip_ref, tok_ref, wg_ref, gain_ref,
    nb_ref, ow_ref, cot_ref,
    out_ref, g_ref, dgate_ref, gated_ref, norms_ref, mv_ref,
):
    bc = bc_ref[...]
    out_gate = shifted_gate(bc)
    exp_log = jnp.exp(log_ref[...])
    summed = y_ref[...] + skip_ref[...] * act_ref[...].astype(F32)
    for k in range(4):
        state = state_in(k, (s0_ref, s1_ref), sv_ref)
        summed = summed + carry(k, out_gate, exp_log, state)
    gate = dot(tok_ref[...], wg_ref[...]).astype(BF).astype(F32)
    sig = sigmoid(gate)
    center = summed - jnp.mean(summed, axis=1, keepdims=True)
    inv = lax.rsqrt(jnp.mean(center * center, axis=1, keepdims=True) + 1e-5)
    unit = center * inv
    normed = unit * gain_ref[...] + nb_ref[...]
    gated = (normed * gate * sig).astype(BF)
    gated_ref[...] = gated
    out_ref[...] = dot(gated, ow_ref[...]).astype(BF)
    grad = dot(cot_ref[...], ow_ref[...], 1, 1)
    dnormed = grad * gate * sig
    dgate_ref[...] = (grad * normed * (sig * (1.0 + gate * (1.0 - sig)))).astype(BF)
    norms_ref[0:1, :] = jnp.sum(dnormed * unit, axis=0, keepdims=True)
    norms_ref[1:2, :] = jnp.sum(dnormed, axis=0, keepdims=True)
    dunit = dnormed * gain_ref[...]
    g = inv * (
        dunit
        - jnp.mean(dunit, axis=1, keepdims=True)
        - unit * jnp.mean(dunit * unit, axis=1, keepdims=True)
    )
    g = g.astype(BF)
    g_ref[...] = g
    g = g.astype(F32)
    states = [
        dot(spread_states(out_gate, k), by_head(exp_log, k) * g, 0, 0, HI) for k in (2, 3)
    ]
    write_message(mv_ref, states, jnp.exp(tot_ref[...]))


def back_kernel(
    act_ref, bc_ref, step_ref, log_ref, g_ref, sv_ref, s0_ref, s1_ref,
    dact_ref, dbc_ref, dstep_ref, dlog_ref,
):
    bc = bc_ref[...]
    out_gate = shifted_gate(bc)
    log = log_ref[...]
    step = step_ref[...]
    log_t, step_t = (log.T, step.T)
    exp_log = jnp.exp(log)
    act = act_ref[...]
    g = g_ref[...]
    gw = g.astype(F32)
    lane = iota((T, DI), 1) // 64
    lane16 = iota((T, T), 1) >> 4
    lane1 = iota((T, T), 1)
    pair = [dot(jnp.where(lane == h, g, jnp.zeros_like(g)), act, 1, 1) for h in range(HEADS)]
    weights = [jnp.zeros((T, T), F32)] * HEADS
    d_in = jnp.zeros((T, T), F32)
    d_out = jnp.zeros((T, T), F32)
    row_sums = jnp.zeros((T, T), F32)
    step_rows = []
    for k in range(4):
        scores = tables(k, bc, out_gate)
        d_scores = jnp.zeros((T, T), F32)
        for h in range(HEADS):
            i = 3 * k + h
            dec = decay(k, h, log, log_t)
            dec_step = dec * step_t[i : i + 1, :]
            weights[h] = weights[h] + scores * dec_step
            d_scores = d_scores + pair[h] * dec_step
            d_step = pair[h] * dec * scores
            step_rows.append(jnp.sum(d_step, axis=0, keepdims=True))
            rows = jnp.sum(d_step * step_t[i : i + 1, :], axis=1, keepdims=True)
            row_sums = jnp.where(lane1 == i, rows, row_sums)
        d_out = d_out + dot(d_scores, jnp.where(lane16 == k, bc, 0.0), precision=HI)
        d_in = d_in + dot(d_scores, jnp.where(lane16 == k, out_gate, 0.0), 0, 0, HI)
        state = state_in(k, (s0_ref, s1_ref), sv_ref)
        expg = by_head(exp_log, k) * gw
        carried = dot(spread_states(out_gate, k), state, precision=HI)
        row_sums = row_sums + head_sum(carried * expg, k)
        d_out = d_out + gather_states(dot(expg, state, 1, 1, HI), k)
    d_step = jnp.concatenate(step_rows + [jnp.zeros((T - 12, T), F32)], axis=0).T
    dact_ref[...] = per_head(lambda h: dot(weights[h], gw, 0, 0, HI))
    dbc_ref[...] = d_in + pltpu.roll(d_out, 64, 1)
    dstep_ref[...] = d_step
    dlog_ref[...] = row_sums - step * d_step


def gate_grads_kernel(tok_ref, dgate_ref, gated_ref, cot_ref, gin_ref, gout_ref):
    gin_ref[...] = dot(tok_ref[...], dgate_ref[...], 0, 0)
    gout_ref[...] = dot(cot_ref[...], gated_ref[...], 0, 0)


def last_kernel(
    tok_ref, wbr_ref, cw_ref, before_ref, act_ref, rawd_ref, bc_ref, step_ref, log_ref, tot_ref, g_ref,
    sv_ref, s0_ref, s1_ref, lv_ref, l0_ref, l1_ref, dact_ref, dbc_ref, dstep_ref, dlog_ref, skip_ref, wd_ref, wbc_ref,
    sb_ref, ld_ref, gin_gate_ref, gout_ref, norms_ref,
    gb_ref, pack_ref,
):
    step, log, tot, bc = (step_ref[...], log_ref[...], tot_ref[...], bc_ref[...])
    act = act_ref[...]
    wide = act.astype(F32)
    g = g_ref[...].astype(F32)
    d_act = dact_ref[...] + skip_ref[...] * g
    d_bc = dbc_ref[...]
    to_end = jnp.exp(tot - log)
    weight = to_end * step
    through = jnp.exp(tot)
    inner = jnp.zeros((T, T), F32)
    cross = jnp.zeros((T, T), F32)
    for k in range(4):
        later = state_in(k, (l0_ref, l1_ref), lv_ref)
        earlier = state_in(k, (s0_ref, s1_ref), sv_ref)
        reach = dot(spread_states(bc, k), later, precision=HI)
        wk = by_head(weight, k)
        d_act = d_act + wk * reach
        inner = inner + head_sum(wide * reach, k)
        d_bc = d_bc + gather_states(dot(wk * wide, later, 1, 1, HI), k)
        cross = cross + dot(as_f32(on_line(k)), head_sum(later * earlier, k), precision=HI)
    d_step = dstep_ref[...] + to_end * inner
    left = weight * inner
    d_log = dlog_ref[...]
    parts = []
    for k in range(4):
        m = as_f32(mask(k))
        rest = as_f32(same_line(k >= 2)) - m.T
        parts.append(dot(m, d_log, 0, 0, HI) + dot(rest, left, precision=HI))
    d_log_step = pick_lanes(parts) + cross * through
    rate = -jnp.exp(ld_ref[...])
    d_rate = jnp.sum(d_log_step * step, axis=0, keepdims=True) * rate
    d_raw = (d_step + rate * d_log_step) * sigmoid(rawd_ref[...] + sb_ref[...])
    live = iota((T, T), 1) < 12
    d_raw = jnp.where(live, d_raw, 0.0)
    d_bias = jnp.sum(d_raw, axis=0, keepdims=True)
    d_raw = d_raw.astype(BF)
    d_bc = d_bc.astype(BF)
    d_act = d_act + dot(d_raw, wd_ref[...], 1, 1) + dot(d_bc, wbc_ref[...], 1, 1)
    before = before_ref[...]
    sig = sigmoid(before)
    gb = (d_act * sig * (1.0 + before * (1.0 - sig))).astype(BF)
    gb_ref[...] = gb
    gbw = gb.astype(F32)
    padded = conv_in(tok_ref, wbr_ref)
    tok = tok_ref[...].astype(F32).reshape(R + 2, PITCH, D)
    gin = jnp.zeros((D, DI), F32)
    conv_rows = [None] * 9
    for b in range(3):
        near = padded[:, b : b + C, :]
        near_tok = tok[:, b : b + C, :]
        for a in range(3):
            i = 3 * a + b
            conv_rows[i] = jnp.sum(gbw * near[a : a + R].reshape(T, DI), axis=0, keepdims=True)
            gin = gin + cw_ref[i : i + 1, :] * dot(
                near_tok[a : a + R].reshape(T, D).astype(BF), gb, 0, 0
            )
    wide_row = lambda x: jnp.concatenate([x, jnp.zeros((1, DI - T), F32)], axis=1)
    small = jnp.concatenate(
        conv_rows
        + [
            jnp.sum(gbw, axis=0, keepdims=True),
            jnp.sum(g * wide, axis=0, keepdims=True),
            norms_ref[0:1, :],
            norms_ref[1:2, :],
            wide_row(d_bias),
            wide_row(jnp.where(live[:1], d_rate, 0.0)),
            jnp.zeros((1, DI), F32),
        ],
        axis=0,
    )
    both = [
        gin, gin_gate_ref[...], gout_ref[...], small, dot(d_bc, act, 0, 0),
        dot(d_raw, act, 0, 0)[:16],
    ]
    full = jnp.concatenate(both, axis=0)
    rest = small - small.astype(BF).astype(F32)
    pack_ref[0:448, :] = full[:, :128].astype(BF)
    pack_ref[448:672, :] = jnp.concatenate([full[:224, 128:], full[224:, 128:]], axis=1).astype(BF)
    pack_ref[672:688, :] = rest[:, :128].astype(BF)
    pack_ref[688:704, :] = jnp.concatenate(
        [rest[:, 128:], jnp.zeros((16, 64), F32)], axis=1
    ).astype(BF)
    pack_ref[704:1024, :] = jnp.zeros((320, T), BF)


def out_kernel(gb_ref, cw_ref, dgate_ref, wbr_ref, wg_ref, out_ref):
    padded = gb_ref[...].astype(F32).reshape(R + 2, PITCH, DI)
    total = jnp.zeros((R, C, DI), F32)
    for b in range(3):
        shifted = padded[:, 2 - b : 2 - b + C, :]
        for a in range(3):
            total = total + cw_ref[3 * a + b : 3 * a + b + 1, :] * shifted[2 - a : 2 - a + R]
    d_branch = total.reshape(T, DI).astype(BF)
    out_ref[...] = (
        dot(d_branch, wbr_ref[...], 1, 1) + dot(dgate_ref[...], wg_ref[...], 1, 1)
    ).astype(BF)


def sum_kernel(scale, x_ref, out_ref):
    total = x_ref[0].astype(F32)
    for i in range(1, x_ref.shape[0]):
        total = total + x_ref[i].astype(F32)
    out_ref[...] = jnp.broadcast_to(total * scale, out_ref.shape)


def unpack_kernel(
    x_ref, gin_ref, conv_ref, cb_ref, scan_ref, sb_ref, ld_ref, skip_ref, gain_ref, nb_ref, gout_ref
):
    low, high = (x_ref[0:448, :], x_ref[448:672, :])
    full = jnp.concatenate(
        [low, jnp.concatenate([high[:, :64], high[:, 64:]], axis=0)], axis=1
    )
    rest = jnp.concatenate([x_ref[672:688, :], x_ref[688:704, :64]], axis=1)
    gin_ref[...] = jnp.concatenate([full[:96], full[96:192]], axis=1)
    gout_ref[...] = full[192:288].T
    small = full[288:304] + rest
    for a in range(3):
        conv_ref[a] = small[3 * a : 3 * a + 3]
    cb_ref[...] = small[9:10]
    skip_ref[...] = jnp.broadcast_to(small[10:11], (4, DI))
    gain_ref[...] = small[11:12]
    nb_ref[...] = small[12:13]
    for k in range(4):
        sb_ref[k : k + 1, :] = small[13:14, 3 * k : 3 * k + 3]
        ld_ref[k : k + 1, :] = small[14:15, 3 * k : 3 * k + 3]
    scan = jnp.concatenate([full[304:448], jnp.zeros((112, DI), F32)], axis=0).T
    for k in range(4):
        scan_ref[k] = jnp.concatenate(
            [
                scan[:, 128 + 3 * k : 131 + 3 * k],
                scan[:, 16 * k : 16 * k + 16],
                scan[:, 64 + 16 * k : 80 + 16 * k],
            ],
            axis=1,
        )


def call(kernel, outs, *args, flops=10**8, scratch=(), scalars=0):
    whole = pl.BlockSpec(memory_space=pltpu.VMEM)
    small = pl.BlockSpec(memory_space=pltpu.SMEM)
    return pl.pallas_call(
        kernel,
        out_shape=[jax.ShapeDtypeStruct(s, t) for s, t in outs],
        in_specs=[small] * scalars + [whole] * (len(args) - scalars),
        out_specs=[whole] * len(outs),
        scratch_shapes=list(scratch),
        compiler_params=pltpu.CompilerParams(vmem_limit_bytes=40 * 2**20),
        cost_estimate=pl.CostEstimate(flops=flops, bytes_accessed=10**6, transcendentals=0),
    )(*args)


def edges(x, axis, dim):
    size, length = (lax.axis_size(axis), x.shape[dim])
    up = [(i, i + 1) for i in range(size - 1)]
    down = [(j, i) for i, j in up]
    before = lax.ppermute(lax.slice_in_dim(x, length - 1, length, axis=dim), axis, up)
    after = lax.ppermute(lax.slice_in_dim(x, 0, 1, axis=dim), axis, down)
    return before, after


def with_rim(x):
    before, after = edges(x, "row", 0)
    x = jnp.concatenate([before, x, after], axis=0)
    before, after = edges(x, "col", 1)
    full = jnp.concatenate([before, x, after], axis=1)
    full = jnp.pad(full, ((0, 0), (0, PITCH - C - 2), (0, 0)))
    return full.reshape((R + 2) * PITCH, x.shape[-1])


def all_to_all(x, axis):
    return lax.all_to_all(x, axis, 0, 0, tiled=True)


def whole_rows(x):
    count = lax.axis_size("col")
    everything = all_to_all(jnp.broadcast_to(x, (count,) + x.shape), "col")
    everything = everything.reshape(count, x.shape[0], C, -1)
    return jnp.swapaxes(everything, 0, 1).reshape(x.shape[0], count * C, -1)


def exchange(message, axis, backward):
    size = lax.axis_size(axis)
    got = all_to_all(message, axis)
    shape = (size, message.shape[0] // size, 8, 128)
    (states,) = call(partial(chain_kernel, backward), [(shape, F32)], got.reshape(shape), flops=10**7)
    return all_to_all(states.reshape(message.shape), axis)


def reduced(pack, scale):
    rows, cols = (lax.axis_size("row"), lax.axis_size("col"))
    chunk = pack.shape[0] // rows
    got = all_to_all(pack.reshape(rows, chunk, 128), "row")
    (part,) = call(partial(sum_kernel, 1.0), [((cols, chunk, 128), F32)], got, flops=10**7)
    got = all_to_all(part, "col")
    (part,) = call(partial(sum_kernel, scale), [((rows, chunk, 128), F32)], got, flops=10**7)
    return all_to_all(part, "row").reshape(pack.shape)


def local(
    tokens, in_weight, conv_weight, conv_bias, scan_weight, step_bias, log_decay, skip_gain, norm_gain,
    norm_bias, out_weight, cotangent,
):
    own = tokens.reshape(T, D)
    place = lax.axis_index("col")
    before, after = edges(tokens, "row", 0)
    band = whole_rows(jnp.concatenate([before, tokens, after], axis=0))
    band = jnp.pad(band, ((0, 0), (1, SPAN - 1 - band.shape[1]), (0, 0)))
    halo = lax.dynamic_slice_in_dim(band, place * C, PITCH, axis=1).reshape((R + 2) * PITCH, D)
    band = band.reshape((R + 2) * SPAN, D)
    cot = cotangent.reshape(T, D)
    w_branch, w_gate = (in_weight[:, :DI], in_weight[:, DI:])
    taps = jnp.pad(conv_weight.reshape(9, DI), ((0, 7), (0, 0)))
    by_channel = jnp.moveaxis(scan_weight, 1, 0)
    w_step = jnp.pad(by_channel[:, :, :HEADS].reshape(DI, 12), ((0, 0), (0, 116)))
    w_bc = jnp.concatenate(
        [
            by_channel[:, :, HEADS : HEADS + NS].reshape(DI, 64),
            by_channel[:, :, HEADS + NS :].reshape(DI, 64),
        ],
        axis=1,
    )
    row = lambda x: x.reshape(1, -1)
    bias = jnp.pad(row(step_bias), ((0, 0), (0, 116)))
    rate = jnp.pad(row(log_decay), ((0, 0), (0, 116)))
    skip = row(jnp.sum(skip_gain, axis=0))
    square = ((T, T), F32)
    wide = ((T, DI), F32)
    low = ((T, DI), BF)
    message = ((64, 8, 128), F32)
    states = ((256, DI), F32)
    long = ((8 * T, T), F32)

    before, act, raw_d, bc, step, log, tot, mv = call(
        first_kernel, [wide, low, square, square, square, square, square, message],
        halo, w_branch, taps, row(conv_bias), w_step, w_bc, bias, rate,
    )
    sv = exchange(mv, "row", False)
    s0, s1, later, gate_c = call(
        row_scan_kernel, [states, states, long, long],
        place.reshape(1), band, w_branch, taps, row(conv_bias), w_step, w_bc, bias, rate,
        scratch=[pltpu.VMEM((R + 2, SPAN, DI), F32)], scalars=1, flops=10**9,
    )
    (y,) = call(local_kernel, [wide], act, bc, step, log)
    out, g, d_gate, gated, norms, mv = call(
        norm_kernel, [((T, D), BF), low, low, low, ((8, DI), F32), message],
        y, act, bc, log, tot, sv, s0, s1, skip, own, w_gate, row(norm_gain), row(norm_bias), out_weight, cot,
    )
    lv = exchange(mv, "row", True)
    band_g = whole_rows(g.reshape(R, C * DI)).reshape(8 * T, DI)
    l0, l1 = call(row_back_kernel, [states, states], band_g, later, gate_c, flops=10**9)
    d_act, d_bc, d_step, d_log = call(
        back_kernel, [wide, square, square, square], act, bc, step, log, g, sv, s0, s1
    )
    gin_gate, gout = call(
        gate_grads_kernel, [((D, DI), F32), ((D, DI), F32)], own, d_gate, gated, cot, flops=10**7
    )
    gb, pack = call(
        last_kernel, [low, ((1024, 128), BF)],
        halo, w_branch, taps, before, act, raw_d, bc, step, log, tot, g, sv, s0, s1, lv, l0, l1, d_act, d_bc,
        d_step, d_log, skip, w_step, w_bc, bias, rate, gin_gate, gout, norms,
    )
    gb_halo = with_rim(gb.reshape(R, C, DI))
    (d_tokens,) = call(out_kernel, [((T, D), BF)], gb_halo, taps, d_gate, w_branch, w_gate)
    scale = float(T * lax.axis_size("row") * lax.axis_size("col")) ** (-0.5)
    row_shape = ((1, DI), F32)
    gin, g_conv, g_cb, g_scan, g_bias, g_rate, g_skip, g_gain, g_shift, gout = call(
        unpack_kernel,
        [
            ((D, 2 * DI), F32), ((3, 3, DI), F32), row_shape, ((4, DI, HEADS + 2 * NS), F32),
            ((4, HEADS), F32), ((4, HEADS), F32), ((4, DI), F32), row_shape, row_shape, ((DI, D), F32),
        ],
        reduced(pack, scale), flops=10**7,
    )
    return (
        out.reshape(R, C * D), d_tokens.reshape(R, C * D), gin, g_conv, g_cb.reshape(DI), g_scan, g_bias,
        g_rate, g_skip, g_gain.reshape(DI), g_shift.reshape(DI), gout,
    )


def solution(mesh):
    in_specs = (P("row", "col"), P(), P(), P(), P(), P(), P(), P(), P(), P(), P(), P("row", "col"))
    out_specs = (P("row", "col"), P("row", "col"), P(), P(), P(), P(), P(), P(), P(), P(), P(), P())
    return jax.shard_map(local, mesh=mesh, in_specs=in_specs, out_specs=out_specs, check_vma=False)
```

```python
from functools import partial

import jax
import jax.numpy as jnp
from jax import lax
from jax.experimental import pallas as pl
from jax.experimental.pallas import tpu as pltpu
from jax.sharding import PartitionSpec as P

D = 96
DI = 192
NS = 16
HEADS = 3
R = 16
C = 8
T = R * C
PITCH = 24

F32 = jnp.float32
BF = jnp.bfloat16
FAR = -1e30


def dot(a, b, ca=1, cb=0):
    return lax.dot_general(a, b, (((ca,), (cb,)), ((), ())), preferred_element_type=F32)


def halves(x):
    if x.dtype == BF:
        return [x]
    high = x.astype(BF)
    return [high, (x - high.astype(F32)).astype(BF)]


def fine(a, b, ca=1, cb=0):
    a, b = (halves(a), halves(b))
    out = dot(a[0], b[0], ca, cb)
    for i, j in ((0, 1), (1, 0)):
        if i < len(a) and j < len(b):
            out = out + dot(a[i], b[j], ca, cb)
    return out


def iota(shape, dim):
    return lax.broadcasted_iota(jnp.int32, shape, dim)


def mask(k):
    t, s = (iota((T, T), 0), iota((T, T), 1))
    rt, ct, rs, cs = (t >> 3, t & 7, s >> 3, s & 7)
    if k == 0:
        return (rt == rs) & (cs <= ct)
    if k == 1:
        return (rt == rs) & (cs >= ct)
    if k == 2:
        return (ct == cs) & (rs <= rt)
    return (ct == cs) & (rs >= rt)


def same_line(vertical):
    t, s = (iota((T, T), 0), iota((T, T), 1))
    return (t & 7) == (s & 7) if vertical else (t >> 3) == (s >> 3)


def pick_lanes(parts):
    lane = iota((T, T), 1) // 3
    out = parts[3]
    for k in range(3):
        out = jnp.where(lane == k, parts[k], out)
    return out


def as_f32(m):
    return jnp.where(m, 1.0, 0.0).astype(F32)


def ones(m):
    return as_f32(m).astype(BF)


def states_of(k):
    return 256 if k < 2 else 128


def line_and_entry(j, k):
    if k < 2:
        return (j >> 4, j & 15)
    return ((j >> 3) & 7, 2 * (j & 7) + (j >> 6))


def on_line(k):
    t, j = (iota((T, states_of(k)), 0), iota((T, states_of(k)), 1))
    return line_and_entry(j, k)[0] == (t >> 3 if k < 2 else t & 7)


def spread_states(bc, k):
    i, j = (iota((T, states_of(k)), 0), iota((T, states_of(k)), 1))
    wide = fine(bc, ones(i == 16 * k + line_and_entry(j, k)[1]))
    return jnp.where(on_line(k), wide, 0.0)


def gather_states(wide, k):
    j, i = (iota((states_of(k), T), 0), iota((states_of(k), T), 1))
    entry = line_and_entry(j, k)[1]
    return fine(jnp.where(on_line(k), wide, 0.0), ones(i == 16 * k + entry))


def by_head(values, k):
    lane = iota((T, DI), 1)
    a, b, c = (values[:, 3 * k + h : 3 * k + h + 1] for h in range(HEADS))
    return jnp.where(lane < 64, a, jnp.where(lane < 128, b, c))


def head_sum(wide, k):
    c, j = (iota((DI, T), 0), iota((DI, T), 1))
    return fine(wide, ones(j == 3 * k + c // 64))


def per_head(f):
    lane = iota((T, DI), 1)
    a, b, c = (f(h) for h in range(HEADS))
    return jnp.where(lane < 64, a, jnp.where(lane < 128, b, c))


def write_message(ref, wide_ref, states, totals):
    for d in range(2):
        s = states[d]
        for h in range(HEADS):
            wide_ref[:, d * 3 + h, :] = jnp.concatenate(
                [s[:64, 64 * h : 64 * h + 64], s[64:, 64 * h : 64 * h + 64]], axis=1
            )
    j, t = (iota((64, T), 0), iota((64, T), 1))
    i, o = (iota((T, T), 0), iota((T, T), 1))
    totals = fine(ones(t == (j >> 3)), fine(totals, ones(i == o + 6)))
    high = totals.astype(BF).astype(F32)
    wide_ref[:, 6, :] = high
    wide_ref[:, 7, :] = totals - high
    ref[...] = wide_ref[...].reshape(512, 128).astype(BF)


def open_message(ref, wide_ref):
    wide_ref[...] = ref[...].astype(F32).reshape(64, 8, 128)


def read_message(ref, d):
    x = [ref[:, d * 3 + h, :] for h in range(HEADS)]
    top = jnp.concatenate([v[:, :64] for v in x], axis=1)
    bottom = jnp.concatenate([v[:, 64:] for v in x], axis=1)
    return jnp.concatenate([top, bottom], axis=0)


def chain_kernel(backward, got_ref, out_ref):
    m = 512 // lax.axis_size("row")
    n = 512 // m
    got = got_ref[...].astype(F32).reshape(n, m // 8, 8, 128)
    shape = (m // 8, 8, 128)
    sub, lane = (iota(shape, 1), iota(shape, 2))
    ahead = sub < 3 if not backward else sub >= 3

    def factor(i):
        row = jnp.broadcast_to(got[i, :, 6:7, :] + got[i, :, 7:8, :], shape)
        return jnp.sum(jnp.where(lane == sub, row, 0.0), axis=2, keepdims=True)

    factors = [factor(i) for i in range(n)]
    up = [jnp.zeros(shape, F32)]
    for i in range(n - 1):
        up.append(factors[i] * up[i] + got[i])
    down = [jnp.zeros(shape, F32)]
    for i in range(n - 1, 0, -1):
        down.append(factors[i] * down[-1] + got[i])
    down = down[::-1]
    full = jnp.concatenate([jnp.where(ahead, u, v) for u, v in zip(up, down)], axis=0)
    out_ref[...] = full.reshape(512, 128).astype(BF)


def state_in(k, rows, columns):
    return rows[k][...] if k < 2 else read_message(columns, k - 2)


def sigmoid(x):
    return jax.nn.sigmoid(x)


def softplus(x):
    return jnp.maximum(x, 0.0) + jnp.log1p(jnp.exp(-jnp.abs(x)))


def fill_rim(pad_ref, above, own, below, left, right):
    pad_ref[0:1, 8:16, :] = above.reshape(1, C, -1)
    pad_ref[1 : R + 1, 8:16, :] = own.reshape(R, C, -1)
    pad_ref[R + 1 : R + 2, 8:16, :] = below.reshape(1, C, -1)
    for r in range(R + 2):
        pad_ref[r, 7:8, :] = left[r : r + 1]
        pad_ref[r, 16:17, :] = right[r : r + 1]


def edge_factor(me, blocks, j):
    return jnp.clip(j, 0, blocks - 1), jnp.where((j >= 0) & (j < blocks), 1.0, 0.0)


def fill_blocks(me, got_ref, pad_ref, f):
    for i in range(3):
        at, inside = edge_factor(me, got_ref.shape[0], me + i - 1)
        pad_ref[:, 8 * i : 8 * i + 8, :] = f(got_ref[at]).reshape(R + 2, C, -1) * inside


def as_branch(wbr_ref):
    return lambda x: dot(x, wbr_ref[...]).astype(BF).astype(F32)


def first_kernel(
    me_ref, got_ref, wbr_ref, cw_ref, cb_ref, wd_ref, wbc_ref, sb_ref, ld_ref,
    before_ref, act_ref, rawd_ref, bc_ref, step_ref, log_ref, tot_ref, mv_ref, pad_ref, wide_ref,
):
    fill_blocks(me_ref[0], got_ref, pad_ref, as_branch(wbr_ref))
    total = jnp.zeros((R, C, DI), F32)
    for b in range(3):
        shifted = pad_ref[:, 7 + b : 7 + b + C, :]
        for a in range(3):
            total = total + cw_ref[3 * a + b : 3 * a + b + 1, :] * shifted[a : a + R]
    before = total.reshape(T, DI) + cb_ref[...]
    act = (before * sigmoid(before)).astype(BF)
    before_ref[...] = before
    act_ref[...] = act
    raw_d = dot(act, wd_ref[...])
    bc = dot(act, wbc_ref[...])
    step = softplus(raw_d + sb_ref[...])
    log_step = step * -jnp.exp(ld_ref[...])
    log = pick_lanes([fine(ones(mask(k)), log_step) for k in range(4)])
    rows, cols = (fine(ones(same_line(v)), log_step) for v in (False, True))
    tot = pick_lanes([rows, rows, cols, cols])
    rawd_ref[...] = raw_d
    bc_ref[...] = bc
    step_ref[...] = step
    log_ref[...] = log
    tot_ref[...] = tot
    weight = jnp.exp(tot - log) * step
    wide = act.astype(F32)
    states = [
        fine(spread_states(bc, k), by_head(weight, k) * wide, 0, 0) for k in (2, 3)
    ]
    write_message(mv_ref, wide_ref, states, jnp.exp(tot))


def row_pair(me, blocks_ref, group):
    lines = []
    for r in range(2):
        at = pl.ds(16 * group, 16)
        for j in range(8):
            lines.append(blocks_ref[me ^ j, at, :].astype(F32)[8 * r : 8 * r + 8])
    return jnp.concatenate(lines, axis=0)


def row_scan_kernel(
    me_ref, got_ref, wbr_ref, cw_ref, cb_ref, wd_ref, wbc_ref, sb_ref, ld_ref,
    s0_ref, s1_ref, later_ref, gate_ref, pad_ref,
):
    nothing = jnp.zeros((R + 2, 8, DI), F32)
    pad_ref[:, 0:8, :] = nothing
    pad_ref[:, 72:80, :] = nothing
    for j in range(8):
        pad_ref[:, 8 + 8 * j : 16 + 8 * j, :] = as_branch(wbr_ref)(got_ref[j]).reshape(R + 2, C, DI)
    low = me_ref[0] * C
    high = low + C
    t, u = (iota((T, T), 0), iota((T, T), 1))
    same = (t >> 6) == (u >> 6)
    t, u = (t & 63, u & 63)
    reach = [
        same & (u > t) & (u < low),
        same & (u < t) & (u >= high),
        same & (u <= t) & (u >= high),
        same & (u >= t) & (u < low),
    ]
    reach = jnp.concatenate([ones(m) for m in reach], axis=0)
    before, after = (t < low, t >= high)
    first = iota((T, T), 1) < 3
    valid_in = jnp.where(first, as_f32(before), as_f32(after))
    valid_out = jnp.where(first, as_f32(after), as_f32(before))
    tj, j = (iota((T, 32), 0), iota((T, 32), 1))
    line = (tj >> 6) == (j >> 4)
    i, ji = (iota((T, 32), 0), iota((T, 32), 1))
    rate = -jnp.exp(ld_ref[...])
    for group in range(R // 2):
        total = jnp.zeros((2, 64, DI), F32)
        for b in range(3):
            shifted = pad_ref[2 * group : 2 * group + 4, 7 + b : 71 + b, :]
            for a in range(3):
                total = total + cw_ref[3 * a + b : 3 * a + b + 1, :] * shifted[a : a + 2]
        wide = total.reshape(T, DI) + cb_ref[...]
        act = (wide * sigmoid(wide)).astype(BF)
        wide = act.astype(F32)
        step = softplus(dot(act, wd_ref[...]) + sb_ref[...])
        bc = dot(act, wbc_ref[...])
        x = fine(reach, step * rate)
        w_in = jnp.exp(jnp.where(first, x[:T], x[T : 2 * T])) * step * valid_in
        later_ref[group * T : group * T + T, :] = (
            jnp.exp(jnp.where(first, x[2 * T : 3 * T], x[3 * T :])) * valid_out
        )
        gate_ref[group * T : group * T + T, :] = shifted_gate(bc)
        for k, ref in enumerate((s0_ref, s1_ref)):
            entry = ones(i == 16 * k + (ji & 15))
            spread = jnp.where(line, fine(bc, entry), 0.0)
            ref[32 * group : 32 * group + 32, :] = fine(spread, by_head(w_in, k) * wide, 0, 0)


def row_back_kernel(me_ref, blocks_ref, later_ref, gate_ref, l0_ref, l1_ref):
    tj, j = (iota((T, 32), 0), iota((T, 32), 1))
    line = (tj >> 6) == (j >> 4)
    for group in range(R // 2):
        part = slice(group * T, group * T + T)
        g = row_pair(me_ref[0], blocks_ref, group)
        later = later_ref[part, :]
        gate = gate_ref[part, :]
        for k, ref in enumerate((l0_ref, l1_ref)):
            entry = ones(tj == 16 * k + (j & 15))
            spread = jnp.where(line, fine(gate, entry), 0.0)
            ref[32 * group : 32 * group + 32, :] = fine(spread, by_head(later, k) * g, 0, 0)


def tables(k, bc, out_gate):
    lane = iota((T, T), 1) >> 4
    return fine(jnp.where(lane == k, out_gate, 0.0), bc, 1, 1)


def decay(k, h, log, log_t):
    i = 3 * k + h
    return jnp.exp(jnp.where(mask(k), log[:, i : i + 1] - log_t[i : i + 1, :], FAR))


def shifted_gate(bc):
    return pltpu.roll(bc, 64, 1)


def local_kernel(act_ref, bc_ref, step_ref, log_ref, y_ref):
    bc = bc_ref[...]
    out_gate = shifted_gate(bc)
    log = log_ref[...]
    log_t, step_t = (log.T, step_ref[...].T)
    weights = [jnp.zeros((T, T), F32)] * HEADS
    for k in range(4):
        scores = tables(k, bc, out_gate)
        for h in range(HEADS):
            i = 3 * k + h
            weights[h] = weights[h] + scores * (
                decay(k, h, log, log_t) * step_t[i : i + 1, :]
            )
    act = act_ref[...]
    y_ref[...] = per_head(lambda h: fine(weights[h], act))


def carry(k, out_gate, exp_log, state):
    return by_head(exp_log, k) * fine(spread_states(out_gate, k), state)


def norm_kernel(
    y_ref, act_ref, bc_ref, log_ref, tot_ref, sv_ref, s0_ref, s1_ref, skip_ref, tok_ref, wg_ref, gain_ref,
    nb_ref, ow_ref, cot_ref,
    out_ref, g_ref, dgate_ref, gated_ref, norms_ref, mv_ref, wide_ref,
):
    open_message(sv_ref, wide_ref)
    bc = bc_ref[...]
    out_gate = shifted_gate(bc)
    exp_log = jnp.exp(log_ref[...])
    summed = y_ref[...] + skip_ref[...] * act_ref[...].astype(F32)
    for k in range(4):
        state = state_in(k, (s0_ref, s1_ref), wide_ref)
        summed = summed + carry(k, out_gate, exp_log, state)
    gate = dot(tok_ref[...], wg_ref[...]).astype(BF).astype(F32)
    sig = sigmoid(gate)
    center = summed - jnp.mean(summed, axis=1, keepdims=True)
    inv = lax.rsqrt(jnp.mean(center * center, axis=1, keepdims=True) + 1e-5)
    unit = center * inv
    normed = unit * gain_ref[...] + nb_ref[...]
    gated = (normed * gate * sig).astype(BF)
    gated_ref[...] = gated
    out_ref[...] = dot(gated, ow_ref[...]).astype(BF)
    grad = dot(cot_ref[...], ow_ref[...], 1, 1)
    dnormed = grad * gate * sig
    dgate_ref[...] = (grad * normed * (sig * (1.0 + gate * (1.0 - sig)))).astype(BF)
    norms_ref[0:1, :] = jnp.sum(dnormed * unit, axis=0, keepdims=True)
    norms_ref[1:2, :] = jnp.sum(dnormed, axis=0, keepdims=True)
    dunit = dnormed * gain_ref[...]
    g = inv * (
        dunit
        - jnp.mean(dunit, axis=1, keepdims=True)
        - unit * jnp.mean(dunit * unit, axis=1, keepdims=True)
    )
    g = g.astype(BF)
    g_ref[...] = g
    g = g.astype(F32)
    states = [
        fine(spread_states(out_gate, k), by_head(exp_log, k) * g, 0, 0) for k in (2, 3)
    ]
    write_message(mv_ref, wide_ref, states, jnp.exp(tot_ref[...]))


def back_kernel(
    act_ref, bc_ref, step_ref, log_ref, g_ref, sv_ref, s0_ref, s1_ref,
    dact_ref, dbc_ref, dstep_ref, dlog_ref, wide_ref,
):
    open_message(sv_ref, wide_ref)
    bc = bc_ref[...]
    out_gate = shifted_gate(bc)
    log = log_ref[...]
    step = step_ref[...]
    log_t, step_t = (log.T, step.T)
    exp_log = jnp.exp(log)
    act = act_ref[...]
    g = g_ref[...]
    gw = g.astype(F32)
    lane = iota((T, DI), 1) // 64
    lane16 = iota((T, T), 1) >> 4
    lane1 = iota((T, T), 1)
    pair = [dot(jnp.where(lane == h, g, jnp.zeros_like(g)), act, 1, 1) for h in range(HEADS)]
    weights = [jnp.zeros((T, T), F32)] * HEADS
    d_in = jnp.zeros((T, T), F32)
    d_out = jnp.zeros((T, T), F32)
    row_sums = jnp.zeros((T, T), F32)
    step_rows = []
    for k in range(4):
        scores = tables(k, bc, out_gate)
        d_scores = jnp.zeros((T, T), F32)
        for h in range(HEADS):
            i = 3 * k + h
            dec = decay(k, h, log, log_t)
            dec_step = dec * step_t[i : i + 1, :]
            weights[h] = weights[h] + scores * dec_step
            d_scores = d_scores + pair[h] * dec_step
            d_step = pair[h] * dec * scores
            step_rows.append(jnp.sum(d_step, axis=0, keepdims=True))
            rows = jnp.sum(d_step * step_t[i : i + 1, :], axis=1, keepdims=True)
            row_sums = jnp.where(lane1 == i, rows, row_sums)
        d_out = d_out + fine(d_scores, jnp.where(lane16 == k, bc, 0.0))
        d_in = d_in + fine(d_scores, jnp.where(lane16 == k, out_gate, 0.0), 0, 0)
        state = state_in(k, (s0_ref, s1_ref), wide_ref)
        expg = by_head(exp_log, k) * gw
        carried = fine(spread_states(out_gate, k), state)
        row_sums = row_sums + head_sum(carried * expg, k)
        d_out = d_out + gather_states(fine(expg, state, 1, 1), k)
    d_step = jnp.concatenate(step_rows + [jnp.zeros((T - 12, T), F32)], axis=0).T
    dact_ref[...] = per_head(lambda h: fine(weights[h], g, 0, 0))
    dbc_ref[...] = d_in + pltpu.roll(d_out, 64, 1)
    dstep_ref[...] = d_step
    dlog_ref[...] = row_sums - step * d_step


def gate_grads_kernel(tok_ref, dgate_ref, gated_ref, cot_ref, gin_ref, gout_ref):
    gin_ref[...] = dot(tok_ref[...], dgate_ref[...], 0, 0)
    gout_ref[...] = dot(cot_ref[...], gated_ref[...], 0, 0)


def last_kernel(
    me_ref, got_ref, wbr_ref, cw_ref, before_ref, act_ref, rawd_ref, bc_ref, step_ref, log_ref, tot_ref, g_ref,
    sv_ref, s0_ref, s1_ref, lv_ref, l0_ref, l1_ref, dact_ref, dbc_ref, dstep_ref, dlog_ref, skip_ref, wd_ref, wbc_ref,
    sb_ref, ld_ref, gin_gate_ref, gout_ref, norms_ref,
    gb_ref, pack_ref, pad_ref, tok_ref, early_ref, late_ref,
):
    open_message(sv_ref, early_ref)
    open_message(lv_ref, late_ref)
    step, log, tot, bc = (step_ref[...], log_ref[...], tot_ref[...], bc_ref[...])
    act = act_ref[...]
    wide = act.astype(F32)
    g = g_ref[...].astype(F32)
    d_act = dact_ref[...] + skip_ref[...] * g
    d_bc = dbc_ref[...]
    to_end = jnp.exp(tot - log)
    weight = to_end * step
    through = jnp.exp(tot)
    inner = jnp.zeros((T, T), F32)
    cross = jnp.zeros((T, T), F32)
    for k in range(4):
        later = state_in(k, (l0_ref, l1_ref), late_ref)
        earlier = state_in(k, (s0_ref, s1_ref), early_ref)
        reach = fine(spread_states(bc, k), later)
        wk = by_head(weight, k)
        d_act = d_act + wk * reach
        inner = inner + head_sum(wide * reach, k)
        d_bc = d_bc + gather_states(fine(wk * wide, later, 1, 1), k)
        cross = cross + fine(ones(on_line(k)), head_sum(later * earlier, k))
    d_step = dstep_ref[...] + to_end * inner
    left = weight * inner
    d_log = dlog_ref[...]
    parts = []
    for k in range(4):
        after = mask(k ^ 1)
        rest = same_line(k >= 2) & jnp.logical_not(after)
        parts.append(fine(ones(after), d_log) + fine(ones(rest), left))
    d_log_step = pick_lanes(parts) + cross * through
    rate = -jnp.exp(ld_ref[...])
    d_rate = jnp.sum(d_log_step * step, axis=0, keepdims=True) * rate
    d_raw = (d_step + rate * d_log_step) * sigmoid(rawd_ref[...] + sb_ref[...])
    live = iota((T, T), 1) < 12
    d_raw = jnp.where(live, d_raw, 0.0)
    d_bias = jnp.sum(d_raw, axis=0, keepdims=True)
    d_raw = d_raw.astype(BF)
    d_bc = d_bc.astype(BF)
    d_act = d_act + dot(d_raw, wd_ref[...], 1, 1) + dot(d_bc, wbc_ref[...], 1, 1)
    before = before_ref[...]
    sig = sigmoid(before)
    gb = (d_act * sig * (1.0 + before * (1.0 - sig))).astype(BF)
    gb_ref[...] = gb
    gbw = gb.astype(F32)
    fill_blocks(me_ref[0], got_ref, pad_ref, as_branch(wbr_ref))
    fill_blocks(me_ref[0], got_ref, tok_ref, lambda x: x.astype(F32))
    gin = jnp.zeros((D, DI), F32)
    conv_rows = [None] * 9
    for b in range(3):
        near = pad_ref[:, 7 + b : 7 + b + C, :]
        near_tok = tok_ref[:, 7 + b : 7 + b + C, :]
        for a in range(3):
            i = 3 * a + b
            conv_rows[i] = jnp.sum(gbw * near[a : a + R].reshape(T, DI), axis=0, keepdims=True)
            gin = gin + cw_ref[i : i + 1, :] * dot(
                near_tok[a : a + R].reshape(T, D).astype(BF), gb, 0, 0
            )
    wide_row = lambda x: jnp.concatenate([x, jnp.zeros((1, DI - T), F32)], axis=1)
    small = jnp.concatenate(
        conv_rows
        + [
            jnp.sum(gbw, axis=0, keepdims=True),
            jnp.sum(g * wide, axis=0, keepdims=True),
            norms_ref[0:1, :],
            norms_ref[1:2, :],
            wide_row(d_bias),
            wide_row(jnp.where(live[:1], d_rate, 0.0)),
            jnp.zeros((1, DI), F32),
        ],
        axis=0,
    )
    both = [
        gin, gin_gate_ref[...], gout_ref[...], small, dot(d_bc, act, 0, 0),
        dot(d_raw, act, 0, 0)[:16],
    ]
    full = jnp.concatenate(both, axis=0)
    rest = small - small.astype(BF).astype(F32)
    pack_ref[0:448, :] = full[:, :128].astype(BF)
    pack_ref[448:672, :] = jnp.concatenate([full[:224, 128:], full[224:, 128:]], axis=1).astype(BF)
    pack_ref[672:688, :] = rest[:, :128].astype(BF)
    pack_ref[688:704, :] = jnp.concatenate(
        [rest[:, 128:], jnp.zeros((16, 64), F32)], axis=1
    ).astype(BF)
    pack_ref[704:1024, :] = jnp.zeros((320, T), BF)


def out_kernel(
    above_ref, own_ref, below_ref, left_ref, right_ref, cw_ref, dgate_ref, wbr_ref, wg_ref,
    out_ref, pad_ref,
):
    around = (above_ref, own_ref, below_ref, left_ref, right_ref)
    fill_rim(pad_ref, *(ref[...].astype(F32) for ref in around))
    total = jnp.zeros((R, C, DI), F32)
    for b in range(3):
        shifted = pad_ref[:, 9 - b : 9 - b + C, :]
        for a in range(3):
            total = total + cw_ref[3 * a + b : 3 * a + b + 1, :] * shifted[2 - a : 2 - a + R]
    d_branch = total.reshape(T, DI).astype(BF)
    out_ref[...] = (
        dot(d_branch, wbr_ref[...], 1, 1) + dot(dgate_ref[...], wg_ref[...], 1, 1)
    ).astype(BF)


def sum_kernel(scale, x_ref, out_ref):
    total = x_ref[0].astype(F32)
    for i in range(1, x_ref.shape[0]):
        total = total + x_ref[i].astype(F32)
    out_ref[...] = jnp.broadcast_to(total * scale, out_ref.shape)


def unpack_kernel(
    x_ref, gin_ref, conv_ref, cb_ref, scan_ref, sb_ref, ld_ref, skip_ref, gain_ref, nb_ref, gout_ref
):
    low, high = (x_ref[0:448, :], x_ref[448:672, :])
    full = jnp.concatenate(
        [low, jnp.concatenate([high[:, :64], high[:, 64:]], axis=0)], axis=1
    )
    rest = jnp.concatenate([x_ref[672:688, :], x_ref[688:704, :64]], axis=1)
    gin_ref[...] = jnp.concatenate([full[:96], full[96:192]], axis=1)
    gout_ref[...] = full[192:288].T
    small = full[288:304] + rest
    for a in range(3):
        conv_ref[a] = small[3 * a : 3 * a + 3]
    cb_ref[...] = small[9:10]
    skip_ref[...] = jnp.broadcast_to(small[10:11], (4, DI))
    gain_ref[...] = small[11:12]
    nb_ref[...] = small[12:13]
    for k in range(4):
        sb_ref[k : k + 1, :] = small[13:14, 3 * k : 3 * k + 3]
        ld_ref[k : k + 1, :] = small[14:15, 3 * k : 3 * k + 3]
    scan = jnp.concatenate([full[304:448], jnp.zeros((112, DI), F32)], axis=0).T
    for k in range(4):
        scan_ref[k] = jnp.concatenate(
            [
                scan[:, 128 + 3 * k : 131 + 3 * k],
                scan[:, 16 * k : 16 * k + 16],
                scan[:, 64 + 16 * k : 80 + 16 * k],
            ],
            axis=1,
        )


def call(kernel, outs, *args, flops=10**8, scratch=(), scalars=0):
    whole = pl.BlockSpec(memory_space=pltpu.VMEM)
    small = pl.BlockSpec(memory_space=pltpu.SMEM)
    return pl.pallas_call(
        kernel,
        out_shape=[jax.ShapeDtypeStruct(s, t) for s, t in outs],
        in_specs=[small] * scalars + [whole] * (len(args) - scalars),
        out_specs=[whole] * len(outs),
        scratch_shapes=list(scratch),
        compiler_params=pltpu.CompilerParams(vmem_limit_bytes=40 * 2**20),
        cost_estimate=pl.CostEstimate(flops=flops, bytes_accessed=10**6, transcendentals=0),
    )(*args)


def neighbours(last, first, axis):
    size = lax.axis_size(axis)
    up = [(i, i + 1) for i in range(size - 1)]
    down = [(j, i) for i, j in up]
    return lax.ppermute(last, axis, up), lax.ppermute(first, axis, down)


def with_rim(x):
    above, below = neighbours(x[T - C :], x[:C], "row")
    grid = x.reshape(R, C, -1)
    side = lambda c: jnp.concatenate([above[c : c + 1], grid[:, c], below[c : c + 1]], axis=0)
    left, right = neighbours(side(C - 1), side(0), "col")
    return above, x, below, left, right


def all_to_all(x, axis):
    return lax.all_to_all(x, axis, 0, 0, tiled=True)


def along_col(x):
    count = lax.axis_size("col")
    blocks = x[None]
    step = 1
    while step < count:
        pairs = [(i, i ^ step) for i in range(count)]
        blocks = jnp.concatenate([blocks, lax.ppermute(blocks, "col", pairs)], axis=0)
        step *= 2
    return blocks


def exchange(message, axis, backward):
    chunks = (64, 8, 128)
    got = all_to_all(message.reshape(chunks), axis).reshape(512, 128)
    (states,) = call(partial(chain_kernel, backward), [((512, 128), BF)], got, flops=10**7)
    return all_to_all(states.reshape(chunks), axis).reshape(512, 128)


def reduced(pack, scale):
    rows, cols = (lax.axis_size("row"), lax.axis_size("col"))
    chunk = pack.shape[0] // rows
    got = all_to_all(pack.reshape(rows, chunk, 128), "row")
    (part,) = call(partial(sum_kernel, 1.0), [((cols, chunk, 128), F32)], got, flops=10**7)
    got = all_to_all(part, "col")
    (part,) = call(partial(sum_kernel, scale), [((rows, chunk, 128), F32)], got, flops=10**7)
    return all_to_all(part, "row").reshape(pack.shape)


def local(
    tokens, in_weight, conv_weight, conv_bias, scan_weight, step_bias, log_decay, skip_gain, norm_gain,
    norm_bias, out_weight, cotangent,
):
    own = tokens.reshape(T, D)
    above, below = neighbours(own[T - C :], own[:C], "row")
    band = jnp.concatenate([above, own, below], axis=0)
    got = all_to_all(jnp.broadcast_to(band, (lax.axis_size("col"),) + band.shape), "col")
    place = lax.axis_index("col").reshape(1)
    cot = cotangent.reshape(T, D)
    w_branch, w_gate = (in_weight[:, :DI], in_weight[:, DI:])
    taps = jnp.pad(conv_weight.reshape(9, DI), ((0, 7), (0, 0)))
    by_channel = jnp.moveaxis(scan_weight, 1, 0)
    w_step = jnp.pad(by_channel[:, :, :HEADS].reshape(DI, 12), ((0, 0), (0, 116)))
    w_bc = jnp.concatenate(
        [
            by_channel[:, :, HEADS : HEADS + NS].reshape(DI, 64),
            by_channel[:, :, HEADS + NS :].reshape(DI, 64),
        ],
        axis=1,
    )
    row = lambda x: x.reshape(1, -1)
    bias = jnp.pad(row(step_bias), ((0, 0), (0, 116)))
    rate = jnp.pad(row(log_decay), ((0, 0), (0, 116)))
    skip = row(jnp.sum(skip_gain, axis=0))
    square = ((T, T), F32)
    wide = ((T, DI), F32)
    low = ((T, DI), BF)
    message = ((512, 128), BF)
    opened = pltpu.VMEM((64, 8, 128), F32)
    states = ((256, DI), F32)
    long = ((8 * T, T), F32)

    before, act, raw_d, bc, step, log, tot, mv = call(
        first_kernel, [wide, low, square, square, square, square, square, message],
        place, got, w_branch, taps, row(conv_bias), w_step, w_bc, bias, rate,
        scratch=[pltpu.VMEM((R + 2, PITCH, DI), F32), opened], scalars=1,
    )
    sv = exchange(mv, "row", False)
    s0, s1, later, gate_c = call(
        row_scan_kernel, [states, states, long, long],
        place, got, w_branch, taps, row(conv_bias), w_step, w_bc, bias, rate,
        scratch=[pltpu.VMEM((R + 2, 80, DI), F32)], scalars=1, flops=10**9,
    )
    (y,) = call(local_kernel, [wide], act, bc, step, log)
    out, g, d_gate, gated, norms, mv = call(
        norm_kernel, [((T, D), BF), low, low, low, ((8, DI), F32), message],
        y, act, bc, log, tot, sv, s0, s1, skip, own, w_gate, row(norm_gain), row(norm_bias), out_weight, cot,
        scratch=[opened],
    )
    lv = exchange(mv, "row", True)
    l0, l1 = call(
        row_back_kernel, [states, states], place, along_col(g), later, gate_c, scalars=1, flops=10**9
    )
    d_act, d_bc, d_step, d_log = call(
        back_kernel, [wide, square, square, square], act, bc, step, log, g, sv, s0, s1,
        scratch=[opened],
    )
    gin_gate, gout = call(
        gate_grads_kernel, [((D, DI), F32), ((D, DI), F32)], own, d_gate, gated, cot, flops=10**7
    )
    gb, pack = call(
        last_kernel, [low, ((1024, 128), BF)],
        place, got, w_branch, taps, before, act, raw_d, bc, step, log, tot, g, sv, s0, s1, lv, l0, l1, d_act, d_bc,
        d_step, d_log, skip, w_step, w_bc, bias, rate, gin_gate, gout, norms,
        scratch=[pltpu.VMEM((R + 2, PITCH, DI), F32), pltpu.VMEM((R + 2, PITCH, D), F32), opened, opened],
        scalars=1,
    )
    (d_tokens,) = call(
        out_kernel, [((T, D), BF)], *with_rim(gb), taps, d_gate, w_branch, w_gate,
        scratch=[pltpu.VMEM((R + 2, PITCH, DI), F32)],
    )
    scale = float(T * lax.axis_size("row") * lax.axis_size("col")) ** (-0.5)
    row_shape = ((1, DI), F32)
    gin, g_conv, g_cb, g_scan, g_bias, g_rate, g_skip, g_gain, g_shift, gout = call(
        unpack_kernel,
        [
            ((D, 2 * DI), F32), ((3, 3, DI), F32), row_shape, ((4, DI, HEADS + 2 * NS), F32),
            ((4, HEADS), F32), ((4, HEADS), F32), ((4, DI), F32), row_shape, row_shape, ((DI, D), F32),
        ],
        reduced(pack, scale), flops=10**7,
    )
    return (
        out.reshape(R, C * D), d_tokens.reshape(R, C * D), gin, g_conv, g_cb.reshape(DI), g_scan, g_bias,
        g_rate, g_skip, g_gain.reshape(DI), g_shift.reshape(DI), gout,
    )


def solution(mesh):
    in_specs = (P("row", "col"), P(), P(), P(), P(), P(), P(), P(), P(), P(), P(), P("row", "col"))
    out_specs = (P("row", "col"), P("row", "col"), P(), P(), P(), P(), P(), P(), P(), P(), P(), P())
    return jax.shard_map(local, mesh=mesh, in_specs=in_specs, out_specs=out_specs, check_vma=False)
```

```python
from functools import partial

import jax
import jax.numpy as jnp
from jax import lax
from jax.experimental import pallas as pl
from jax.experimental.pallas import tpu as pltpu
from jax.sharding import PartitionSpec as P

D = 96
DI = 192
NS = 16
HEADS = 3
R = 16
C = 8
T = R * C
PITCH = 24

F32 = jnp.float32
BF = jnp.bfloat16
FAR = -1e30


def dot(a, b, ca=1, cb=0):
    return lax.dot_general(a, b, (((ca,), (cb,)), ((), ())), preferred_element_type=F32)


def halves(x):
    if x.dtype == BF:
        return [x]
    high = x.astype(BF)
    return [high, (x - high.astype(F32)).astype(BF)]


def fine(a, b, ca=1, cb=0):
    a, b = (halves(a), halves(b))
    out = dot(a[0], b[0], ca, cb)
    for i, j in ((0, 1), (1, 0)):
        if i < len(a) and j < len(b):
            out = out + dot(a[i], b[j], ca, cb)
    return out


def iota(shape, dim):
    return lax.broadcasted_iota(jnp.int32, shape, dim)


def mask(k):
    t, s = (iota((T, T), 0), iota((T, T), 1))
    rt, ct, rs, cs = (t >> 3, t & 7, s >> 3, s & 7)
    if k == 0:
        return (rt == rs) & (cs <= ct)
    if k == 1:
        return (rt == rs) & (cs >= ct)
    if k == 2:
        return (ct == cs) & (rs <= rt)
    return (ct == cs) & (rs >= rt)


def same_line(vertical):
    t, s = (iota((T, T), 0), iota((T, T), 1))
    return (t & 7) == (s & 7) if vertical else (t >> 3) == (s >> 3)


def pick_lanes(parts):
    lane = iota((T, T), 1) // 3
    out = parts[3]
    for k in range(3):
        out = jnp.where(lane == k, parts[k], out)
    return out


def as_f32(m):
    return jnp.where(m, 1.0, 0.0).astype(F32)


def ones(m):
    return as_f32(m).astype(BF)


def states_of(k):
    return 256 if k < 2 else 128


def line_and_entry(j, k):
    if k < 2:
        return (j >> 4, j & 15)
    return ((j >> 3) & 7, 2 * (j & 7) + (j >> 6))


def on_line(k):
    t, j = (iota((T, states_of(k)), 0), iota((T, states_of(k)), 1))
    return line_and_entry(j, k)[0] == (t >> 3 if k < 2 else t & 7)


def spread_states(bc, k):
    i, j = (iota((T, states_of(k)), 0), iota((T, states_of(k)), 1))
    wide = fine(bc, ones(i == 16 * k + line_and_entry(j, k)[1]))
    return jnp.where(on_line(k), wide, 0.0)


def gather_states(wide, k):
    j, i = (iota((states_of(k), T), 0), iota((states_of(k), T), 1))
    entry = line_and_entry(j, k)[1]
    return fine(jnp.where(on_line(k), wide, 0.0), ones(i == 16 * k + entry))


def by_head(values, k):
    lane = iota((T, DI), 1)
    a, b, c = (values[:, 3 * k + h : 3 * k + h + 1] for h in range(HEADS))
    return jnp.where(lane < 64, a, jnp.where(lane < 128, b, c))


def head_sum(wide, k):
    c, j = (iota((DI, T), 0), iota((DI, T), 1))
    return fine(wide, ones(j == 3 * k + c // 64))


def per_head(f):
    lane = iota((T, DI), 1)
    a, b, c = (f(h) for h in range(HEADS))
    return jnp.where(lane < 64, a, jnp.where(lane < 128, b, c))


def write_message(ref, wide_ref, states, totals):
    for d in range(2):
        s = states[d]
        for h in range(HEADS):
            wide_ref[:, d * 3 + h, :] = jnp.concatenate(
                [s[:64, 64 * h : 64 * h + 64], s[64:, 64 * h : 64 * h + 64]], axis=1
            )
    j, t = (iota((64, T), 0), iota((64, T), 1))
    i, o = (iota((T, T), 0), iota((T, T), 1))
    totals = fine(ones(t == (j >> 3)), fine(totals, ones(i == o + 6)))
    high = totals.astype(BF).astype(F32)
    wide_ref[:, 6, :] = high
    wide_ref[:, 7, :] = totals - high
    ref[...] = wide_ref[...].reshape(512, 128).astype(BF)


def open_message(ref, wide_ref):
    wide_ref[...] = ref[...].astype(F32).reshape(64, 8, 128)


def read_message(ref, d):
    x = [ref[:, d * 3 + h, :] for h in range(HEADS)]
    top = jnp.concatenate([v[:, :64] for v in x], axis=1)
    bottom = jnp.concatenate([v[:, 64:] for v in x], axis=1)
    return jnp.concatenate([top, bottom], axis=0)


def chain_kernel(backward, got_ref, out_ref):
    m = 512 // lax.axis_size("row")
    n = 512 // m
    got = got_ref[...].astype(F32).reshape(n, m // 8, 8, 128)
    shape = (m // 8, 8, 128)
    sub, lane = (iota(shape, 1), iota(shape, 2))
    ahead = sub < 3 if not backward else sub >= 3

    def factor(i):
        row = jnp.broadcast_to(got[i, :, 6:7, :] + got[i, :, 7:8, :], shape)
        return jnp.sum(jnp.where(lane == sub, row, 0.0), axis=2, keepdims=True)

    factors = [factor(i) for i in range(n)]
    up = [jnp.zeros(shape, F32)]
    for i in range(n - 1):
        up.append(factors[i] * up[i] + got[i])
    down = [jnp.zeros(shape, F32)]
    for i in range(n - 1, 0, -1):
        down.append(factors[i] * down[-1] + got[i])
    down = down[::-1]
    full = jnp.concatenate([jnp.where(ahead, u, v) for u, v in zip(up, down)], axis=0)
    out_ref[...] = full.reshape(512, 128).astype(BF)


def state_in(k, rows, columns):
    return rows[k][...] if k < 2 else read_message(columns, k - 2)


def sigmoid(x):
    return jax.nn.sigmoid(x)


def softplus(x):
    return jnp.maximum(x, 0.0) + jnp.log1p(jnp.exp(-jnp.abs(x)))


def fill_rim(pad_ref, above, own, below, left, right):
    pad_ref[0:1, 8:16, :] = above.reshape(1, C, -1)
    pad_ref[1 : R + 1, 8:16, :] = own.reshape(R, C, -1)
    pad_ref[R + 1 : R + 2, 8:16, :] = below.reshape(1, C, -1)
    for r in range(R + 2):
        pad_ref[r, 7:8, :] = left[r : r + 1]
        pad_ref[r, 16:17, :] = right[r : r + 1]


def edge_factor(me, blocks, j):
    return jnp.clip(j, 0, blocks - 1), jnp.where((j >= 0) & (j < blocks), 1.0, 0.0)


def fill_blocks(me, got_ref, edge_refs, pad_ref, f):
    for i, edge_ref in enumerate(edge_refs):
        at, inside = edge_factor(me, got_ref.shape[0], me + i - 1)
        place = slice(8 * i, 8 * i + 8)
        edge = f(edge_ref[...])
        pad_ref[0:1, place, :] = edge[:C].reshape(1, C, -1)
        pad_ref[1 : R + 1, place, :] = f(got_ref[at]).reshape(R, C, -1) * inside
        pad_ref[R + 1 : R + 2, place, :] = edge[C:].reshape(1, C, -1)


def as_branch(wbr_ref):
    return lambda x: dot(x, wbr_ref[...]).astype(BF).astype(F32)


def first_kernel(
    me_ref, got_ref, left_ref, edge_ref, right_ref, wbr_ref, cw_ref, cb_ref, wd_ref, wbc_ref, sb_ref, ld_ref,
    before_ref, act_ref, rawd_ref, bc_ref, step_ref, log_ref, tot_ref, mv_ref, pad_ref, wide_ref,
):
    edges = (left_ref, edge_ref, right_ref)
    fill_blocks(me_ref[0], got_ref, edges, pad_ref, as_branch(wbr_ref))
    total = jnp.zeros((R, C, DI), F32)
    for b in range(3):
        shifted = pad_ref[:, 7 + b : 7 + b + C, :]
        for a in range(3):
            total = total + cw_ref[3 * a + b : 3 * a + b + 1, :] * shifted[a : a + R]
    before = total.reshape(T, DI) + cb_ref[...]
    act = (before * sigmoid(before)).astype(BF)
    before_ref[...] = before
    act_ref[...] = act
    raw_d = dot(act, wd_ref[...])
    bc = dot(act, wbc_ref[...])
    step = softplus(raw_d + sb_ref[...])
    log_step = step * -jnp.exp(ld_ref[...])
    log = pick_lanes([fine(ones(mask(k)), log_step) for k in range(4)])
    rows, cols = (fine(ones(same_line(v)), log_step) for v in (False, True))
    tot = pick_lanes([rows, rows, cols, cols])
    rawd_ref[...] = raw_d
    bc_ref[...] = bc
    step_ref[...] = step
    log_ref[...] = log
    tot_ref[...] = tot
    weight = jnp.exp(tot - log) * step
    wide = act.astype(F32)
    states = [
        fine(spread_states(bc, k), by_head(weight, k) * wide, 0, 0) for k in (2, 3)
    ]
    write_message(mv_ref, wide_ref, states, jnp.exp(tot))


def row_pair(me, blocks_ref, group):
    lines = []
    for r in range(2):
        at = pl.ds(16 * group, 16)
        for j in range(8):
            lines.append(blocks_ref[me ^ j, at, :].astype(F32)[8 * r : 8 * r + 8])
    return jnp.concatenate(lines, axis=0)


def row_scan_kernel(
    me_ref, got_ref, edges_ref, wbr_ref, cw_ref, cb_ref, wd_ref, wbc_ref, sb_ref, ld_ref,
    s0_ref, s1_ref, later_ref, gate_ref, pad_ref,
):
    nothing = jnp.zeros((R + 2, 8, DI), F32)
    pad_ref[:, 0:8, :] = nothing
    pad_ref[:, 72:80, :] = nothing
    for j in range(8):
        place = slice(8 + 8 * j, 16 + 8 * j)
        edge = as_branch(wbr_ref)(edges_ref[me_ref[0] ^ j])
        pad_ref[0:1, place, :] = edge[:C].reshape(1, C, DI)
        pad_ref[1 : R + 1, place, :] = as_branch(wbr_ref)(got_ref[j]).reshape(R, C, DI)
        pad_ref[R + 1 : R + 2, place, :] = edge[C:].reshape(1, C, DI)
    low = me_ref[0] * C
    high = low + C
    t, u = (iota((T, T), 0), iota((T, T), 1))
    same = (t >> 6) == (u >> 6)
    t, u = (t & 63, u & 63)
    reach = [
        same & (u > t) & (u < low),
        same & (u < t) & (u >= high),
        same & (u <= t) & (u >= high),
        same & (u >= t) & (u < low),
    ]
    reach = jnp.concatenate([ones(m) for m in reach], axis=0)
    before, after = (t < low, t >= high)
    first = iota((T, T), 1) < 3
    valid_in = jnp.where(first, as_f32(before), as_f32(after))
    valid_out = jnp.where(first, as_f32(after), as_f32(before))
    tj, j = (iota((T, 32), 0), iota((T, 32), 1))
    line = (tj >> 6) == (j >> 4)
    i, ji = (iota((T, 32), 0), iota((T, 32), 1))
    rate = -jnp.exp(ld_ref[...])
    for group in range(R // 2):
        total = jnp.zeros((2, 64, DI), F32)
        for b in range(3):
            shifted = pad_ref[2 * group : 2 * group + 4, 7 + b : 71 + b, :]
            for a in range(3):
                total = total + cw_ref[3 * a + b : 3 * a + b + 1, :] * shifted[a : a + 2]
        wide = total.reshape(T, DI) + cb_ref[...]
        act = (wide * sigmoid(wide)).astype(BF)
        wide = act.astype(F32)
        step = softplus(dot(act, wd_ref[...]) + sb_ref[...])
        bc = dot(act, wbc_ref[...])
        x = fine(reach, step * rate)
        w_in = jnp.exp(jnp.where(first, x[:T], x[T : 2 * T])) * step * valid_in
        later_ref[group * T : group * T + T, :] = (
            jnp.exp(jnp.where(first, x[2 * T : 3 * T], x[3 * T :])) * valid_out
        )
        gate_ref[group * T : group * T + T, :] = shifted_gate(bc)
        for k, ref in enumerate((s0_ref, s1_ref)):
            entry = ones(i == 16 * k + (ji & 15))
            spread = jnp.where(line, fine(bc, entry), 0.0)
            ref[32 * group : 32 * group + 32, :] = fine(spread, by_head(w_in, k) * wide, 0, 0)


def row_back_kernel(me_ref, blocks_ref, later_ref, gate_ref, l0_ref, l1_ref):
    tj, j = (iota((T, 32), 0), iota((T, 32), 1))
    line = (tj >> 6) == (j >> 4)
    for group in range(R // 2):
        part = slice(group * T, group * T + T)
        g = row_pair(me_ref[0], blocks_ref, group)
        later = later_ref[part, :]
        gate = gate_ref[part, :]
        for k, ref in enumerate((l0_ref, l1_ref)):
            entry = ones(tj == 16 * k + (j & 15))
            spread = jnp.where(line, fine(gate, entry), 0.0)
            ref[32 * group : 32 * group + 32, :] = fine(spread, by_head(later, k) * g, 0, 0)


def tables(k, bc, out_gate):
    lane = iota((T, T), 1) >> 4
    return fine(jnp.where(lane == k, out_gate, 0.0), bc, 1, 1)


def decay(k, h, log, log_t):
    i = 3 * k + h
    return jnp.exp(jnp.where(mask(k), log[:, i : i + 1] - log_t[i : i + 1, :], FAR))


def shifted_gate(bc):
    return pltpu.roll(bc, 64, 1)


def local_kernel(act_ref, bc_ref, step_ref, log_ref, y_ref):
    bc = bc_ref[...]
    out_gate = shifted_gate(bc)
    log = log_ref[...]
    log_t, step_t = (log.T, step_ref[...].T)
    weights = [jnp.zeros((T, T), F32)] * HEADS
    for k in range(4):
        scores = tables(k, bc, out_gate)
        for h in range(HEADS):
            i = 3 * k + h
            weights[h] = weights[h] + scores * (
                decay(k, h, log, log_t) * step_t[i : i + 1, :]
            )
    act = act_ref[...]
    y_ref[...] = per_head(lambda h: fine(weights[h], act))


def carry(k, out_gate, exp_log, state):
    return by_head(exp_log, k) * fine(spread_states(out_gate, k), state)


def norm_kernel(
    y_ref, act_ref, bc_ref, log_ref, tot_ref, sv_ref, s0_ref, s1_ref, skip_ref, tok_ref, wg_ref, gain_ref,
    nb_ref, ow_ref, cot_ref,
    out_ref, g_ref, dgate_ref, gated_ref, norms_ref, mv_ref, wide_ref,
):
    open_message(sv_ref, wide_ref)
    bc = bc_ref[...]
    out_gate = shifted_gate(bc)
    exp_log = jnp.exp(log_ref[...])
    summed = y_ref[...] + skip_ref[...] * act_ref[...].astype(F32)
    for k in range(4):
        state = state_in(k, (s0_ref, s1_ref), wide_ref)
        summed = summed + carry(k, out_gate, exp_log, state)
    gate = dot(tok_ref[...], wg_ref[...]).astype(BF).astype(F32)
    sig = sigmoid(gate)
    center = summed - jnp.mean(summed, axis=1, keepdims=True)
    inv = lax.rsqrt(jnp.mean(center * center, axis=1, keepdims=True) + 1e-5)
    unit = center * inv
    normed = unit * gain_ref[...] + nb_ref[...]
    gated = (normed * gate * sig).astype(BF)
    gated_ref[...] = gated
    out_ref[...] = dot(gated, ow_ref[...]).astype(BF)
    grad = dot(cot_ref[...], ow_ref[...], 1, 1)
    dnormed = grad * gate * sig
    dgate_ref[...] = (grad * normed * (sig * (1.0 + gate * (1.0 - sig)))).astype(BF)
    norms_ref[0:1, :] = jnp.sum(dnormed * unit, axis=0, keepdims=True)
    norms_ref[1:2, :] = jnp.sum(dnormed, axis=0, keepdims=True)
    dunit = dnormed * gain_ref[...]
    g = inv * (
        dunit
        - jnp.mean(dunit, axis=1, keepdims=True)
        - unit * jnp.mean(dunit * unit, axis=1, keepdims=True)
    )
    g = g.astype(BF)
    g_ref[...] = g
    g = g.astype(F32)
    states = [
        fine(spread_states(out_gate, k), by_head(exp_log, k) * g, 0, 0) for k in (2, 3)
    ]
    write_message(mv_ref, wide_ref, states, jnp.exp(tot_ref[...]))


def back_kernel(
    act_ref, bc_ref, step_ref, log_ref, g_ref, sv_ref, s0_ref, s1_ref,
    dact_ref, dbc_ref, dstep_ref, dlog_ref, wide_ref,
):
    open_message(sv_ref, wide_ref)
    bc = bc_ref[...]
    out_gate = shifted_gate(bc)
    log = log_ref[...]
    step = step_ref[...]
    log_t, step_t = (log.T, step.T)
    exp_log = jnp.exp(log)
    act = act_ref[...]
    g = g_ref[...]
    gw = g.astype(F32)
    lane = iota((T, DI), 1) // 64
    lane16 = iota((T, T), 1) >> 4
    lane1 = iota((T, T), 1)
    pair = [dot(jnp.where(lane == h, g, jnp.zeros_like(g)), act, 1, 1) for h in range(HEADS)]
    weights = [jnp.zeros((T, T), F32)] * HEADS
    d_in = jnp.zeros((T, T), F32)
    d_out = jnp.zeros((T, T), F32)
    row_sums = jnp.zeros((T, T), F32)
    step_rows = []
    for k in range(4):
        scores = tables(k, bc, out_gate)
        d_scores = jnp.zeros((T, T), F32)
        for h in range(HEADS):
            i = 3 * k + h
            dec = decay(k, h, log, log_t)
            dec_step = dec * step_t[i : i + 1, :]
            weights[h] = weights[h] + scores * dec_step
            d_scores = d_scores + pair[h] * dec_step
            d_step = pair[h] * dec * scores
            step_rows.append(jnp.sum(d_step, axis=0, keepdims=True))
            rows = jnp.sum(d_step * step_t[i : i + 1, :], axis=1, keepdims=True)
            row_sums = jnp.where(lane1 == i, rows, row_sums)
        d_out = d_out + fine(d_scores, jnp.where(lane16 == k, bc, 0.0))
        d_in = d_in + fine(d_scores, jnp.where(lane16 == k, out_gate, 0.0), 0, 0)
        state = state_in(k, (s0_ref, s1_ref), wide_ref)
        expg = by_head(exp_log, k) * gw
        carried = fine(spread_states(out_gate, k), state)
        row_sums = row_sums + head_sum(carried * expg, k)
        d_out = d_out + gather_states(fine(expg, state, 1, 1), k)
    d_step = jnp.concatenate(step_rows + [jnp.zeros((T - 12, T), F32)], axis=0).T
    dact_ref[...] = per_head(lambda h: fine(weights[h], g, 0, 0))
    dbc_ref[...] = d_in + pltpu.roll(d_out, 64, 1)
    dstep_ref[...] = d_step
    dlog_ref[...] = row_sums - step * d_step


def gate_grads_kernel(tok_ref, dgate_ref, gated_ref, cot_ref, gin_ref, gout_ref):
    gin_ref[...] = dot(tok_ref[...], dgate_ref[...], 0, 0)
    gout_ref[...] = dot(cot_ref[...], gated_ref[...], 0, 0)


def last_kernel(
    me_ref, got_ref, left_ref, edge_ref, right_ref, wbr_ref, cw_ref, before_ref, act_ref, rawd_ref, bc_ref, step_ref, log_ref, tot_ref, g_ref,
    sv_ref, s0_ref, s1_ref, lv_ref, l0_ref, l1_ref, dact_ref, dbc_ref, dstep_ref, dlog_ref, skip_ref, wd_ref, wbc_ref,
    sb_ref, ld_ref, gin_gate_ref, gout_ref, norms_ref,
    gb_ref, pack_ref, pad_ref, tok_ref, early_ref, late_ref,
):
    open_message(sv_ref, early_ref)
    open_message(lv_ref, late_ref)
    step, log, tot, bc = (step_ref[...], log_ref[...], tot_ref[...], bc_ref[...])
    act = act_ref[...]
    wide = act.astype(F32)
    g = g_ref[...].astype(F32)
    d_act = dact_ref[...] + skip_ref[...] * g
    d_bc = dbc_ref[...]
    to_end = jnp.exp(tot - log)
    weight = to_end * step
    through = jnp.exp(tot)
    inner = jnp.zeros((T, T), F32)
    cross = jnp.zeros((T, T), F32)
    for k in range(4):
        later = state_in(k, (l0_ref, l1_ref), late_ref)
        earlier = state_in(k, (s0_ref, s1_ref), early_ref)
        reach = fine(spread_states(bc, k), later)
        wk = by_head(weight, k)
        d_act = d_act + wk * reach
        inner = inner + head_sum(wide * reach, k)
        d_bc = d_bc + gather_states(fine(wk * wide, later, 1, 1), k)
        cross = cross + fine(ones(on_line(k)), head_sum(later * earlier, k))
    d_step = dstep_ref[...] + to_end * inner
    left = weight * inner
    d_log = dlog_ref[...]
    parts = []
    for k in range(4):
        after = mask(k ^ 1)
        rest = same_line(k >= 2) & jnp.logical_not(after)
        parts.append(fine(ones(after), d_log) + fine(ones(rest), left))
    d_log_step = pick_lanes(parts) + cross * through
    rate = -jnp.exp(ld_ref[...])
    d_rate = jnp.sum(d_log_step * step, axis=0, keepdims=True) * rate
    d_raw = (d_step + rate * d_log_step) * sigmoid(rawd_ref[...] + sb_ref[...])
    live = iota((T, T), 1) < 12
    d_raw = jnp.where(live, d_raw, 0.0)
    d_bias = jnp.sum(d_raw, axis=0, keepdims=True)
    d_raw = d_raw.astype(BF)
    d_bc = d_bc.astype(BF)
    d_act = d_act + dot(d_raw, wd_ref[...], 1, 1) + dot(d_bc, wbc_ref[...], 1, 1)
    before = before_ref[...]
    sig = sigmoid(before)
    gb = (d_act * sig * (1.0 + before * (1.0 - sig))).astype(BF)
    gb_ref[...] = gb
    gbw = gb.astype(F32)
    edges = (left_ref, edge_ref, right_ref)
    fill_blocks(me_ref[0], got_ref, edges, pad_ref, as_branch(wbr_ref))
    fill_blocks(me_ref[0], got_ref, edges, tok_ref, lambda x: x.astype(F32))
    gin = jnp.zeros((D, DI), F32)
    conv_rows = [None] * 9
    for b in range(3):
        near = pad_ref[:, 7 + b : 7 + b + C, :]
        near_tok = tok_ref[:, 7 + b : 7 + b + C, :]
        for a in range(3):
            i = 3 * a + b
            conv_rows[i] = jnp.sum(gbw * near[a : a + R].reshape(T, DI), axis=0, keepdims=True)
            gin = gin + cw_ref[i : i + 1, :] * dot(
                near_tok[a : a + R].reshape(T, D).astype(BF), gb, 0, 0
            )
    wide_row = lambda x: jnp.concatenate([x, jnp.zeros((1, DI - T), F32)], axis=1)
    small = jnp.concatenate(
        conv_rows
        + [
            jnp.sum(gbw, axis=0, keepdims=True),
            jnp.sum(g * wide, axis=0, keepdims=True),
            norms_ref[0:1, :],
            norms_ref[1:2, :],
            wide_row(d_bias),
            wide_row(jnp.where(live[:1], d_rate, 0.0)),
            jnp.zeros((1, DI), F32),
        ],
        axis=0,
    )
    both = [
        gin, gin_gate_ref[...], gout_ref[...], small, dot(d_bc, act, 0, 0),
        dot(d_raw, act, 0, 0)[:16],
    ]
    full = jnp.concatenate(both, axis=0)
    rest = small - small.astype(BF).astype(F32)
    pack_ref[0:448, :] = full[:, :128].astype(BF)
    pack_ref[448:672, :] = jnp.concatenate([full[:224, 128:], full[224:, 128:]], axis=1).astype(BF)
    pack_ref[672:688, :] = rest[:, :128].astype(BF)
    pack_ref[688:704, :] = jnp.concatenate(
        [rest[:, 128:], jnp.zeros((16, 64), F32)], axis=1
    ).astype(BF)
    pack_ref[704:1024, :] = jnp.zeros((320, T), BF)


def out_kernel(
    above_ref, own_ref, below_ref, left_ref, right_ref, cw_ref, dgate_ref, wbr_ref, wg_ref,
    out_ref, pad_ref,
):
    around = (above_ref, own_ref, below_ref, left_ref, right_ref)
    fill_rim(pad_ref, *(ref[...].astype(F32) for ref in around))
    total = jnp.zeros((R, C, DI), F32)
    for b in range(3):
        shifted = pad_ref[:, 9 - b : 9 - b + C, :]
        for a in range(3):
            total = total + cw_ref[3 * a + b : 3 * a + b + 1, :] * shifted[2 - a : 2 - a + R]
    d_branch = total.reshape(T, DI).astype(BF)
    out_ref[...] = (
        dot(d_branch, wbr_ref[...], 1, 1) + dot(dgate_ref[...], wg_ref[...], 1, 1)
    ).astype(BF)


def sum_kernel(scale, x_ref, out_ref):
    total = x_ref[0].astype(F32)
    for i in range(1, x_ref.shape[0]):
        total = total + x_ref[i].astype(F32)
    out_ref[...] = jnp.broadcast_to((total * scale).astype(out_ref.dtype), out_ref.shape)


def unpack_kernel(
    x_ref, gin_ref, conv_ref, cb_ref, scan_ref, sb_ref, ld_ref, skip_ref, gain_ref, nb_ref, gout_ref
):
    low, high = (x_ref[0:448, :].astype(F32), x_ref[448:672, :].astype(F32))
    full = jnp.concatenate(
        [low, jnp.concatenate([high[:, :64], high[:, 64:]], axis=0)], axis=1
    )
    rest = jnp.concatenate([x_ref[672:688, :], x_ref[688:704, :64]], axis=1).astype(F32)
    gin_ref[...] = jnp.concatenate([full[:96], full[96:192]], axis=1)
    gout_ref[...] = full[192:288].T
    small = full[288:304] + rest
    for a in range(3):
        conv_ref[a] = small[3 * a : 3 * a + 3]
    cb_ref[...] = small[9:10]
    skip_ref[...] = jnp.broadcast_to(small[10:11], (4, DI))
    gain_ref[...] = small[11:12]
    nb_ref[...] = small[12:13]
    for k in range(4):
        sb_ref[k : k + 1, :] = small[13:14, 3 * k : 3 * k + 3]
        ld_ref[k : k + 1, :] = small[14:15, 3 * k : 3 * k + 3]
    for k in range(4):
        scan_ref[0:3, k, :] = full[432 + 3 * k : 435 + 3 * k]
        scan_ref[3:19, k, :] = full[304 + 16 * k : 320 + 16 * k]
        scan_ref[19:35, k, :] = full[368 + 16 * k : 384 + 16 * k]


def call(kernel, outs, *args, flops=10**8, scratch=(), scalars=0):
    whole = pl.BlockSpec(memory_space=pltpu.VMEM)
    small = pl.BlockSpec(memory_space=pltpu.SMEM)
    return pl.pallas_call(
        kernel,
        out_shape=[jax.ShapeDtypeStruct(s, t) for s, t in outs],
        in_specs=[small] * scalars + [whole] * (len(args) - scalars),
        out_specs=[whole] * len(outs),
        scratch_shapes=list(scratch),
        compiler_params=pltpu.CompilerParams(vmem_limit_bytes=40 * 2**20),
        cost_estimate=pl.CostEstimate(flops=flops, bytes_accessed=10**6, transcendentals=0),
    )(*args)


def neighbours(last, first, axis):
    size = lax.axis_size(axis)
    up = [(i, i + 1) for i in range(size - 1)]
    down = [(j, i) for i, j in up]
    return lax.ppermute(last, axis, up), lax.ppermute(first, axis, down)


def with_rim(x):
    above, below = neighbours(x[T - C :], x[:C], "row")
    grid = x.reshape(R, C, -1)
    side = lambda c: jnp.concatenate([above[c : c + 1], grid[:, c], below[c : c + 1]], axis=0)
    left, right = neighbours(side(C - 1), side(0), "col")
    return above, x, below, left, right


def all_to_all(x, axis):
    return lax.all_to_all(x, axis, 0, 0, tiled=True)


def swapped(x, step):
    return lax.ppermute(x, "col", [(i, i ^ step) for i in range(lax.axis_size("col"))])


def in_pairs(x):
    return jnp.stack([x, swapped(x, 1)])


def along_col(pair):
    others = [swapped(pair, step) for step in range(2, lax.axis_size("col"), 2)]
    return jnp.concatenate([pair] + others, axis=0)


def exchange(message, axis, backward, meanwhile=()):
    chunks = (64, 8, 128)
    got, meanwhile = lax.optimization_barrier(
        (all_to_all(message.reshape(chunks), axis).reshape(512, 128), meanwhile)
    )
    (states,) = call(partial(chain_kernel, backward), [((512, 128), BF)], got, flops=10**7)
    return all_to_all(states.reshape(chunks), axis).reshape(512, 128), meanwhile


def reduced(pack, scale, meanwhile):
    rows, cols = (lax.axis_size("row"), lax.axis_size("col"))
    chunk = pack.shape[0] // rows
    got = all_to_all(pack.reshape(rows, chunk, 128), "row")
    (part,) = call(partial(sum_kernel, 1.0), [((cols, chunk, 128), F32)], got, flops=10**7)
    part, meanwhile = lax.optimization_barrier((part, meanwhile))
    got = all_to_all(part, "col")
    (part,) = call(partial(sum_kernel, scale), [((rows, chunk, 128), BF)], got, flops=10**7)
    return all_to_all(part, "row").reshape(pack.shape), meanwhile


def local(
    tokens, in_weight, conv_weight, conv_bias, scan_weight, step_bias, log_decay, skip_gain, norm_gain,
    norm_bias, out_weight, cotangent,
):
    own = tokens.reshape(T, D)
    count = lax.axis_size("col")
    got = all_to_all(jnp.broadcast_to(tokens, (count,) + tokens.shape), "col").reshape(count, T, D)
    edge = jnp.concatenate(neighbours(own[T - C :], own[:C], "row"), axis=0)
    left, right = neighbours(edge, edge, "col")
    place = lax.axis_index("col").reshape(1)
    cot = cotangent.reshape(T, D)
    w_branch, w_gate = (in_weight[:, :DI], in_weight[:, DI:])
    taps = jnp.pad(conv_weight.reshape(9, DI), ((0, 7), (0, 0)))
    by_channel = jnp.moveaxis(scan_weight, 1, 0)
    w_step = jnp.pad(by_channel[:, :, :HEADS].reshape(DI, 12), ((0, 0), (0, 116)))
    w_bc = jnp.concatenate(
        [
            by_channel[:, :, HEADS : HEADS + NS].reshape(DI, 64),
            by_channel[:, :, HEADS + NS :].reshape(DI, 64),
        ],
        axis=1,
    )
    row = lambda x: x.reshape(1, -1)
    bias = jnp.pad(row(step_bias), ((0, 0), (0, 116)))
    rate = jnp.pad(row(log_decay), ((0, 0), (0, 116)))
    skip = row(jnp.sum(skip_gain, axis=0))
    square = ((T, T), F32)
    wide = ((T, DI), F32)
    low = ((T, DI), BF)
    message = ((512, 128), BF)
    opened = pltpu.VMEM((64, 8, 128), F32)
    states = ((256, DI), F32)
    long = ((8 * T, T), F32)

    before, act, raw_d, bc, step, log, tot, mv = call(
        first_kernel, [wide, low, square, square, square, square, square, message],
        place, got, left, edge, right, w_branch, taps, row(conv_bias), w_step, w_bc, bias, rate,
        scratch=[pltpu.VMEM((R + 2, PITCH, DI), F32), opened], scalars=1,
    )
    mv, edge_pair = lax.optimization_barrier((mv, in_pairs(edge)))
    sv, edges = exchange(mv, "row", False, along_col(edge_pair))
    s0, s1, later, gate_c = call(
        row_scan_kernel, [states, states, long, long],
        place, got, edges, w_branch, taps, row(conv_bias), w_step, w_bc, bias, rate,
        scratch=[pltpu.VMEM((R + 2, 80, DI), F32)], scalars=1, flops=10**9,
    )
    (y,) = call(local_kernel, [wide], act, bc, step, log)
    out, g, d_gate, gated, norms, mv = call(
        norm_kernel, [((T, D), BF), low, low, low, ((8, DI), F32), message],
        y, act, bc, log, tot, sv, s0, s1, skip, own, w_gate, row(norm_gain), row(norm_bias), out_weight, cot,
        scratch=[opened],
    )
    lv, pair = exchange(mv, "row", True, in_pairs(g))
    d_act, d_bc, d_step, d_log = call(
        back_kernel, [wide, square, square, square], act, bc, step, log, g, sv, s0, s1,
        scratch=[opened],
    )
    l0, l1 = call(
        row_back_kernel, [states, states], place, along_col(pair), later, gate_c, scalars=1, flops=10**9
    )
    gin_gate, gout = call(
        gate_grads_kernel, [((D, DI), F32), ((D, DI), F32)], own, d_gate, gated, cot, flops=10**7
    )
    gb, pack = call(
        last_kernel, [low, ((1024, 128), BF)],
        place, got, left, edge, right, w_branch, taps, before, act, raw_d, bc, step, log, tot, g, sv, s0, s1, lv, l0, l1, d_act, d_bc,
        d_step, d_log, skip, w_step, w_bc, bias, rate, gin_gate, gout, norms,
        scratch=[pltpu.VMEM((R + 2, PITCH, DI), F32), pltpu.VMEM((R + 2, PITCH, D), F32), opened, opened],
        scalars=1,
    )
    scale = float(T * lax.axis_size("row") * lax.axis_size("col")) ** (-0.5)
    total, rim = reduced(pack, scale, with_rim(gb))
    (d_tokens,) = call(
        out_kernel, [((T, D), BF)], *rim, taps, d_gate, w_branch, w_gate,
        scratch=[pltpu.VMEM((R + 2, PITCH, DI), F32)],
    )
    row_shape = ((1, DI), F32)
    gin, g_conv, g_cb, g_scan, g_bias, g_rate, g_skip, g_gain, g_shift, gout = call(
        unpack_kernel,
        [
            ((D, 2 * DI), F32), ((3, 3, DI), F32), row_shape, ((HEADS + 2 * NS, 4, DI), F32),
            ((4, HEADS), F32), ((4, HEADS), F32), ((4, DI), F32), row_shape, row_shape, ((DI, D), F32),
        ],
        total, flops=10**7,
    )
    return (
        out.reshape(R, C * D), d_tokens.reshape(R, C * D), gin, g_conv, g_cb.reshape(DI),
        jnp.transpose(g_scan, (1, 2, 0)), g_bias,
        g_rate, g_skip, g_gain.reshape(DI), g_shift.reshape(DI), gout,
    )


def solution(mesh):
    in_specs = (P("row", "col"), P(), P(), P(), P(), P(), P(), P(), P(), P(), P(), P("row", "col"))
    out_specs = (P("row", "col"), P("row", "col"), P(), P(), P(), P(), P(), P(), P(), P(), P(), P())
    return jax.shard_map(local, mesh=mesh, in_specs=in_specs, out_specs=out_specs, check_vma=False)
```

```python
from functools import partial

import jax
import jax.numpy as jnp
from jax import lax
from jax.experimental import pallas as pl
from jax.experimental.pallas import tpu as pltpu
from jax.sharding import PartitionSpec as P

D = 96
DI = 192
NS = 16
HEADS = 3
R = 16
C = 8
T = R * C
PITCH = 24

F32 = jnp.float32
BF = jnp.bfloat16
FAR = -1e30


def dot(a, b, ca=1, cb=0):
    return lax.dot_general(a, b, (((ca,), (cb,)), ((), ())), preferred_element_type=F32)


def halves(x):
    if x.dtype == BF:
        return [x]
    high = x.astype(BF)
    return [high, (x - high.astype(F32)).astype(BF)]


def fine(a, b, ca=1, cb=0):
    a, b = (halves(a), halves(b))
    out = dot(a[0], b[0], ca, cb)
    for i, j in ((0, 1), (1, 0)):
        if i < len(a) and j < len(b):
            out = out + dot(a[i], b[j], ca, cb)
    return out


def iota(shape, dim):
    return lax.broadcasted_iota(jnp.int32, shape, dim)


def mask(k):
    t, s = (iota((T, T), 0), iota((T, T), 1))
    rt, ct, rs, cs = (t >> 3, t & 7, s >> 3, s & 7)
    if k == 0:
        return (rt == rs) & (cs <= ct)
    if k == 1:
        return (rt == rs) & (cs >= ct)
    if k == 2:
        return (ct == cs) & (rs <= rt)
    return (ct == cs) & (rs >= rt)


def same_line(vertical):
    t, s = (iota((T, T), 0), iota((T, T), 1))
    return (t & 7) == (s & 7) if vertical else (t >> 3) == (s >> 3)


def pick_lanes(parts):
    lane = iota((T, T), 1) // 3
    out = parts[3]
    for k in range(3):
        out = jnp.where(lane == k, parts[k], out)
    return out


def as_f32(m):
    return jnp.where(m, 1.0, 0.0).astype(F32)


def ones(m):
    return as_f32(m).astype(BF)


def states_of(k):
    return 256 if k < 2 else 128


def line_and_entry(j, k):
    if k < 2:
        return (j >> 4, j & 15)
    return ((j >> 3) & 7, 2 * (j & 7) + (j >> 6))


def on_line(k):
    t, j = (iota((T, states_of(k)), 0), iota((T, states_of(k)), 1))
    return line_and_entry(j, k)[0] == (t >> 3 if k < 2 else t & 7)


def spread_states(bc, k):
    i, j = (iota((T, states_of(k)), 0), iota((T, states_of(k)), 1))
    wide = fine(bc, ones(i == 16 * k + line_and_entry(j, k)[1]))
    return jnp.where(on_line(k), wide, 0.0)


def gather_states(wide, k):
    j, i = (iota((states_of(k), T), 0), iota((states_of(k), T), 1))
    entry = line_and_entry(j, k)[1]
    return fine(jnp.where(on_line(k), wide, 0.0), ones(i == 16 * k + entry))


def by_head(values, k):
    lane = iota((T, DI), 1)
    a, b, c = (values[:, 3 * k + h : 3 * k + h + 1] for h in range(HEADS))
    return jnp.where(lane < 64, a, jnp.where(lane < 128, b, c))


def head_sum(wide, k):
    c, j = (iota((DI, T), 0), iota((DI, T), 1))
    return fine(wide, ones(j == 3 * k + c // 64))


def per_head(f):
    lane = iota((T, DI), 1)
    a, b, c = (f(h) for h in range(HEADS))
    return jnp.where(lane < 64, a, jnp.where(lane < 128, b, c))


def write_message(ref, wide_ref, states, totals):
    for d in range(2):
        s = states[d]
        for h in range(HEADS):
            wide_ref[:, d * 3 + h, :] = jnp.concatenate(
                [s[:64, 64 * h : 64 * h + 64], s[64:, 64 * h : 64 * h + 64]], axis=1
            )
    j, t = (iota((64, T), 0), iota((64, T), 1))
    i, o = (iota((T, T), 0), iota((T, T), 1))
    totals = fine(ones(t == (j >> 3)), fine(totals, ones(i == o + 6)))
    high = totals.astype(BF).astype(F32)
    wide_ref[:, 6, :] = high
    wide_ref[:, 7, :] = totals - high
    ref[...] = wide_ref[...].reshape(512, 128).astype(BF)


def open_message(ref, wide_ref):
    wide_ref[...] = ref[...].astype(F32).reshape(64, 8, 128)


def read_message(ref, d):
    x = [ref[:, d * 3 + h, :] for h in range(HEADS)]
    top = jnp.concatenate([v[:, :64] for v in x], axis=1)
    bottom = jnp.concatenate([v[:, 64:] for v in x], axis=1)
    return jnp.concatenate([top, bottom], axis=0)


def chain_kernel(backward, got_ref, out_ref):
    m = 512 // lax.axis_size("row")
    n = 512 // m
    got = got_ref[...].astype(F32).reshape(n, m // 8, 8, 128)
    shape = (m // 8, 8, 128)
    sub, lane = (iota(shape, 1), iota(shape, 2))
    ahead = sub < 3 if not backward else sub >= 3

    def factor(i):
        row = jnp.broadcast_to(got[i, :, 6:7, :] + got[i, :, 7:8, :], shape)
        return jnp.sum(jnp.where(lane == sub, row, 0.0), axis=2, keepdims=True)

    factors = [factor(i) for i in range(n)]
    up = [jnp.zeros(shape, F32)]
    for i in range(n - 1):
        up.append(factors[i] * up[i] + got[i])
    down = [jnp.zeros(shape, F32)]
    for i in range(n - 1, 0, -1):
        down.append(factors[i] * down[-1] + got[i])
    down = down[::-1]
    full = jnp.concatenate([jnp.where(ahead, u, v) for u, v in zip(up, down)], axis=0)
    out_ref[...] = full.reshape(512, 128).astype(BF)


def state_in(k, rows, columns):
    return rows[k][...] if k < 2 else read_message(columns, k - 2)


def sigmoid(x):
    return jax.nn.sigmoid(x)


def softplus(x):
    return jnp.maximum(x, 0.0) + jnp.log1p(jnp.exp(-jnp.abs(x)))


def fill_rim(pad_ref, above, own, below, left, right):
    pad_ref[0:1, 8:16, :] = above.reshape(1, C, -1)
    pad_ref[1 : R + 1, 8:16, :] = own.reshape(R, C, -1)
    pad_ref[R + 1 : R + 2, 8:16, :] = below.reshape(1, C, -1)
    for r in range(R + 2):
        pad_ref[r, 7:8, :] = left[r : r + 1]
        pad_ref[r, 16:17, :] = right[r : r + 1]


def edge_factor(me, blocks, j):
    return jnp.clip(j, 0, blocks - 1), jnp.where((j >= 0) & (j < blocks), 1.0, 0.0)


def fill_blocks(me, got_ref, pad_ref, f):
    for i in range(3):
        at, inside = edge_factor(me, got_ref.shape[0], me + i - 1)
        pad_ref[:, 8 * i : 8 * i + 8, :] = f(got_ref[at]).reshape(R + 2, C, -1) * inside


def as_branch(wbr_ref):
    return lambda x: dot(x, wbr_ref[...]).astype(BF).astype(F32)


def first_kernel(
    me_ref, got_ref, wbr_ref, cw_ref, cb_ref, wd_ref, wbc_ref, sb_ref, ld_ref,
    before_ref, act_ref, rawd_ref, bc_ref, step_ref, log_ref, tot_ref, mv_ref, pad_ref, wide_ref,
):
    fill_blocks(me_ref[0], got_ref, pad_ref, as_branch(wbr_ref))
    total = jnp.zeros((R, C, DI), F32)
    for b in range(3):
        shifted = pad_ref[:, 7 + b : 7 + b + C, :]
        for a in range(3):
            total = total + cw_ref[3 * a + b : 3 * a + b + 1, :] * shifted[a : a + R]
    before = total.reshape(T, DI) + cb_ref[...]
    act = (before * sigmoid(before)).astype(BF)
    before_ref[...] = before
    act_ref[...] = act
    raw_d = dot(act, wd_ref[...])
    bc = dot(act, wbc_ref[...])
    step = softplus(raw_d + sb_ref[...])
    log_step = step * -jnp.exp(ld_ref[...])
    log = pick_lanes([fine(ones(mask(k)), log_step) for k in range(4)])
    rows, cols = (fine(ones(same_line(v)), log_step) for v in (False, True))
    tot = pick_lanes([rows, rows, cols, cols])
    rawd_ref[...] = raw_d
    bc_ref[...] = bc
    step_ref[...] = step
    log_ref[...] = log
    tot_ref[...] = tot
    weight = jnp.exp(tot - log) * step
    wide = act.astype(F32)
    states = [
        fine(spread_states(bc, k), by_head(weight, k) * wide, 0, 0) for k in (2, 3)
    ]
    write_message(mv_ref, wide_ref, states, jnp.exp(tot))


def row_pair(me, blocks_ref, group):
    lines = []
    for r in range(2):
        at = pl.ds(16 * group, 16)
        for j in range(8):
            lines.append(blocks_ref[me ^ j, at, :].astype(F32)[8 * r : 8 * r + 8])
    return jnp.concatenate(lines, axis=0)


def row_scan_kernel(
    me_ref, got_ref, wbr_ref, cw_ref, cb_ref, wd_ref, wbc_ref, sb_ref, ld_ref,
    s0_ref, s1_ref, later_ref, gate_ref, pad_ref,
):
    nothing = jnp.zeros((R + 2, 8, DI), F32)
    pad_ref[:, 0:8, :] = nothing
    pad_ref[:, 72:80, :] = nothing
    for j in range(8):
        pad_ref[:, 8 + 8 * j : 16 + 8 * j, :] = as_branch(wbr_ref)(got_ref[j]).reshape(R + 2, C, DI)
    low = me_ref[0] * C
    high = low + C
    t, u = (iota((T, T), 0), iota((T, T), 1))
    same = (t >> 6) == (u >> 6)
    t, u = (t & 63, u & 63)
    reach = [
        same & (u > t) & (u < low),
        same & (u < t) & (u >= high),
        same & (u <= t) & (u >= high),
        same & (u >= t) & (u < low),
    ]
    reach = jnp.concatenate([ones(m) for m in reach], axis=0)
    before, after = (t < low, t >= high)
    first = iota((T, T), 1) < 3
    valid_in = jnp.where(first, as_f32(before), as_f32(after))
    valid_out = jnp.where(first, as_f32(after), as_f32(before))
    tj, j = (iota((T, 32), 0), iota((T, 32), 1))
    line = (tj >> 6) == (j >> 4)
    i, ji = (iota((T, 32), 0), iota((T, 32), 1))
    rate = -jnp.exp(ld_ref[...])
    for group in range(R // 2):
        total = jnp.zeros((2, 64, DI), F32)
        for b in range(3):
            shifted = pad_ref[2 * group : 2 * group + 4, 7 + b : 71 + b, :]
            for a in range(3):
                total = total + cw_ref[3 * a + b : 3 * a + b + 1, :] * shifted[a : a + 2]
        wide = total.reshape(T, DI) + cb_ref[...]
        act = (wide * sigmoid(wide)).astype(BF)
        wide = act.astype(F32)
        step = softplus(dot(act, wd_ref[...]) + sb_ref[...])
        bc = dot(act, wbc_ref[...])
        x = fine(reach, step * rate)
        w_in = jnp.exp(jnp.where(first, x[:T], x[T : 2 * T])) * step * valid_in
        later_ref[group * T : group * T + T, :] = (
            jnp.exp(jnp.where(first, x[2 * T : 3 * T], x[3 * T :])) * valid_out
        )
        gate_ref[group * T : group * T + T, :] = shifted_gate(bc)
        for k, ref in enumerate((s0_ref, s1_ref)):
            entry = ones(i == 16 * k + (ji & 15))
            spread = jnp.where(line, fine(bc, entry), 0.0)
            ref[32 * group : 32 * group + 32, :] = fine(spread, by_head(w_in, k) * wide, 0, 0)


def row_back_kernel(me_ref, blocks_ref, later_ref, gate_ref, l0_ref, l1_ref):
    tj, j = (iota((T, 32), 0), iota((T, 32), 1))
    line = (tj >> 6) == (j >> 4)
    for group in range(R // 2):
        part = slice(group * T, group * T + T)
        g = row_pair(me_ref[0], blocks_ref, group)
        later = later_ref[part, :]
        gate = gate_ref[part, :]
        for k, ref in enumerate((l0_ref, l1_ref)):
            entry = ones(tj == 16 * k + (j & 15))
            spread = jnp.where(line, fine(gate, entry), 0.0)
            ref[32 * group : 32 * group + 32, :] = fine(spread, by_head(later, k) * g, 0, 0)


def tables(k, bc, out_gate):
    lane = iota((T, T), 1) >> 4
    return fine(jnp.where(lane == k, out_gate, 0.0), bc, 1, 1)


def decay(k, h, log, log_t):
    i = 3 * k + h
    return jnp.exp(jnp.where(mask(k), log[:, i : i + 1] - log_t[i : i + 1, :], FAR))


def shifted_gate(bc):
    return pltpu.roll(bc, 64, 1)


def local_kernel(act_ref, bc_ref, step_ref, log_ref, y_ref):
    bc = bc_ref[...]
    out_gate = shifted_gate(bc)
    log = log_ref[...]
    log_t, step_t = (log.T, step_ref[...].T)
    weights = [jnp.zeros((T, T), F32)] * HEADS
    for k in range(4):
        scores = tables(k, bc, out_gate)
        for h in range(HEADS):
            i = 3 * k + h
            weights[h] = weights[h] + scores * (
                decay(k, h, log, log_t) * step_t[i : i + 1, :]
            )
    act = act_ref[...]
    y_ref[...] = per_head(lambda h: fine(weights[h], act))


def carry(k, out_gate, exp_log, state):
    return by_head(exp_log, k) * fine(spread_states(out_gate, k), state)


def norm_kernel(
    y_ref, act_ref, bc_ref, log_ref, tot_ref, sv_ref, s0_ref, s1_ref, skip_ref, tok_ref, wg_ref, gain_ref,
    nb_ref, ow_ref, cot_ref,
    out_ref, g_ref, dgate_ref, gated_ref, norms_ref, mv_ref, wide_ref,
):
    open_message(sv_ref, wide_ref)
    bc = bc_ref[...]
    out_gate = shifted_gate(bc)
    exp_log = jnp.exp(log_ref[...])
    summed = y_ref[...] + skip_ref[...] * act_ref[...].astype(F32)
    for k in range(4):
        state = state_in(k, (s0_ref, s1_ref), wide_ref)
        summed = summed + carry(k, out_gate, exp_log, state)
    gate = dot(tok_ref[...], wg_ref[...]).astype(BF).astype(F32)
    sig = sigmoid(gate)
    center = summed - jnp.mean(summed, axis=1, keepdims=True)
    inv = lax.rsqrt(jnp.mean(center * center, axis=1, keepdims=True) + 1e-5)
    unit = center * inv
    normed = unit * gain_ref[...] + nb_ref[...]
    gated = (normed * gate * sig).astype(BF)
    gated_ref[...] = gated
    out_ref[...] = dot(gated, ow_ref[...]).astype(BF)
    grad = dot(cot_ref[...], ow_ref[...], 1, 1)
    dnormed = grad * gate * sig
    dgate_ref[...] = (grad * normed * (sig * (1.0 + gate * (1.0 - sig)))).astype(BF)
    norms_ref[0:1, :] = jnp.sum(dnormed * unit, axis=0, keepdims=True)
    norms_ref[1:2, :] = jnp.sum(dnormed, axis=0, keepdims=True)
    dunit = dnormed * gain_ref[...]
    g = inv * (
        dunit
        - jnp.mean(dunit, axis=1, keepdims=True)
        - unit * jnp.mean(dunit * unit, axis=1, keepdims=True)
    )
    g = g.astype(BF)
    g_ref[...] = g
    g = g.astype(F32)
    states = [
        fine(spread_states(out_gate, k), by_head(exp_log, k) * g, 0, 0) for k in (2, 3)
    ]
    write_message(mv_ref, wide_ref, states, jnp.exp(tot_ref[...]))


def back_kernel(
    act_ref, bc_ref, step_ref, log_ref, g_ref, sv_ref, s0_ref, s1_ref,
    dact_ref, dbc_ref, dstep_ref, dlog_ref, wide_ref,
):
    open_message(sv_ref, wide_ref)
    bc = bc_ref[...]
    out_gate = shifted_gate(bc)
    log = log_ref[...]
    step = step_ref[...]
    log_t, step_t = (log.T, step.T)
    exp_log = jnp.exp(log)
    act = act_ref[...]
    g = g_ref[...]
    gw = g.astype(F32)
    lane = iota((T, DI), 1) // 64
    lane16 = iota((T, T), 1) >> 4
    lane1 = iota((T, T), 1)
    pair = [dot(jnp.where(lane == h, g, jnp.zeros_like(g)), act, 1, 1) for h in range(HEADS)]
    weights = [jnp.zeros((T, T), F32)] * HEADS
    d_in = jnp.zeros((T, T), F32)
    d_out = jnp.zeros((T, T), F32)
    row_sums = jnp.zeros((T, T), F32)
    step_rows = []
    for k in range(4):
        scores = tables(k, bc, out_gate)
        d_scores = jnp.zeros((T, T), F32)
        for h in range(HEADS):
            i = 3 * k + h
            dec = decay(k, h, log, log_t)
            dec_step = dec * step_t[i : i + 1, :]
            weights[h] = weights[h] + scores * dec_step
            d_scores = d_scores + pair[h] * dec_step
            d_step = pair[h] * dec * scores
            step_rows.append(jnp.sum(d_step, axis=0, keepdims=True))
            rows = jnp.sum(d_step * step_t[i : i + 1, :], axis=1, keepdims=True)
            row_sums = jnp.where(lane1 == i, rows, row_sums)
        d_out = d_out + fine(d_scores, jnp.where(lane16 == k, bc, 0.0))
        d_in = d_in + fine(d_scores, jnp.where(lane16 == k, out_gate, 0.0), 0, 0)
        state = state_in(k, (s0_ref, s1_ref), wide_ref)
        expg = by_head(exp_log, k) * gw
        carried = fine(spread_states(out_gate, k), state)
        row_sums = row_sums + head_sum(carried * expg, k)
        d_out = d_out + gather_states(fine(expg, state, 1, 1), k)
    d_step = jnp.concatenate(step_rows + [jnp.zeros((T - 12, T), F32)], axis=0).T
    dact_ref[...] = per_head(lambda h: fine(weights[h], g, 0, 0))
    dbc_ref[...] = d_in + pltpu.roll(d_out, 64, 1)
    dstep_ref[...] = d_step
    dlog_ref[...] = row_sums - step * d_step


def gate_grads_kernel(tok_ref, dgate_ref, gated_ref, cot_ref, gin_ref, gout_ref):
    gin_ref[...] = dot(tok_ref[...], dgate_ref[...], 0, 0)
    gout_ref[...] = dot(cot_ref[...], gated_ref[...], 0, 0)


def last_kernel(
    me_ref, got_ref, wbr_ref, cw_ref, before_ref, act_ref, rawd_ref, bc_ref, step_ref, log_ref, tot_ref, g_ref,
    sv_ref, s0_ref, s1_ref, lv_ref, l0_ref, l1_ref, dact_ref, dbc_ref, dstep_ref, dlog_ref, skip_ref, wd_ref, wbc_ref,
    sb_ref, ld_ref, gin_gate_ref, gout_ref, norms_ref,
    gb_ref, pack_ref, pad_ref, tok_ref, early_ref, late_ref,
):
    open_message(sv_ref, early_ref)
    open_message(lv_ref, late_ref)
    step, log, tot, bc = (step_ref[...], log_ref[...], tot_ref[...], bc_ref[...])
    act = act_ref[...]
    wide = act.astype(F32)
    g = g_ref[...].astype(F32)
    d_act = dact_ref[...] + skip_ref[...] * g
    d_bc = dbc_ref[...]
    to_end = jnp.exp(tot - log)
    weight = to_end * step
    through = jnp.exp(tot)
    inner = jnp.zeros((T, T), F32)
    cross = jnp.zeros((T, T), F32)
    for k in range(4):
        later = state_in(k, (l0_ref, l1_ref), late_ref)
        earlier = state_in(k, (s0_ref, s1_ref), early_ref)
        reach = fine(spread_states(bc, k), later)
        wk = by_head(weight, k)
        d_act = d_act + wk * reach
        inner = inner + head_sum(wide * reach, k)
        d_bc = d_bc + gather_states(fine(wk * wide, later, 1, 1), k)
        cross = cross + fine(ones(on_line(k)), head_sum(later * earlier, k))
    d_step = dstep_ref[...] + to_end * inner
    left = weight * inner
    d_log = dlog_ref[...]
    parts = []
    for k in range(4):
        after = mask(k ^ 1)
        rest = same_line(k >= 2) & jnp.logical_not(after)
        parts.append(fine(ones(after), d_log) + fine(ones(rest), left))
    d_log_step = pick_lanes(parts) + cross * through
    rate = -jnp.exp(ld_ref[...])
    d_rate = jnp.sum(d_log_step * step, axis=0, keepdims=True) * rate
    d_raw = (d_step + rate * d_log_step) * sigmoid(rawd_ref[...] + sb_ref[...])
    live = iota((T, T), 1) < 12
    d_raw = jnp.where(live, d_raw, 0.0)
    d_bias = jnp.sum(d_raw, axis=0, keepdims=True)
    d_raw = d_raw.astype(BF)
    d_bc = d_bc.astype(BF)
    d_act = d_act + dot(d_raw, wd_ref[...], 1, 1) + dot(d_bc, wbc_ref[...], 1, 1)
    before = before_ref[...]
    sig = sigmoid(before)
    gb = (d_act * sig * (1.0 + before * (1.0 - sig))).astype(BF)
    gb_ref[...] = gb
    gbw = gb.astype(F32)
    fill_blocks(me_ref[0], got_ref, pad_ref, as_branch(wbr_ref))
    fill_blocks(me_ref[0], got_ref, tok_ref, lambda x: x.astype(F32))
    gin = jnp.zeros((D, DI), F32)
    conv_rows = [None] * 9
    for b in range(3):
        near = pad_ref[:, 7 + b : 7 + b + C, :]
        near_tok = tok_ref[:, 7 + b : 7 + b + C, :]
        for a in range(3):
            i = 3 * a + b
            conv_rows[i] = jnp.sum(gbw * near[a : a + R].reshape(T, DI), axis=0, keepdims=True)
            gin = gin + cw_ref[i : i + 1, :] * dot(
                near_tok[a : a + R].reshape(T, D).astype(BF), gb, 0, 0
            )
    wide_row = lambda x: jnp.concatenate([x, jnp.zeros((1, DI - T), F32)], axis=1)
    small = jnp.concatenate(
        conv_rows
        + [
            jnp.sum(gbw, axis=0, keepdims=True),
            jnp.sum(g * wide, axis=0, keepdims=True),
            norms_ref[0:1, :],
            norms_ref[1:2, :],
            wide_row(d_bias),
            wide_row(jnp.where(live[:1], d_rate, 0.0)),
            jnp.zeros((1, DI), F32),
        ],
        axis=0,
    )
    both = [
        gin, gin_gate_ref[...], gout_ref[...], small, dot(d_bc, act, 0, 0),
        dot(d_raw, act, 0, 0)[:16],
    ]
    full = jnp.concatenate(both, axis=0)
    rest = small - small.astype(BF).astype(F32)
    pack_ref[0:448, :] = full[:, :128].astype(BF)
    pack_ref[448:672, :] = jnp.concatenate([full[:224, 128:], full[224:, 128:]], axis=1).astype(BF)
    pack_ref[672:688, :] = rest[:, :128].astype(BF)
    pack_ref[688:704, :] = jnp.concatenate(
        [rest[:, 128:], jnp.zeros((16, 64), F32)], axis=1
    ).astype(BF)
    pack_ref[704:1024, :] = jnp.zeros((320, T), BF)


def out_kernel(
    above_ref, own_ref, below_ref, left_ref, right_ref, cw_ref, dgate_ref, wbr_ref, wg_ref,
    out_ref, pad_ref,
):
    around = (above_ref, own_ref, below_ref, left_ref, right_ref)
    fill_rim(pad_ref, *(ref[...].astype(F32) for ref in around))
    total = jnp.zeros((R, C, DI), F32)
    for b in range(3):
        shifted = pad_ref[:, 9 - b : 9 - b + C, :]
        for a in range(3):
            total = total + cw_ref[3 * a + b : 3 * a + b + 1, :] * shifted[2 - a : 2 - a + R]
    d_branch = total.reshape(T, DI).astype(BF)
    out_ref[...] = (
        dot(d_branch, wbr_ref[...], 1, 1) + dot(dgate_ref[...], wg_ref[...], 1, 1)
    ).astype(BF)


def sum_kernel(scale, x_ref, out_ref):
    total = x_ref[0].astype(F32)
    for i in range(1, x_ref.shape[0]):
        total = total + x_ref[i].astype(F32)
    out_ref[...] = jnp.broadcast_to((total * scale).astype(out_ref.dtype), out_ref.shape)


def unpack_kernel(
    x_ref, gin_ref, conv_ref, cb_ref, scan_ref, sb_ref, ld_ref, skip_ref, gain_ref, nb_ref, gout_ref
):
    low, high = (x_ref[0:448, :].astype(F32), x_ref[448:672, :].astype(F32))
    full = jnp.concatenate(
        [low, jnp.concatenate([high[:, :64], high[:, 64:]], axis=0)], axis=1
    )
    rest = jnp.concatenate([x_ref[672:688, :], x_ref[688:704, :64]], axis=1).astype(F32)
    gin_ref[...] = jnp.concatenate([full[:96], full[96:192]], axis=1)
    gout_ref[...] = full[192:288].T
    small = full[288:304] + rest
    for a in range(3):
        conv_ref[a] = small[3 * a : 3 * a + 3]
    cb_ref[...] = small[9:10]
    skip_ref[...] = jnp.broadcast_to(small[10:11], (4, DI))
    gain_ref[...] = small[11:12]
    nb_ref[...] = small[12:13]
    for k in range(4):
        sb_ref[k : k + 1, :] = small[13:14, 3 * k : 3 * k + 3]
        ld_ref[k : k + 1, :] = small[14:15, 3 * k : 3 * k + 3]
    for k in range(4):
        scan_ref[0:3, k, :] = full[432 + 3 * k : 435 + 3 * k]
        scan_ref[3:19, k, :] = full[304 + 16 * k : 320 + 16 * k]
        scan_ref[19:35, k, :] = full[368 + 16 * k : 384 + 16 * k]


def call(kernel, outs, *args, flops=10**8, scratch=(), scalars=0):
    whole = pl.BlockSpec(memory_space=pltpu.VMEM)
    small = pl.BlockSpec(memory_space=pltpu.SMEM)
    return pl.pallas_call(
        kernel,
        out_shape=[jax.ShapeDtypeStruct(s, t) for s, t in outs],
        in_specs=[small] * scalars + [whole] * (len(args) - scalars),
        out_specs=[whole] * len(outs),
        scratch_shapes=list(scratch),
        compiler_params=pltpu.CompilerParams(vmem_limit_bytes=40 * 2**20),
        cost_estimate=pl.CostEstimate(flops=flops, bytes_accessed=10**6, transcendentals=0),
    )(*args)


def neighbours(last, first, axis):
    size = lax.axis_size(axis)
    up = [(i, i + 1) for i in range(size - 1)]
    down = [(j, i) for i, j in up]
    return lax.ppermute(last, axis, up), lax.ppermute(first, axis, down)


def with_rim(x):
    above, below = neighbours(x[T - C :], x[:C], "row")
    grid = x.reshape(R, C, -1)
    side = lambda c: jnp.concatenate([above[c : c + 1], grid[:, c], below[c : c + 1]], axis=0)
    left, right = neighbours(side(C - 1), side(0), "col")
    return above, x, below, left, right


def all_to_all(x, axis):
    return lax.all_to_all(x, axis, 0, 0, tiled=True)


def swapped(x, step):
    return lax.ppermute(x, "col", [(i, i ^ step) for i in range(lax.axis_size("col"))])


def in_pairs(x):
    return jnp.stack([x, swapped(x, 1)])


def along_col(pair):
    others = [swapped(pair, step) for step in range(2, lax.axis_size("col"), 2)]
    return jnp.concatenate([pair] + others, axis=0)


def exchange(message, axis, backward, meanwhile=()):
    chunks = (64, 8, 128)
    got, meanwhile = lax.optimization_barrier(
        (all_to_all(message.reshape(chunks), axis).reshape(512, 128), meanwhile)
    )
    (states,) = call(partial(chain_kernel, backward), [((512, 128), BF)], got, flops=10**7)
    return all_to_all(states.reshape(chunks), axis).reshape(512, 128), meanwhile


def reduced(pack, scale):
    rows, cols = (lax.axis_size("row"), lax.axis_size("col"))
    chunk = pack.shape[0] // rows
    got = all_to_all(pack.reshape(rows, chunk, 128), "row")
    (part,) = call(partial(sum_kernel, 1.0), [((cols, chunk, 128), F32)], got, flops=10**7)
    got = all_to_all(part, "col")
    (part,) = call(partial(sum_kernel, scale), [((rows, chunk, 128), BF)], got, flops=10**7)
    return all_to_all(part, "row").reshape(pack.shape)


def local(
    tokens, in_weight, conv_weight, conv_bias, scan_weight, step_bias, log_decay, skip_gain, norm_gain,
    norm_bias, out_weight, cotangent,
):
    own = tokens.reshape(T, D)
    above, below = neighbours(own[T - C :], own[:C], "row")
    band = jnp.concatenate([above, own, below], axis=0)
    got = all_to_all(jnp.broadcast_to(band, (lax.axis_size("col"),) + band.shape), "col")
    place = lax.axis_index("col").reshape(1)
    cot = cotangent.reshape(T, D)
    w_branch, w_gate = (in_weight[:, :DI], in_weight[:, DI:])
    taps = jnp.pad(conv_weight.reshape(9, DI), ((0, 7), (0, 0)))
    by_channel = jnp.moveaxis(scan_weight, 1, 0)
    w_step = jnp.pad(by_channel[:, :, :HEADS].reshape(DI, 12), ((0, 0), (0, 116)))
    w_bc = jnp.concatenate(
        [
            by_channel[:, :, HEADS : HEADS + NS].reshape(DI, 64),
            by_channel[:, :, HEADS + NS :].reshape(DI, 64),
        ],
        axis=1,
    )
    row = lambda x: x.reshape(1, -1)
    bias = jnp.pad(row(step_bias), ((0, 0), (0, 116)))
    rate = jnp.pad(row(log_decay), ((0, 0), (0, 116)))
    skip = row(jnp.sum(skip_gain, axis=0))
    square = ((T, T), F32)
    wide = ((T, DI), F32)
    low = ((T, DI), BF)
    message = ((512, 128), BF)
    opened = pltpu.VMEM((64, 8, 128), F32)
    states = ((256, DI), F32)
    long = ((8 * T, T), F32)

    before, act, raw_d, bc, step, log, tot, mv = call(
        first_kernel, [wide, low, square, square, square, square, square, message],
        place, got, w_branch, taps, row(conv_bias), w_step, w_bc, bias, rate,
        scratch=[pltpu.VMEM((R + 2, PITCH, DI), F32), opened], scalars=1,
    )
    sv, _ = exchange(mv, "row", False)
    s0, s1, later, gate_c = call(
        row_scan_kernel, [states, states, long, long],
        place, got, w_branch, taps, row(conv_bias), w_step, w_bc, bias, rate,
        scratch=[pltpu.VMEM((R + 2, 80, DI), F32)], scalars=1, flops=10**9,
    )
    (y,) = call(local_kernel, [wide], act, bc, step, log)
    out, g, d_gate, gated, norms, mv = call(
        norm_kernel, [((T, D), BF), low, low, low, ((8, DI), F32), message],
        y, act, bc, log, tot, sv, s0, s1, skip, own, w_gate, row(norm_gain), row(norm_bias), out_weight, cot,
        scratch=[opened],
    )
    lv, pair = exchange(mv, "row", True, in_pairs(g))
    lv, blocks = lax.optimization_barrier((lv, along_col(pair)))
    d_act, d_bc, d_step, d_log = call(
        back_kernel, [wide, square, square, square], act, bc, step, log, g, sv, s0, s1,
        scratch=[opened],
    )
    l0, l1 = call(
        row_back_kernel, [states, states], place, blocks, later, gate_c, scalars=1, flops=10**9
    )
    gin_gate, gout = call(
        gate_grads_kernel, [((D, DI), F32), ((D, DI), F32)], own, d_gate, gated, cot, flops=10**7
    )
    gb, pack = call(
        last_kernel, [low, ((1024, 128), BF)],
        place, got, w_branch, taps, before, act, raw_d, bc, step, log, tot, g, sv, s0, s1, lv, l0, l1, d_act, d_bc,
        d_step, d_log, skip, w_step, w_bc, bias, rate, gin_gate, gout, norms,
        scratch=[pltpu.VMEM((R + 2, PITCH, DI), F32), pltpu.VMEM((R + 2, PITCH, D), F32), opened, opened],
        scalars=1,
    )
    scale = float(T * lax.axis_size("row") * lax.axis_size("col")) ** (-0.5)
    total = reduced(pack, scale)
    rim = with_rim(gb)
    (d_tokens,) = call(
        out_kernel, [((T, D), BF)], *rim, taps, d_gate, w_branch, w_gate,
        scratch=[pltpu.VMEM((R + 2, PITCH, DI), F32)],
    )
    row_shape = ((1, DI), F32)
    gin, g_conv, g_cb, g_scan, g_bias, g_rate, g_skip, g_gain, g_shift, gout = call(
        unpack_kernel,
        [
            ((D, 2 * DI), F32), ((3, 3, DI), F32), row_shape, ((HEADS + 2 * NS, 4, DI), F32),
            ((4, HEADS), F32), ((4, HEADS), F32), ((4, DI), F32), row_shape, row_shape, ((DI, D), F32),
        ],
        total, flops=10**7,
    )
    return (
        out.reshape(R, C * D), d_tokens.reshape(R, C * D), gin, g_conv, g_cb.reshape(DI),
        jnp.transpose(g_scan, (1, 2, 0)), g_bias,
        g_rate, g_skip, g_gain.reshape(DI), g_shift.reshape(DI), gout,
    )


def solution(mesh):
    in_specs = (P("row", "col"), P(), P(), P(), P(), P(), P(), P(), P(), P(), P(), P("row", "col"))
    out_specs = (P("row", "col"), P("row", "col"), P(), P(), P(), P(), P(), P(), P(), P(), P(), P())
    return jax.shard_map(local, mesh=mesh, in_specs=in_specs, out_specs=out_specs, check_vma=False)
```

```python
from functools import partial

import jax
import jax.numpy as jnp
from jax import lax
from jax.experimental import pallas as pl
from jax.experimental.pallas import tpu as pltpu
from jax.sharding import PartitionSpec as P

D = 96
DI = 192
NS = 16
HEADS = 3
R = 16
C = 8
T = R * C
PITCH = 24
BIAS = slice(9, 10)
GAIN = slice(10, 11)
SHIFT = slice(11, 12)
SKIP = slice(12, 13)

F32 = jnp.float32
BF = jnp.bfloat16
FAR = -1e30


def dot(a, b, ca=1, cb=0):
    return lax.dot_general(a, b, (((ca,), (cb,)), ((), ())), preferred_element_type=F32)


def halves(x):
    if x.dtype == BF:
        return [x]
    high = x.astype(BF)
    return [high, (x - high.astype(F32)).astype(BF)]


def fine(a, b, ca=1, cb=0):
    a, b = (halves(a), halves(b))
    out = dot(a[0], b[0], ca, cb)
    for i, j in ((0, 1), (1, 0)):
        if i < len(a) and j < len(b):
            out = out + dot(a[i], b[j], ca, cb)
    return out


def iota(shape, dim):
    return lax.broadcasted_iota(jnp.int32, shape, dim)


def mask(k):
    t, s = (iota((T, T), 0), iota((T, T), 1))
    rt, ct, rs, cs = (t >> 3, t & 7, s >> 3, s & 7)
    if k == 0:
        return (rt == rs) & (cs <= ct)
    if k == 1:
        return (rt == rs) & (cs >= ct)
    if k == 2:
        return (ct == cs) & (rs <= rt)
    return (ct == cs) & (rs >= rt)


def same_line(vertical):
    t, s = (iota((T, T), 0), iota((T, T), 1))
    return (t & 7) == (s & 7) if vertical else (t >> 3) == (s >> 3)


def pick_lanes(parts):
    lane = iota((T, T), 1) // 3
    out = parts[3]
    for k in range(3):
        out = jnp.where(lane == k, parts[k], out)
    return out


def as_f32(m):
    return jnp.where(m, 1.0, 0.0).astype(F32)


def ones(m):
    return as_f32(m).astype(BF)


def states_of(k):
    return 256 if k < 2 else 128


def line_and_entry(j, k):
    if k < 2:
        return (j >> 4, j & 15)
    return ((j >> 3) & 7, 2 * (j & 7) + (j >> 6))


def on_line(k):
    t, j = (iota((T, states_of(k)), 0), iota((T, states_of(k)), 1))
    return line_and_entry(j, k)[0] == (t >> 3 if k < 2 else t & 7)


def spread_states(bc, k):
    i, j = (iota((T, states_of(k)), 0), iota((T, states_of(k)), 1))
    wide = fine(bc, ones(i == 16 * k + line_and_entry(j, k)[1]))
    return jnp.where(on_line(k), wide, 0.0)


def gather_states(wide, k):
    j, i = (iota((states_of(k), T), 0), iota((states_of(k), T), 1))
    entry = line_and_entry(j, k)[1]
    return fine(jnp.where(on_line(k), wide, 0.0), ones(i == 16 * k + entry))


def by_head(values, k):
    lane = iota((T, DI), 1)
    a, b, c = (values[:, 3 * k + h : 3 * k + h + 1] for h in range(HEADS))
    return jnp.where(lane < 64, a, jnp.where(lane < 128, b, c))


def head_sum(wide, k):
    c, j = (iota((DI, T), 0), iota((DI, T), 1))
    return fine(wide, ones(j == 3 * k + c // 64))


def per_head(f):
    lane = iota((T, DI), 1)
    a, b, c = (f(h) for h in range(HEADS))
    return jnp.where(lane < 64, a, jnp.where(lane < 128, b, c))


def write_message(ref, wide_ref, states, totals):
    for d in range(2):
        s = states[d]
        for h in range(HEADS):
            wide_ref[:, d * 3 + h, :] = jnp.concatenate(
                [s[:64, 64 * h : 64 * h + 64], s[64:, 64 * h : 64 * h + 64]], axis=1
            )
    j, t = (iota((64, T), 0), iota((64, T), 1))
    i, o = (iota((T, T), 0), iota((T, T), 1))
    totals = fine(ones(t == (j >> 3)), fine(totals, ones(i == o + 6)))
    high = totals.astype(BF).astype(F32)
    wide_ref[:, 6, :] = high
    wide_ref[:, 7, :] = totals - high
    ref[...] = wide_ref[...].reshape(512, 128).astype(BF)


def open_message(ref, wide_ref):
    wide_ref[...] = ref[...].astype(F32).reshape(64, 8, 128)


def read_message(ref, d):
    x = [ref[:, d * 3 + h, :] for h in range(HEADS)]
    top = jnp.concatenate([v[:, :64] for v in x], axis=1)
    bottom = jnp.concatenate([v[:, 64:] for v in x], axis=1)
    return jnp.concatenate([top, bottom], axis=0)


def chain_kernel(backward, got_ref, out_ref):
    m = 512 // lax.axis_size("row")
    n = 512 // m
    got = got_ref[...].astype(F32).reshape(n, m // 8, 8, 128)
    shape = (m // 8, 8, 128)
    sub, lane = (iota(shape, 1), iota(shape, 2))
    ahead = sub < 3 if not backward else sub >= 3

    def factor(i):
        row = jnp.broadcast_to(got[i, :, 6:7, :] + got[i, :, 7:8, :], shape)
        return jnp.sum(jnp.where(lane == sub, row, 0.0), axis=2, keepdims=True)

    factors = [factor(i) for i in range(n)]
    up = [jnp.zeros(shape, F32)]
    for i in range(n - 1):
        up.append(factors[i] * up[i] + got[i])
    down = [jnp.zeros(shape, F32)]
    for i in range(n - 1, 0, -1):
        down.append(factors[i] * down[-1] + got[i])
    down = down[::-1]
    full = jnp.concatenate([jnp.where(ahead, u, v) for u, v in zip(up, down)], axis=0)
    out_ref[...] = full.reshape(512, 128).astype(BF)


def state_in(k, rows, columns):
    return rows[k][...] if k < 2 else read_message(columns, k - 2)


def sigmoid(x):
    return jax.nn.sigmoid(x)


def softplus(x):
    return jnp.maximum(x, 0.0) + jnp.log1p(jnp.exp(-jnp.abs(x)))


def fill_rim(pad_ref, above, own, below, left, right):
    pad_ref[0:1, 8:16, :] = above.reshape(1, C, -1)
    pad_ref[1 : R + 1, 8:16, :] = own.reshape(R, C, -1)
    pad_ref[R + 1 : R + 2, 8:16, :] = below.reshape(1, C, -1)
    for r in range(R + 2):
        pad_ref[r, 7:8, :] = left[r : r + 1]
        pad_ref[r, 16:17, :] = right[r : r + 1]


def edge_factor(me, blocks, j):
    return jnp.clip(j, 0, blocks - 1), jnp.where((j >= 0) & (j < blocks), 1.0, 0.0)


def fill_blocks(me, got_ref, pad_ref, f):
    for i in range(3):
        at, inside = edge_factor(me, got_ref.shape[0], me + i - 1)
        pad_ref[:, 8 * i : 8 * i + 8, :] = f(got_ref[at]).reshape(R + 2, C, -1) * inside


def as_branch(wbr_ref):
    return lambda x: dot(x, wbr_ref[...]).astype(BF).astype(F32)


def first_kernel(
    me_ref, got_ref, wbr_ref, cw_ref, wd_ref, wbc_ref, sb_ref, ld_ref,
    before_ref, act_ref, rawd_ref, bc_ref, step_ref, log_ref, tot_ref, mv_ref, pad_ref, wide_ref,
):
    fill_blocks(me_ref[0], got_ref, pad_ref, as_branch(wbr_ref))
    total = jnp.zeros((R, C, DI), F32)
    for b in range(3):
        shifted = pad_ref[:, 7 + b : 7 + b + C, :]
        for a in range(3):
            total = total + cw_ref[3 * a + b : 3 * a + b + 1, :] * shifted[a : a + R]
    before = total.reshape(T, DI) + cw_ref[BIAS, :]
    act = (before * sigmoid(before)).astype(BF)
    before_ref[...] = before
    act_ref[...] = act
    raw_d = dot(act, wd_ref[...])
    bc = dot(act, wbc_ref[...])
    step = softplus(raw_d + sb_ref[...])
    log_step = step * -jnp.exp(ld_ref[...])
    log = pick_lanes([fine(ones(mask(k)), log_step) for k in range(4)])
    rows, cols = (fine(ones(same_line(v)), log_step) for v in (False, True))
    tot = pick_lanes([rows, rows, cols, cols])
    rawd_ref[...] = raw_d
    bc_ref[...] = bc
    step_ref[...] = step
    log_ref[...] = log
    tot_ref[...] = tot
    weight = jnp.exp(tot - log) * step
    wide = act.astype(F32)
    states = [
        fine(spread_states(bc, k), by_head(weight, k) * wide, 0, 0) for k in (2, 3)
    ]
    write_message(mv_ref, wide_ref, states, jnp.exp(tot))


def row_pair(me, blocks_ref, group):
    lines = []
    for r in range(2):
        at = pl.ds(16 * group, 16)
        for j in range(8):
            lines.append(blocks_ref[me ^ j, at, :].astype(F32)[8 * r : 8 * r + 8])
    return jnp.concatenate(lines, axis=0)


def row_scan_kernel(
    me_ref, got_ref, wbr_ref, cw_ref, wd_ref, wbc_ref, sb_ref, ld_ref,
    s0_ref, s1_ref, later_ref, pad_ref,
):
    nothing = jnp.zeros((R + 2, 8, DI), F32)
    pad_ref[:, 0:8, :] = nothing
    pad_ref[:, 72:80, :] = nothing
    for j in range(8):
        pad_ref[:, 8 + 8 * j : 16 + 8 * j, :] = as_branch(wbr_ref)(got_ref[j]).reshape(R + 2, C, DI)
    low = me_ref[0] * C
    high = low + C
    t, u = (iota((T, T), 0), iota((T, T), 1))
    same = (t >> 6) == (u >> 6)
    t, u = (t & 63, u & 63)
    reach = [
        same & (u > t) & (u < low),
        same & (u < t) & (u >= high),
        same & (u <= t) & (u >= high),
        same & (u >= t) & (u < low),
    ]
    reach = jnp.concatenate([ones(m) for m in reach], axis=0)
    before, after = (t < low, t >= high)
    first = iota((T, T), 1) < 3
    valid_in = jnp.where(first, as_f32(before), as_f32(after))
    valid_out = jnp.where(first, as_f32(after), as_f32(before))
    tj, j = (iota((T, 32), 0), iota((T, 32), 1))
    line = (tj >> 6) == (j >> 4)
    i, ji = (iota((T, 32), 0), iota((T, 32), 1))
    rate = -jnp.exp(ld_ref[...])
    for group in range(R // 2):
        total = jnp.zeros((2, 64, DI), F32)
        for b in range(3):
            shifted = pad_ref[2 * group : 2 * group + 4, 7 + b : 71 + b, :]
            for a in range(3):
                total = total + cw_ref[3 * a + b : 3 * a + b + 1, :] * shifted[a : a + 2]
        wide = total.reshape(T, DI) + cw_ref[BIAS, :]
        act = (wide * sigmoid(wide)).astype(BF)
        wide = act.astype(F32)
        step = softplus(dot(act, wd_ref[...]) + sb_ref[...])
        bc = dot(act, wbc_ref[...])
        x = fine(reach, step * rate)
        w_in = jnp.exp(jnp.where(first, x[:T], x[T : 2 * T])) * step * valid_in
        later = jnp.exp(jnp.where(first, x[2 * T : 3 * T], x[3 * T :])) * valid_out
        later_ref[group * T : group * T + T, :] = jnp.where(
            iota((T, T), 1) < 64, shifted_gate(bc), pltpu.roll(later, 64, 1)
        )
        for k, ref in enumerate((s0_ref, s1_ref)):
            entry = ones(i == 16 * k + (ji & 15))
            spread = jnp.where(line, fine(bc, entry), 0.0)
            ref[32 * group : 32 * group + 32, :] = fine(spread, by_head(w_in, k) * wide, 0, 0)


def row_back(me, blocks_ref, later_ref, out_refs):
    tj, j = (iota((T, 32), 0), iota((T, 32), 1))
    line = (tj >> 6) == (j >> 4)
    for group in range(R // 2):
        g = row_pair(me, blocks_ref, group)
        gate = later_ref[group * T : group * T + T, :]
        later = pltpu.roll(gate, 64, 1)
        for k, ref in enumerate(out_refs):
            entry = ones(tj == 16 * k + (j & 15))
            spread = jnp.where(line, fine(gate, entry), 0.0)
            ref[32 * group : 32 * group + 32, :] = fine(spread, by_head(later, k) * g, 0, 0)


def tables(k, bc, out_gate):
    lane = iota((T, T), 1) >> 4
    return fine(jnp.where(lane == k, out_gate, 0.0), bc, 1, 1)


def decay(k, h, log, log_t):
    i = 3 * k + h
    return jnp.exp(jnp.where(mask(k), log[:, i : i + 1] - log_t[i : i + 1, :], FAR))


def shifted_gate(bc):
    return pltpu.roll(bc, 64, 1)


def local_kernel(act_ref, bc_ref, step_ref, log_ref, y_ref):
    bc = bc_ref[...]
    out_gate = shifted_gate(bc)
    log = log_ref[...]
    log_t, step_t = (log.T, step_ref[...].T)
    weights = [jnp.zeros((T, T), F32)] * HEADS
    for k in range(4):
        scores = tables(k, bc, out_gate)
        for h in range(HEADS):
            i = 3 * k + h
            weights[h] = weights[h] + scores * (
                decay(k, h, log, log_t) * step_t[i : i + 1, :]
            )
    act = act_ref[...]
    y_ref[...] = per_head(lambda h: fine(weights[h], act))


def carry(k, out_gate, exp_log, state):
    return by_head(exp_log, k) * fine(spread_states(out_gate, k), state)


def norm_kernel(
    y_ref, act_ref, bc_ref, log_ref, tot_ref, sv_ref, s0_ref, s1_ref, vec_ref, tok_ref, wg_ref, ow_ref,
    cot_ref,
    out_ref, g_ref, dgate_ref, gated_ref, norms_ref, mv_ref, wide_ref,
):
    open_message(sv_ref, wide_ref)
    bc = bc_ref[...]
    out_gate = shifted_gate(bc)
    exp_log = jnp.exp(log_ref[...])
    gain = vec_ref[GAIN, :]
    summed = y_ref[...] + vec_ref[SKIP, :] * act_ref[...].astype(F32)
    for k in range(4):
        state = state_in(k, (s0_ref, s1_ref), wide_ref)
        summed = summed + carry(k, out_gate, exp_log, state)
    gate = dot(tok_ref[...], wg_ref[...]).astype(BF).astype(F32)
    sig = sigmoid(gate)
    center = summed - jnp.mean(summed, axis=1, keepdims=True)
    inv = lax.rsqrt(jnp.mean(center * center, axis=1, keepdims=True) + 1e-5)
    unit = center * inv
    normed = unit * gain + vec_ref[SHIFT, :]
    gated = (normed * gate * sig).astype(BF)
    gated_ref[...] = gated
    out_ref[...] = dot(gated, ow_ref[...]).astype(BF)
    grad = dot(cot_ref[...], ow_ref[...], 1, 1)
    dnormed = grad * gate * sig
    dgate_ref[...] = (grad * normed * (sig * (1.0 + gate * (1.0 - sig)))).astype(BF)
    norms_ref[0:1, :] = jnp.sum(dnormed * unit, axis=0, keepdims=True)
    norms_ref[1:2, :] = jnp.sum(dnormed, axis=0, keepdims=True)
    dunit = dnormed * gain
    g = inv * (
        dunit
        - jnp.mean(dunit, axis=1, keepdims=True)
        - unit * jnp.mean(dunit * unit, axis=1, keepdims=True)
    )
    g = g.astype(BF)
    g_ref[...] = g
    g = g.astype(F32)
    states = [
        fine(spread_states(out_gate, k), by_head(exp_log, k) * g, 0, 0) for k in (2, 3)
    ]
    write_message(mv_ref, wide_ref, states, jnp.exp(tot_ref[...]))


def back_kernel(
    act_ref, bc_ref, step_ref, log_ref, g_ref, sv_ref, s0_ref, s1_ref,
    back_ref, wide_ref,
):
    open_message(sv_ref, wide_ref)
    bc = bc_ref[...]
    out_gate = shifted_gate(bc)
    log = log_ref[...]
    step = step_ref[...]
    log_t, step_t = (log.T, step.T)
    exp_log = jnp.exp(log)
    act = act_ref[...]
    g = g_ref[...]
    gw = g.astype(F32)
    lane = iota((T, DI), 1) // 64
    lane16 = iota((T, T), 1) >> 4
    lane1 = iota((T, T), 1)
    pair = [dot(jnp.where(lane == h, g, jnp.zeros_like(g)), act, 1, 1) for h in range(HEADS)]
    weights = [jnp.zeros((T, T), F32)] * HEADS
    d_in = jnp.zeros((T, T), F32)
    d_out = jnp.zeros((T, T), F32)
    row_sums = jnp.zeros((T, T), F32)
    step_rows = []
    for k in range(4):
        scores = tables(k, bc, out_gate)
        d_scores = jnp.zeros((T, T), F32)
        for h in range(HEADS):
            i = 3 * k + h
            dec = decay(k, h, log, log_t)
            dec_step = dec * step_t[i : i + 1, :]
            weights[h] = weights[h] + scores * dec_step
            d_scores = d_scores + pair[h] * dec_step
            d_step = pair[h] * dec * scores
            step_rows.append(jnp.sum(d_step, axis=0, keepdims=True))
            rows = jnp.sum(d_step * step_t[i : i + 1, :], axis=1, keepdims=True)
            row_sums = jnp.where(lane1 == i, rows, row_sums)
        d_out = d_out + fine(d_scores, jnp.where(lane16 == k, bc, 0.0))
        d_in = d_in + fine(d_scores, jnp.where(lane16 == k, out_gate, 0.0), 0, 0)
        state = state_in(k, (s0_ref, s1_ref), wide_ref)
        expg = by_head(exp_log, k) * gw
        carried = fine(spread_states(out_gate, k), state)
        row_sums = row_sums + head_sum(carried * expg, k)
        d_out = d_out + gather_states(fine(expg, state, 1, 1), k)
    d_step = jnp.concatenate(step_rows + [jnp.zeros((T - 12, T), F32)], axis=0).T
    back_ref[:, 0:192] = per_head(lambda h: fine(weights[h], g, 0, 0))
    back_ref[:, 192:256] = jnp.zeros((T, 64), F32)
    back_ref[:, 256:384] = d_in + pltpu.roll(d_out, 64, 1)
    back_ref[:, 384:512] = jnp.where(lane1 < 64, d_step, pltpu.roll(row_sums - step * d_step, 64, 1))


def gate_grads_kernel(
    me_ref, got_ref, tok_ref, dgate_ref, gated_ref, cot_ref, side_ref, shifts_ref, near_ref
):
    fill_blocks(me_ref[0], got_ref, near_ref, lambda x: x.astype(F32))
    for b in range(3):
        near = near_ref[:, 7 + b : 7 + b + C, :]
        for a in range(3):
            i = 3 * a + b
            shifts_ref[D * i : D * i + D, :] = near[a : a + R].reshape(T, D).T.astype(BF)
    side_ref[:D, :] = dot(tok_ref[...], dgate_ref[...], 0, 0)
    side_ref[D:, :] = dot(cot_ref[...], gated_ref[...], 0, 0)


def last_kernel(
    me_ref, pad_ref, shifts_ref, vec_ref, before_ref, act_ref, rawd_ref, bc_ref, step_ref, log_ref, tot_ref, g_ref,
    sv_ref, s0_ref, s1_ref, lv_ref, blocks_ref, later_ref, back_ref, wd_ref,
    wbc_ref,
    sb_ref, ld_ref, side_ref, norms_ref,
    gb_ref, pack_ref, early_ref, late_ref, l0_ref, l1_ref,
):
    row_back(me_ref[0], blocks_ref, later_ref, (l0_ref, l1_ref))
    open_message(sv_ref, early_ref)
    open_message(lv_ref, late_ref)
    step, log, tot, bc = (step_ref[...], log_ref[...], tot_ref[...], bc_ref[...])
    act = act_ref[...]
    wide = act.astype(F32)
    g = g_ref[...].astype(F32)
    d_act = back_ref[:, 0:192] + vec_ref[SKIP, :] * g
    d_bc = back_ref[:, 256:384]
    d_mix = back_ref[:, 384:512]
    to_end = jnp.exp(tot - log)
    weight = to_end * step
    through = jnp.exp(tot)
    inner = jnp.zeros((T, T), F32)
    cross = jnp.zeros((T, T), F32)
    for k in range(4):
        later = state_in(k, (l0_ref, l1_ref), late_ref)
        earlier = state_in(k, (s0_ref, s1_ref), early_ref)
        reach = fine(spread_states(bc, k), later)
        wk = by_head(weight, k)
        d_act = d_act + wk * reach
        inner = inner + head_sum(wide * reach, k)
        d_bc = d_bc + gather_states(fine(wk * wide, later, 1, 1), k)
        cross = cross + fine(ones(on_line(k)), head_sum(later * earlier, k))
    d_step = d_mix + to_end * inner
    left = weight * inner
    d_log = pltpu.roll(d_mix, 64, 1)
    parts = []
    for k in range(4):
        after = mask(k ^ 1)
        rest = same_line(k >= 2) & jnp.logical_not(after)
        parts.append(fine(ones(after), d_log) + fine(ones(rest), left))
    d_log_step = pick_lanes(parts) + cross * through
    rate = -jnp.exp(ld_ref[...])
    d_rate = jnp.sum(d_log_step * step, axis=0, keepdims=True) * rate
    d_raw = (d_step + rate * d_log_step) * sigmoid(rawd_ref[...] + sb_ref[...])
    live = iota((T, T), 1) < 12
    d_raw = jnp.where(live, d_raw, 0.0)
    d_bias = jnp.sum(d_raw, axis=0, keepdims=True)
    d_raw = d_raw.astype(BF)
    d_bc = d_bc.astype(BF)
    d_act = d_act + dot(d_raw, wd_ref[...], 1, 1) + dot(d_bc, wbc_ref[...], 1, 1)
    before = before_ref[...]
    sig = sigmoid(before)
    gb = (d_act * sig * (1.0 + before * (1.0 - sig))).astype(BF)
    gb_ref[...] = gb
    gbw = gb.astype(F32)
    product = dot(shifts_ref[...], gb)
    gin = jnp.zeros((D, DI), F32)
    conv_rows = [None] * 9
    for b in range(3):
        near = pad_ref[:, 7 + b : 7 + b + C, :]
        for a in range(3):
            i = 3 * a + b
            conv_rows[i] = jnp.sum(gbw * near[a : a + R].reshape(T, DI), axis=0, keepdims=True)
            gin = gin + vec_ref[i : i + 1, :] * product[D * i : D * i + D]
    wide_row = lambda x: jnp.concatenate([x, jnp.zeros((1, DI - T), F32)], axis=1)
    small = jnp.concatenate(
        conv_rows
        + [
            jnp.sum(gbw, axis=0, keepdims=True),
            jnp.sum(g * wide, axis=0, keepdims=True),
            norms_ref[0:1, :],
            norms_ref[1:2, :],
            wide_row(d_bias),
            wide_row(jnp.where(live[:1], d_rate, 0.0)),
            jnp.zeros((1, DI), F32),
        ],
        axis=0,
    )
    both = [
        gin, side_ref[...], small, dot(d_bc, act, 0, 0),
        dot(d_raw, act, 0, 0)[:16],
    ]
    full = jnp.concatenate(both, axis=0)
    rest = small - small.astype(BF).astype(F32)
    pack_ref[0:448, :] = full[:, :128].astype(BF)
    pack_ref[448:672, :] = jnp.concatenate([full[:224, 128:], full[224:, 128:]], axis=1).astype(BF)
    pack_ref[672:688, :] = rest[:, :128].astype(BF)
    pack_ref[688:704, :] = jnp.concatenate(
        [rest[:, 128:], jnp.zeros((16, 64), F32)], axis=1
    ).astype(BF)
    pack_ref[704:1024, :] = jnp.zeros((320, T), BF)


def out_kernel(
    above_ref, own_ref, below_ref, left_ref, right_ref, cw_ref, dgate_ref, wbr_ref, wg_ref,
    out_ref, pad_ref,
):
    around = (above_ref, own_ref, below_ref, left_ref, right_ref)
    fill_rim(pad_ref, *(ref[...].astype(F32) for ref in around))
    total = jnp.zeros((R, C, DI), F32)
    for b in range(3):
        shifted = pad_ref[:, 9 - b : 9 - b + C, :]
        for a in range(3):
            total = total + cw_ref[3 * a + b : 3 * a + b + 1, :] * shifted[2 - a : 2 - a + R]
    d_branch = total.reshape(T, DI).astype(BF)
    out_ref[...] = (
        dot(d_branch, wbr_ref[...], 1, 1) + dot(dgate_ref[...], wg_ref[...], 1, 1)
    ).astype(BF)


def sum_kernel(scale, x_ref, out_ref):
    total = x_ref[0].astype(F32)
    for i in range(1, x_ref.shape[0]):
        total = total + x_ref[i].astype(F32)
    out_ref[...] = jnp.broadcast_to((total * scale).astype(out_ref.dtype), out_ref.shape)


def unpack_kernel(
    x_ref, gin_ref, conv_ref, cb_ref, scan_ref, sb_ref, ld_ref, skip_ref, gain_ref, nb_ref, gout_ref
):
    low, high = (x_ref[0:448, :].astype(F32), x_ref[448:672, :].astype(F32))
    full = jnp.concatenate(
        [low, jnp.concatenate([high[:, :64], high[:, 64:]], axis=0)], axis=1
    )
    rest = jnp.concatenate([x_ref[672:688, :], x_ref[688:704, :64]], axis=1).astype(F32)
    gin_ref[...] = jnp.concatenate([full[:96], full[96:192]], axis=1)
    gout_ref[...] = full[192:288].T
    small = full[288:304] + rest
    for a in range(3):
        conv_ref[a] = small[3 * a : 3 * a + 3]
    cb_ref[...] = small[9:10]
    skip_ref[...] = jnp.broadcast_to(small[10:11], (4, DI))
    gain_ref[...] = small[11:12]
    nb_ref[...] = small[12:13]
    for k in range(4):
        sb_ref[k : k + 1, :] = small[13:14, 3 * k : 3 * k + 3]
        ld_ref[k : k + 1, :] = small[14:15, 3 * k : 3 * k + 3]
    for k in range(4):
        scan_ref[0:3, k, :] = full[432 + 3 * k : 435 + 3 * k]
        scan_ref[3:19, k, :] = full[304 + 16 * k : 320 + 16 * k]
        scan_ref[19:35, k, :] = full[368 + 16 * k : 384 + 16 * k]


def call(kernel, outs, *args, flops=10**8, scratch=(), scalars=0):
    whole = pl.BlockSpec(memory_space=pltpu.VMEM)
    small = pl.BlockSpec(memory_space=pltpu.SMEM)
    return pl.pallas_call(
        kernel,
        out_shape=[jax.ShapeDtypeStruct(s, t) for s, t in outs],
        in_specs=[small] * scalars + [whole] * (len(args) - scalars),
        out_specs=[whole] * len(outs),
        scratch_shapes=list(scratch),
        compiler_params=pltpu.CompilerParams(vmem_limit_bytes=40 * 2**20),
        cost_estimate=pl.CostEstimate(flops=flops, bytes_accessed=10**6, transcendentals=0),
    )(*args)


def neighbours(last, first, axis):
    size = lax.axis_size(axis)
    up = [(i, i + 1) for i in range(size - 1)]
    down = [(j, i) for i, j in up]
    return lax.ppermute(last, axis, up), lax.ppermute(first, axis, down)


def with_rim(x):
    above, below = neighbours(x[T - C :], x[:C], "row")
    grid = x.reshape(R, C, -1)
    side = lambda c: jnp.concatenate([above[c : c + 1], grid[:, c], below[c : c + 1]], axis=0)
    left, right = neighbours(side(C - 1), side(0), "col")
    return above, x, below, left, right


def all_to_all(x, axis):
    return lax.all_to_all(x, axis, 0, 0, tiled=True)


def swapped(x, step):
    return lax.ppermute(x, "col", [(i, i ^ step) for i in range(lax.axis_size("col"))])


def in_pairs(x):
    return jnp.stack([x, swapped(x, 1)])


def along_col(pair):
    others = [swapped(pair, step) for step in range(2, lax.axis_size("col"), 2)]
    return jnp.concatenate([pair] + others, axis=0)


def exchange(message, axis, backward, meanwhile=()):
    chunks = (64, 8, 128)
    got, meanwhile = lax.optimization_barrier(
        (all_to_all(message.reshape(chunks), axis).reshape(512, 128), meanwhile)
    )
    (states,) = call(partial(chain_kernel, backward), [((512, 128), BF)], got, flops=10**7)
    return all_to_all(states.reshape(chunks), axis).reshape(512, 128), meanwhile


def reduced(pack, scale):
    rows, cols = (lax.axis_size("row"), lax.axis_size("col"))
    chunk = pack.shape[0] // rows
    got = all_to_all(pack.reshape(rows, chunk, 128), "row")
    (part,) = call(partial(sum_kernel, 1.0), [((cols, chunk, 128), F32)], got, flops=10**7)
    got = all_to_all(part, "col")
    (part,) = call(partial(sum_kernel, scale), [((rows, chunk, 128), BF)], got, flops=10**7)
    return all_to_all(part, "row").reshape(pack.shape)


def local(
    tokens, in_weight, conv_weight, conv_bias, scan_weight, step_bias, log_decay, skip_gain, norm_gain,
    norm_bias, out_weight, cotangent,
):
    own = tokens.reshape(T, D)
    above, below = neighbours(own[T - C :], own[:C], "row")
    band = jnp.concatenate([above, own, below], axis=0)
    got = all_to_all(jnp.broadcast_to(band, (lax.axis_size("col"),) + band.shape), "col")
    place = lax.axis_index("col").reshape(1)
    cot = cotangent.reshape(T, D)
    w_branch, w_gate = (in_weight[:, :DI], in_weight[:, DI:])
    by_channel = jnp.moveaxis(scan_weight, 1, 0)
    w_step = jnp.pad(by_channel[:, :, :HEADS].reshape(DI, 12), ((0, 0), (0, 116)))
    w_bc = jnp.concatenate(
        [
            by_channel[:, :, HEADS : HEADS + NS].reshape(DI, 64),
            by_channel[:, :, HEADS + NS :].reshape(DI, 64),
        ],
        axis=1,
    )
    row = lambda x: x.reshape(1, -1)
    bias = jnp.pad(row(step_bias), ((0, 0), (0, 116)))
    rate = jnp.pad(row(log_decay), ((0, 0), (0, 116)))
    vec = jnp.concatenate(
        [
            conv_weight.reshape(9, DI), row(conv_bias), row(norm_gain), row(norm_bias),
            jnp.sum(skip_gain, axis=0, keepdims=True), jnp.zeros((3, DI), F32),
        ],
        axis=0,
    )
    square = ((T, T), F32)
    wide = ((T, DI), F32)
    low = ((T, DI), BF)
    message = ((512, 128), BF)
    opened = pltpu.VMEM((64, 8, 128), F32)
    states = ((256, DI), F32)
    long = ((8 * T, T), F32)

    before, act, raw_d, bc, step, log, tot, mv, padded = call(
        first_kernel,
        [wide, low, square, square, square, square, square, message, ((R + 2, PITCH, DI), F32)],
        place, got, w_branch, vec, w_step, w_bc, bias, rate, scratch=[opened], scalars=1,
    )
    sv, _ = exchange(mv, "row", False)
    s0, s1, later = call(
        row_scan_kernel, [states, states, long],
        place, got, w_branch, vec, w_step, w_bc, bias, rate,
        scratch=[pltpu.VMEM((R + 2, 80, DI), F32)], scalars=1, flops=10**9,
    )
    (y,) = call(local_kernel, [wide], act, bc, step, log)
    out, g, d_gate, gated, norms, mv = call(
        norm_kernel, [((T, D), BF), low, low, low, ((8, DI), F32), message],
        y, act, bc, log, tot, sv, s0, s1, vec, own, w_gate, out_weight, cot,
        scratch=[opened],
    )
    back = call(
        back_kernel, [((T, 512), F32)], act, bc, step, log, g, sv, s0, s1, scratch=[opened]
    )
    sides = call(
        gate_grads_kernel, [((2 * D, DI), F32), ((9 * D, T), BF)],
        place, got, own, d_gate, gated, cot,
        scratch=[pltpu.VMEM((R + 2, PITCH, D), F32)], scalars=1, flops=10**7,
    )
    lv, (pair, back, sides) = exchange(mv, "row", True, (in_pairs(g), back, sides))
    side, shifts = sides
    lv, blocks = lax.optimization_barrier((lv, along_col(pair)))
    gb, pack = call(
        last_kernel, [low, ((1024, 128), BF)],
        place, padded, shifts, vec, before, act, raw_d, bc, step, log, tot, g, sv, s0, s1, lv, blocks, later,
        *back, w_step, w_bc, bias, rate, side, norms,
        scratch=[opened, opened, pltpu.VMEM((256, DI), F32), pltpu.VMEM((256, DI), F32)],
        scalars=1,
    )
    scale = float(T * lax.axis_size("row") * lax.axis_size("col")) ** (-0.5)
    total = reduced(pack, scale)
    rim = with_rim(gb)
    (d_tokens,) = call(
        out_kernel, [((T, D), BF)], *rim, vec, d_gate, w_branch, w_gate,
        scratch=[pltpu.VMEM((R + 2, PITCH, DI), F32)],
    )
    row_shape = ((1, DI), F32)
    gin, g_conv, g_cb, g_scan, g_bias, g_rate, g_skip, g_gain, g_shift, gout = call(
        unpack_kernel,
        [
            ((D, 2 * DI), F32), ((3, 3, DI), F32), row_shape, ((HEADS + 2 * NS, 4, DI), F32),
            ((4, HEADS), F32), ((4, HEADS), F32), ((4, DI), F32), row_shape, row_shape, ((DI, D), F32),
        ],
        total, flops=10**7,
    )
    return (
        out.reshape(R, C * D), d_tokens.reshape(R, C * D), gin, g_conv, g_cb.reshape(DI),
        jnp.transpose(g_scan, (1, 2, 0)), g_bias,
        g_rate, g_skip, g_gain.reshape(DI), g_shift.reshape(DI), gout,
    )


def solution(mesh):
    in_specs = (P("row", "col"), P(), P(), P(), P(), P(), P(), P(), P(), P(), P(), P("row", "col"))
    out_specs = (P("row", "col"), P("row", "col"), P(), P(), P(), P(), P(), P(), P(), P(), P(), P())
    return jax.shard_map(local, mesh=mesh, in_specs=in_specs, out_specs=out_specs, check_vma=False)
```

```python
from functools import partial

import jax
import jax.numpy as jnp
from jax import lax
from jax.experimental import pallas as pl
from jax.experimental.pallas import tpu as pltpu
from jax.sharding import PartitionSpec as P

D = 96
DI = 192
NS = 16
HEADS = 3
R = 16
C = 8
T = R * C
PITCH = 24
BIAS = slice(9, 10)
GAIN = slice(10, 11)
SHIFT = slice(11, 12)
SKIP = slice(12, 13)
STEP_BIAS = slice(13, 14)
RATE = slice(14, 15)

F32 = jnp.float32
BF = jnp.bfloat16
FAR = -1e30


def dot(a, b, ca=1, cb=0):
    return lax.dot_general(a, b, (((ca,), (cb,)), ((), ())), preferred_element_type=F32)


def halves(x):
    if x.dtype == BF:
        return [x]
    high = x.astype(BF)
    return [high, (x - high.astype(F32)).astype(BF)]


def fine(a, b, ca=1, cb=0):
    a, b = (halves(a), halves(b))
    out = dot(a[0], b[0], ca, cb)
    for i, j in ((0, 1), (1, 0)):
        if i < len(a) and j < len(b):
            out = out + dot(a[i], b[j], ca, cb)
    return out


def iota(shape, dim):
    return lax.broadcasted_iota(jnp.int32, shape, dim)


def mask(k):
    t, s = (iota((T, T), 0), iota((T, T), 1))
    rt, ct, rs, cs = (t >> 3, t & 7, s >> 3, s & 7)
    if k == 0:
        return (rt == rs) & (cs <= ct)
    if k == 1:
        return (rt == rs) & (cs >= ct)
    if k == 2:
        return (ct == cs) & (rs <= rt)
    return (ct == cs) & (rs >= rt)


def same_line(vertical):
    t, s = (iota((T, T), 0), iota((T, T), 1))
    return (t & 7) == (s & 7) if vertical else (t >> 3) == (s >> 3)


def pick_lanes(parts):
    lane = iota((T, T), 1) // 3
    out = parts[3]
    for k in range(3):
        out = jnp.where(lane == k, parts[k], out)
    return out


def as_f32(m):
    return jnp.where(m, 1.0, 0.0).astype(F32)


def ones(m):
    return as_f32(m).astype(BF)


def states_of(k):
    return 256 if k < 2 else 128


def line_and_entry(j, k):
    if k < 2:
        return (j >> 4, j & 15)
    return ((j >> 3) & 7, 2 * (j & 7) + (j >> 6))


def on_line(k):
    t, j = (iota((T, states_of(k)), 0), iota((T, states_of(k)), 1))
    return line_and_entry(j, k)[0] == (t >> 3 if k < 2 else t & 7)


def spread_states(bc, k):
    i, j = (iota((T, states_of(k)), 0), iota((T, states_of(k)), 1))
    wide = fine(bc, ones(i == 16 * k + line_and_entry(j, k)[1]))
    return jnp.where(on_line(k), wide, 0.0)


def gather_states(wide, k):
    j, i = (iota((states_of(k), T), 0), iota((states_of(k), T), 1))
    entry = line_and_entry(j, k)[1]
    return fine(jnp.where(on_line(k), wide, 0.0), ones(i == 16 * k + entry))


def by_head(values, k):
    lane = iota((T, DI), 1)
    a, b, c = (values[:, 3 * k + h : 3 * k + h + 1] for h in range(HEADS))
    return jnp.where(lane < 64, a, jnp.where(lane < 128, b, c))


def head_sum(wide, k):
    c, j = (iota((DI, T), 0), iota((DI, T), 1))
    return fine(wide, ones(j == 3 * k + c // 64))


def per_head(f):
    lane = iota((T, DI), 1)
    a, b, c = (f(h) for h in range(HEADS))
    return jnp.where(lane < 64, a, jnp.where(lane < 128, b, c))


def write_message(ref, wide_ref, states, totals):
    for d in range(2):
        s = states[d]
        for h in range(HEADS):
            wide_ref[:, d * 3 + h, :] = jnp.concatenate(
                [s[:64, 64 * h : 64 * h + 64], s[64:, 64 * h : 64 * h + 64]], axis=1
            )
    j, t = (iota((64, T), 0), iota((64, T), 1))
    i, o = (iota((T, T), 0), iota((T, T), 1))
    totals = fine(ones(t == (j >> 3)), fine(totals, ones(i == o + 6)))
    high = totals.astype(BF).astype(F32)
    wide_ref[:, 6, :] = high
    wide_ref[:, 7, :] = totals - high
    ref[...] = wide_ref[...].reshape(512, 128).astype(BF)


def open_message(ref, wide_ref):
    wide_ref[...] = ref[...].astype(F32).reshape(64, 8, 128)


def read_message(ref, d):
    x = [ref[:, d * 3 + h, :] for h in range(HEADS)]
    top = jnp.concatenate([v[:, :64] for v in x], axis=1)
    bottom = jnp.concatenate([v[:, 64:] for v in x], axis=1)
    return jnp.concatenate([top, bottom], axis=0)


def chain_kernel(backward, got_ref, out_ref):
    m = 512 // lax.axis_size("row")
    n = 512 // m
    got = got_ref[...].astype(F32).reshape(n, m // 8, 8, 128)
    shape = (m // 8, 8, 128)
    sub, lane = (iota(shape, 1), iota(shape, 2))
    ahead = sub < 3 if not backward else sub >= 3

    def factor(i):
        row = jnp.broadcast_to(got[i, :, 6:7, :] + got[i, :, 7:8, :], shape)
        return jnp.sum(jnp.where(lane == sub, row, 0.0), axis=2, keepdims=True)

    factors = [factor(i) for i in range(n)]
    up = [jnp.zeros(shape, F32)]
    for i in range(n - 1):
        up.append(factors[i] * up[i] + got[i])
    down = [jnp.zeros(shape, F32)]
    for i in range(n - 1, 0, -1):
        down.append(factors[i] * down[-1] + got[i])
    down = down[::-1]
    full = jnp.concatenate([jnp.where(ahead, u, v) for u, v in zip(up, down)], axis=0)
    out_ref[...] = full.reshape(512, 128).astype(BF)


def state_in(k, rows, columns):
    return rows[k][...] if k < 2 else read_message(columns, k - 2)


def sigmoid(x):
    return jax.nn.sigmoid(x)


def softplus(x):
    return jnp.maximum(x, 0.0) + jnp.log1p(jnp.exp(-jnp.abs(x)))


def fill_rim(pad_ref, above, own, below, left, right):
    pad_ref[0:1, 8:16, :] = above.reshape(1, C, -1)
    pad_ref[1 : R + 1, 8:16, :] = own.reshape(R, C, -1)
    pad_ref[R + 1 : R + 2, 8:16, :] = below.reshape(1, C, -1)
    for r in range(R + 2):
        pad_ref[r, 7:8, :] = left[r : r + 1]
        pad_ref[r, 16:17, :] = right[r : r + 1]


def edge_factor(me, blocks, j):
    return jnp.clip(j, 0, blocks - 1), jnp.where((j >= 0) & (j < blocks), 1.0, 0.0)


def fill_blocks(me, got_ref, pad_ref, f):
    for i in range(3):
        at, inside = edge_factor(me, got_ref.shape[0], me + i - 1)
        pad_ref[:, 8 * i : 8 * i + 8, :] = f(got_ref[at]).reshape(R + 2, C, -1) * inside


def as_branch(wbr_ref):
    return lambda x: dot(x, wbr_ref[...]).astype(BF).astype(F32)


def first_kernel(
    me_ref, got_ref, wbr_ref, cw_ref, wd_ref, wbc_ref,
    act_ref, bc_ref, step_ref, log_ref, tot_ref, mv_ref, pad_ref, wide_ref,
):
    fill_blocks(me_ref[0], got_ref, pad_ref, as_branch(wbr_ref))
    total = jnp.zeros((R, C, DI), F32)
    for b in range(3):
        shifted = pad_ref[:, 7 + b : 7 + b + C, :]
        for a in range(3):
            total = total + cw_ref[3 * a + b : 3 * a + b + 1, :] * shifted[a : a + R]
    before = total.reshape(T, DI) + cw_ref[BIAS, :]
    act = (before * sigmoid(before)).astype(BF)
    act_ref[...] = act
    raw_d = dot(act, wd_ref[...])
    bc = dot(act, wbc_ref[...])
    step = softplus(raw_d + cw_ref[STEP_BIAS, :T])
    log_step = step * -jnp.exp(cw_ref[RATE, :T])
    log = pick_lanes([fine(ones(mask(k)), log_step) for k in range(4)])
    rows, cols = (fine(ones(same_line(v)), log_step) for v in (False, True))
    tot = pick_lanes([rows, rows, cols, cols])
    bc_ref[...] = bc
    step_ref[...] = step
    log_ref[...] = log
    tot_ref[...] = tot
    weight = jnp.exp(tot - log) * step
    wide = act.astype(F32)
    states = [
        fine(spread_states(bc, k), by_head(weight, k) * wide, 0, 0) for k in (2, 3)
    ]
    write_message(mv_ref, wide_ref, states, jnp.exp(tot))


def row_pair(me, blocks_ref, group):
    lines = []
    for r in range(2):
        at = pl.ds(16 * group, 16)
        for j in range(8):
            lines.append(blocks_ref[me ^ j, at, :].astype(F32)[8 * r : 8 * r + 8])
    return jnp.concatenate(lines, axis=0)


def row_scan_kernel(
    me_ref, got_ref, wbr_ref, cw_ref, wd_ref, wbc_ref,
    s0_ref, s1_ref, later_ref, pad_ref,
):
    nothing = jnp.zeros((R + 2, 8, DI), F32)
    pad_ref[:, 0:8, :] = nothing
    pad_ref[:, 72:80, :] = nothing
    for j in range(8):
        pad_ref[:, 8 + 8 * j : 16 + 8 * j, :] = as_branch(wbr_ref)(got_ref[j]).reshape(R + 2, C, DI)
    low = me_ref[0] * C
    high = low + C
    t, u = (iota((T, T), 0), iota((T, T), 1))
    same = (t >> 6) == (u >> 6)
    t, u = (t & 63, u & 63)
    reach = [
        same & (u > t) & (u < low),
        same & (u < t) & (u >= high),
        same & (u <= t) & (u >= high),
        same & (u >= t) & (u < low),
    ]
    reach = jnp.concatenate([ones(m) for m in reach], axis=0)
    before, after = (t < low, t >= high)
    first = iota((T, T), 1) < 3
    valid_in = jnp.where(first, as_f32(before), as_f32(after))
    valid_out = jnp.where(first, as_f32(after), as_f32(before))
    tj, j = (iota((T, 32), 0), iota((T, 32), 1))
    line = (tj >> 6) == (j >> 4)
    i, ji = (iota((T, 32), 0), iota((T, 32), 1))
    rate = -jnp.exp(cw_ref[RATE, :T])
    for group in range(R // 2):
        total = jnp.zeros((2, 64, DI), F32)
        for b in range(3):
            shifted = pad_ref[2 * group : 2 * group + 4, 7 + b : 71 + b, :]
            for a in range(3):
                total = total + cw_ref[3 * a + b : 3 * a + b + 1, :] * shifted[a : a + 2]
        wide = total.reshape(T, DI) + cw_ref[BIAS, :]
        act = (wide * sigmoid(wide)).astype(BF)
        wide = act.astype(F32)
        step = softplus(dot(act, wd_ref[...]) + cw_ref[STEP_BIAS, :T])
        bc = dot(act, wbc_ref[...])
        x = fine(reach, step * rate)
        w_in = jnp.exp(jnp.where(first, x[:T], x[T : 2 * T])) * step * valid_in
        later = jnp.exp(jnp.where(first, x[2 * T : 3 * T], x[3 * T :])) * valid_out
        later_ref[group * T : group * T + T, :] = jnp.where(
            iota((T, T), 1) < 64, shifted_gate(bc), pltpu.roll(later, 64, 1)
        )
        for k, ref in enumerate((s0_ref, s1_ref)):
            entry = ones(i == 16 * k + (ji & 15))
            spread = jnp.where(line, fine(bc, entry), 0.0)
            ref[32 * group : 32 * group + 32, :] = fine(spread, by_head(w_in, k) * wide, 0, 0)


def row_back(me, blocks_ref, later_ref, out_refs):
    tj, j = (iota((T, 32), 0), iota((T, 32), 1))
    line = (tj >> 6) == (j >> 4)
    for group in range(R // 2):
        g = row_pair(me, blocks_ref, group)
        gate = later_ref[group * T : group * T + T, :]
        later = pltpu.roll(gate, 64, 1)
        for k, ref in enumerate(out_refs):
            entry = ones(tj == 16 * k + (j & 15))
            spread = jnp.where(line, fine(gate, entry), 0.0)
            ref[32 * group : 32 * group + 32, :] = fine(spread, by_head(later, k) * g, 0, 0)


def tables(k, bc, out_gate):
    lane = iota((T, T), 1) >> 4
    return fine(jnp.where(lane == k, out_gate, 0.0), bc, 1, 1)


def decay(k, h, log, log_t):
    i = 3 * k + h
    return jnp.exp(jnp.where(mask(k), log[:, i : i + 1] - log_t[i : i + 1, :], FAR))


def shifted_gate(bc):
    return pltpu.roll(bc, 64, 1)


def local_kernel(act_ref, bc_ref, step_ref, log_ref, y_ref):
    bc = bc_ref[...]
    out_gate = shifted_gate(bc)
    log = log_ref[...]
    log_t, step_t = (log.T, step_ref[...].T)
    weights = [jnp.zeros((T, T), F32)] * HEADS
    for k in range(4):
        scores = tables(k, bc, out_gate)
        for h in range(HEADS):
            i = 3 * k + h
            weights[h] = weights[h] + scores * (
                decay(k, h, log, log_t) * step_t[i : i + 1, :]
            )
    act = act_ref[...]
    y_ref[...] = per_head(lambda h: fine(weights[h], act))


def carry(k, out_gate, exp_log, state):
    return by_head(exp_log, k) * fine(spread_states(out_gate, k), state)


def norm_kernel(
    y_ref, act_ref, bc_ref, log_ref, tot_ref, sv_ref, s0_ref, s1_ref, vec_ref, tok_ref, wg_ref, ow_ref,
    cot_ref,
    out_ref, g_ref, dgate_ref, gated_ref, norms_ref, mv_ref, wide_ref,
):
    open_message(sv_ref, wide_ref)
    bc = bc_ref[...]
    out_gate = shifted_gate(bc)
    exp_log = jnp.exp(log_ref[...])
    gain = vec_ref[GAIN, :]
    summed = y_ref[...] + vec_ref[SKIP, :] * act_ref[...].astype(F32)
    for k in range(4):
        state = state_in(k, (s0_ref, s1_ref), wide_ref)
        summed = summed + carry(k, out_gate, exp_log, state)
    gate = dot(tok_ref[...], wg_ref[...]).astype(BF).astype(F32)
    sig = sigmoid(gate)
    center = summed - jnp.mean(summed, axis=1, keepdims=True)
    inv = lax.rsqrt(jnp.mean(center * center, axis=1, keepdims=True) + 1e-5)
    unit = center * inv
    normed = unit * gain + vec_ref[SHIFT, :]
    gated = (normed * gate * sig).astype(BF)
    gated_ref[...] = gated
    out_ref[...] = dot(gated, ow_ref[...]).astype(BF)
    grad = dot(cot_ref[...], ow_ref[...], 1, 1)
    dnormed = grad * gate * sig
    dgate_ref[...] = (grad * normed * (sig * (1.0 + gate * (1.0 - sig)))).astype(BF)
    norms_ref[0:1, :] = jnp.sum(dnormed * unit, axis=0, keepdims=True)
    norms_ref[1:2, :] = jnp.sum(dnormed, axis=0, keepdims=True)
    dunit = dnormed * gain
    g = inv * (
        dunit
        - jnp.mean(dunit, axis=1, keepdims=True)
        - unit * jnp.mean(dunit * unit, axis=1, keepdims=True)
    )
    g = g.astype(BF)
    g_ref[...] = g
    g = g.astype(F32)
    states = [
        fine(spread_states(out_gate, k), by_head(exp_log, k) * g, 0, 0) for k in (2, 3)
    ]
    write_message(mv_ref, wide_ref, states, jnp.exp(tot_ref[...]))


def back_kernel(
    act_ref, bc_ref, step_ref, log_ref, g_ref, sv_ref, s0_ref, s1_ref,
    back_ref, wide_ref,
):
    open_message(sv_ref, wide_ref)
    bc = bc_ref[...]
    out_gate = shifted_gate(bc)
    log = log_ref[...]
    step = step_ref[...]
    log_t, step_t = (log.T, step.T)
    exp_log = jnp.exp(log)
    act = act_ref[...]
    g = g_ref[...]
    gw = g.astype(F32)
    lane = iota((T, DI), 1) // 64
    lane16 = iota((T, T), 1) >> 4
    lane1 = iota((T, T), 1)
    pair = [dot(jnp.where(lane == h, g, jnp.zeros_like(g)), act, 1, 1) for h in range(HEADS)]
    weights = [jnp.zeros((T, T), F32)] * HEADS
    d_in = jnp.zeros((T, T), F32)
    d_out = jnp.zeros((T, T), F32)
    row_sums = jnp.zeros((T, T), F32)
    step_rows = []
    for k in range(4):
        scores = tables(k, bc, out_gate)
        d_scores = jnp.zeros((T, T), F32)
        for h in range(HEADS):
            i = 3 * k + h
            dec = decay(k, h, log, log_t)
            dec_step = dec * step_t[i : i + 1, :]
            weights[h] = weights[h] + scores * dec_step
            d_scores = d_scores + pair[h] * dec_step
            d_step = pair[h] * dec * scores
            step_rows.append(jnp.sum(d_step, axis=0, keepdims=True))
            rows = jnp.sum(d_step * step_t[i : i + 1, :], axis=1, keepdims=True)
            row_sums = jnp.where(lane1 == i, rows, row_sums)
        d_out = d_out + fine(d_scores, jnp.where(lane16 == k, bc, 0.0))
        d_in = d_in + fine(d_scores, jnp.where(lane16 == k, out_gate, 0.0), 0, 0)
        state = state_in(k, (s0_ref, s1_ref), wide_ref)
        expg = by_head(exp_log, k) * gw
        carried = fine(spread_states(out_gate, k), state)
        row_sums = row_sums + head_sum(carried * expg, k)
        d_out = d_out + gather_states(fine(expg, state, 1, 1), k)
    d_step = jnp.concatenate(step_rows + [jnp.zeros((T - 12, T), F32)], axis=0).T
    back_ref[:, 0:192] = per_head(lambda h: fine(weights[h], g, 0, 0))
    back_ref[:, 192:256] = jnp.zeros((T, 64), F32)
    back_ref[:, 256:384] = d_in + pltpu.roll(d_out, 64, 1)
    back_ref[:, 384:512] = jnp.where(lane1 < 64, d_step, pltpu.roll(row_sums - step * d_step, 64, 1))


def gate_grads_kernel(
    me_ref, got_ref, tok_ref, dgate_ref, gated_ref, cot_ref, side_ref, shifts_ref, near_ref
):
    fill_blocks(me_ref[0], got_ref, near_ref, lambda x: x.astype(F32))
    for b in range(3):
        near = near_ref[:, 7 + b : 7 + b + C, :]
        for a in range(3):
            i = 3 * a + b
            shifts_ref[D * i : D * i + D, :] = near[a : a + R].reshape(T, D).T.astype(BF)
    side_ref[:D, :] = dot(tok_ref[...], dgate_ref[...], 0, 0)
    side_ref[D:, :] = dot(cot_ref[...], gated_ref[...], 0, 0)


def last_kernel(
    me_ref, pad_ref, shifts_ref, vec_ref, act_ref, bc_ref, step_ref, log_ref, tot_ref, g_ref,
    sv_ref, s0_ref, s1_ref, lv_ref, p0_ref, p1_ref, p2_ref, p3_ref, later_ref, back_ref, wd_ref,
    wbc_ref, side_ref, norms_ref,
    gb_ref, pack_ref, early_ref, late_ref, l0_ref, l1_ref, blocks_ref,
):
    for i, pair_ref in enumerate((p0_ref, p1_ref, p2_ref, p3_ref)):
        blocks_ref[2 * i : 2 * i + 2] = pair_ref[...]
    row_back(me_ref[0], blocks_ref, later_ref, (l0_ref, l1_ref))
    open_message(sv_ref, early_ref)
    open_message(lv_ref, late_ref)
    step, log, tot, bc = (step_ref[...], log_ref[...], tot_ref[...], bc_ref[...])
    act = act_ref[...]
    wide = act.astype(F32)
    g = g_ref[...].astype(F32)
    d_act = back_ref[:, 0:192] + vec_ref[SKIP, :] * g
    d_bc = back_ref[:, 256:384]
    d_mix = back_ref[:, 384:512]
    to_end = jnp.exp(tot - log)
    weight = to_end * step
    through = jnp.exp(tot)
    inner = jnp.zeros((T, T), F32)
    cross = jnp.zeros((T, T), F32)
    for k in range(4):
        later = state_in(k, (l0_ref, l1_ref), late_ref)
        earlier = state_in(k, (s0_ref, s1_ref), early_ref)
        reach = fine(spread_states(bc, k), later)
        wk = by_head(weight, k)
        d_act = d_act + wk * reach
        inner = inner + head_sum(wide * reach, k)
        d_bc = d_bc + gather_states(fine(wk * wide, later, 1, 1), k)
        cross = cross + fine(ones(on_line(k)), head_sum(later * earlier, k))
    d_step = d_mix + to_end * inner
    left = weight * inner
    d_log = pltpu.roll(d_mix, 64, 1)
    parts = []
    for k in range(4):
        after = mask(k ^ 1)
        rest = same_line(k >= 2) & jnp.logical_not(after)
        parts.append(fine(ones(after), d_log) + fine(ones(rest), left))
    d_log_step = pick_lanes(parts) + cross * through
    rate = -jnp.exp(vec_ref[RATE, :T])
    d_rate = jnp.sum(d_log_step * step, axis=0, keepdims=True) * rate
    small = step * (1.0 - 0.5 * step + step * step / 6.0)
    d_raw = (d_step + rate * d_log_step) * jnp.where(step < 0.01, small, 1.0 - jnp.exp(-step))
    live = iota((T, T), 1) < 12
    d_raw = jnp.where(live, d_raw, 0.0)
    d_bias = jnp.sum(d_raw, axis=0, keepdims=True)
    d_raw = d_raw.astype(BF)
    d_bc = d_bc.astype(BF)
    d_act = d_act + dot(d_raw, wd_ref[...], 1, 1) + dot(d_bc, wbc_ref[...], 1, 1)
    near = [pad_ref[:, 7 + b : 7 + b + C, :] for b in range(3)]
    near = [near[i % 3][i // 3 : i // 3 + R].reshape(T, DI) for i in range(9)]
    before = jnp.zeros((T, DI), F32) + vec_ref[BIAS, :]
    for i in range(9):
        before = before + vec_ref[i : i + 1, :] * near[i]
    sig = sigmoid(before)
    gb = (d_act * sig * (1.0 + before * (1.0 - sig))).astype(BF)
    gb_ref[...] = gb
    gbw = gb.astype(F32)
    product = dot(shifts_ref[...], gb)
    gin = jnp.zeros((D, DI), F32)
    conv_rows = [jnp.sum(gbw * near[i], axis=0, keepdims=True) for i in range(9)]
    for i in range(9):
        gin = gin + vec_ref[i : i + 1, :] * product[D * i : D * i + D]
    wide_row = lambda x: jnp.concatenate([x, jnp.zeros((1, DI - T), F32)], axis=1)
    small = jnp.concatenate(
        conv_rows
        + [
            jnp.sum(gbw, axis=0, keepdims=True),
            jnp.sum(g * wide, axis=0, keepdims=True),
            norms_ref[0:1, :],
            norms_ref[1:2, :],
            wide_row(d_bias),
            wide_row(jnp.where(live[:1], d_rate, 0.0)),
            jnp.zeros((1, DI), F32),
        ],
        axis=0,
    )
    both = [
        gin, side_ref[...], small, dot(d_bc, act, 0, 0),
        dot(d_raw, act, 0, 0)[:16],
    ]
    full = jnp.concatenate(both, axis=0)
    rest = small - small.astype(BF).astype(F32)
    pack_ref[0:448, :] = full[:, :128].astype(BF)
    pack_ref[448:672, :] = jnp.concatenate([full[:224, 128:], full[224:, 128:]], axis=1).astype(BF)
    pack_ref[672:688, :] = rest[:, :128].astype(BF)
    pack_ref[688:704, :] = jnp.concatenate(
        [rest[:, 128:], jnp.zeros((16, 64), F32)], axis=1
    ).astype(BF)
    pack_ref[704:1024, :] = jnp.zeros((320, T), BF)


def out_kernel(
    above_ref, own_ref, below_ref, left_ref, right_ref, cw_ref, dgate_ref, wbr_ref, wg_ref,
    out_ref, pad_ref,
):
    around = (above_ref, own_ref, below_ref, left_ref, right_ref)
    fill_rim(pad_ref, *(ref[...].astype(F32) for ref in around))
    total = jnp.zeros((R, C, DI), F32)
    for b in range(3):
        shifted = pad_ref[:, 9 - b : 9 - b + C, :]
        for a in range(3):
            total = total + cw_ref[3 * a + b : 3 * a + b + 1, :] * shifted[2 - a : 2 - a + R]
    d_branch = total.reshape(T, DI).astype(BF)
    out_ref[...] = (
        dot(d_branch, wbr_ref[...], 1, 1) + dot(dgate_ref[...], wg_ref[...], 1, 1)
    ).astype(BF)


def sum_kernel(scale, x_ref, out_ref):
    total = x_ref[0].astype(F32)
    for i in range(1, x_ref.shape[0]):
        total = total + x_ref[i].astype(F32)
    out_ref[...] = jnp.broadcast_to((total * scale).astype(out_ref.dtype), out_ref.shape)


def unpack_kernel(
    x_ref, gin_ref, conv_ref, cb_ref, scan_ref, sb_ref, ld_ref, skip_ref, gain_ref, nb_ref, gout_ref
):
    low, high = (x_ref[0:448, :].astype(F32), x_ref[448:672, :].astype(F32))
    full = jnp.concatenate(
        [low, jnp.concatenate([high[:, :64], high[:, 64:]], axis=0)], axis=1
    )
    rest = jnp.concatenate([x_ref[672:688, :], x_ref[688:704, :64]], axis=1).astype(F32)
    gin_ref[...] = jnp.concatenate([full[:96], full[96:192]], axis=1)
    gout_ref[...] = full[192:288].T
    small = full[288:304] + rest
    for a in range(3):
        conv_ref[a] = small[3 * a : 3 * a + 3]
    cb_ref[...] = small[9:10]
    skip_ref[...] = jnp.broadcast_to(small[10:11], (4, DI))
    gain_ref[...] = small[11:12]
    nb_ref[...] = small[12:13]
    for k in range(4):
        sb_ref[k : k + 1, :] = small[13:14, 3 * k : 3 * k + 3]
        ld_ref[k : k + 1, :] = small[14:15, 3 * k : 3 * k + 3]
    for k in range(4):
        scan_ref[0:3, k, :] = full[432 + 3 * k : 435 + 3 * k]
        scan_ref[3:19, k, :] = full[304 + 16 * k : 320 + 16 * k]
        scan_ref[19:35, k, :] = full[368 + 16 * k : 384 + 16 * k]


def call(kernel, outs, *args, flops=10**8, scratch=(), scalars=0):
    whole = pl.BlockSpec(memory_space=pltpu.VMEM)
    small = pl.BlockSpec(memory_space=pltpu.SMEM)
    return pl.pallas_call(
        kernel,
        out_shape=[jax.ShapeDtypeStruct(s, t) for s, t in outs],
        in_specs=[small] * scalars + [whole] * (len(args) - scalars),
        out_specs=[whole] * len(outs),
        scratch_shapes=list(scratch),
        compiler_params=pltpu.CompilerParams(vmem_limit_bytes=40 * 2**20),
        cost_estimate=pl.CostEstimate(flops=flops, bytes_accessed=10**6, transcendentals=0),
    )(*args)


def neighbours(last, first, axis):
    size = lax.axis_size(axis)
    up = [(i, i + 1) for i in range(size - 1)]
    down = [(j, i) for i, j in up]
    return lax.ppermute(last, axis, up), lax.ppermute(first, axis, down)


def with_rim(x):
    above, below = neighbours(x[T - C :], x[:C], "row")
    grid = x.reshape(R, C, -1)
    side = lambda c: jnp.concatenate([above[c : c + 1], grid[:, c], below[c : c + 1]], axis=0)
    left, right = neighbours(side(C - 1), side(0), "col")
    return above, x, below, left, right


def all_to_all(x, axis):
    return lax.all_to_all(x, axis, 0, 0, tiled=True)


def swapped(x, step):
    return lax.ppermute(x, "col", [(i, i ^ step) for i in range(lax.axis_size("col"))])


def in_pairs(x):
    return jnp.stack([x, swapped(x, 1)])


def along_col(pair):
    return [pair] + [swapped(pair, step) for step in range(2, lax.axis_size("col"), 2)]


def exchange(message, axis, backward, meanwhile=()):
    chunks = (64, 8, 128)
    got, meanwhile = lax.optimization_barrier(
        (all_to_all(message.reshape(chunks), axis).reshape(512, 128), meanwhile)
    )
    (states,) = call(partial(chain_kernel, backward), [((512, 128), BF)], got, flops=10**7)
    return all_to_all(states.reshape(chunks), axis).reshape(512, 128), meanwhile


def reduced(pack, scale, later):
    rows, cols = (lax.axis_size("row"), lax.axis_size("col"))
    chunk = pack.shape[0] // rows
    got = all_to_all(pack.reshape(rows, chunk, 128), "row")
    (part,) = call(partial(sum_kernel, 1.0), [((cols, chunk, 128), F32)], got, flops=10**7)
    part, later = lax.optimization_barrier((part, later))
    got = all_to_all(part, "col")
    (part,) = call(partial(sum_kernel, scale), [((rows, chunk, 128), BF)], got, flops=10**7)
    return all_to_all(part, "row").reshape(pack.shape), later


def local(
    tokens, in_weight, conv_weight, conv_bias, scan_weight, step_bias, log_decay, skip_gain, norm_gain,
    norm_bias, out_weight, cotangent,
):
    own = tokens.reshape(T, D)
    above, below = neighbours(own[T - C :], own[:C], "row")
    band = jnp.concatenate([above, own, below], axis=0)
    got = all_to_all(jnp.broadcast_to(band, (lax.axis_size("col"),) + band.shape), "col")
    place = lax.axis_index("col").reshape(1)
    cot = cotangent.reshape(T, D)
    w_branch, w_gate = (in_weight[:, :DI], in_weight[:, DI:])
    by_channel = jnp.moveaxis(scan_weight, 1, 0)
    w_step = jnp.pad(by_channel[:, :, :HEADS].reshape(DI, 12), ((0, 0), (0, 116)))
    w_bc = jnp.concatenate(
        [
            by_channel[:, :, HEADS : HEADS + NS].reshape(DI, 64),
            by_channel[:, :, HEADS + NS :].reshape(DI, 64),
        ],
        axis=1,
    )
    row = lambda x: x.reshape(1, -1)
    bias = jnp.pad(row(step_bias), ((0, 0), (0, DI - 12)))
    rate = jnp.pad(row(log_decay), ((0, 0), (0, DI - 12)))
    vec = jnp.concatenate(
        [
            conv_weight.reshape(9, DI), row(conv_bias), row(norm_gain), row(norm_bias),
            jnp.sum(skip_gain, axis=0, keepdims=True), bias, rate, jnp.zeros((1, DI), F32),
        ],
        axis=0,
    )
    square = ((T, T), F32)
    wide = ((T, DI), F32)
    low = ((T, DI), BF)
    message = ((512, 128), BF)
    opened = pltpu.VMEM((64, 8, 128), F32)
    states = ((256, DI), F32)
    long = ((8 * T, T), F32)

    act, bc, step, log, tot, mv, padded = call(
        first_kernel,
        [low, square, square, square, square, message, ((R + 2, PITCH, DI), F32)],
        place, got, w_branch, vec, w_step, w_bc, scratch=[opened], scalars=1,
    )
    sv, _ = exchange(mv, "row", False)
    s0, s1, later = call(
        row_scan_kernel, [states, states, long],
        place, got, w_branch, vec, w_step, w_bc,
        scratch=[pltpu.VMEM((R + 2, 80, DI), F32)], scalars=1, flops=10**9,
    )
    (y,) = call(local_kernel, [wide], act, bc, step, log)
    out, g, d_gate, gated, norms, mv = call(
        norm_kernel, [((T, D), BF), low, low, low, ((8, DI), F32), message],
        y, act, bc, log, tot, sv, s0, s1, vec, own, w_gate, out_weight, cot,
        scratch=[opened],
    )
    back = call(
        back_kernel, [((T, 512), F32)], act, bc, step, log, g, sv, s0, s1, scratch=[opened]
    )
    sides = call(
        gate_grads_kernel, [((2 * D, DI), F32), ((9 * D, T), BF)],
        place, got, own, d_gate, gated, cot,
        scratch=[pltpu.VMEM((R + 2, PITCH, D), F32)], scalars=1, flops=10**7,
    )
    lv, (pair, back, sides) = exchange(mv, "row", True, (in_pairs(g), back, sides))
    side, shifts = sides
    lv, blocks = lax.optimization_barrier((lv, along_col(pair)))
    gb, pack = call(
        last_kernel, [low, ((1024, 128), BF)],
        place, padded, shifts, vec, act, bc, step, log, tot, g, sv, s0, s1, lv, *blocks, later,
        *back, w_step, w_bc, side, norms,
        scratch=[opened, opened, pltpu.VMEM((256, DI), F32), pltpu.VMEM((256, DI), F32)]
        + [pltpu.VMEM((8, T, DI), BF)],
        scalars=1,
    )
    scale = float(T * lax.axis_size("row") * lax.axis_size("col")) ** (-0.5)
    total, gb = reduced(pack, scale, gb)
    rim = with_rim(gb)
    (d_tokens,) = call(
        out_kernel, [((T, D), BF)], *rim, vec, d_gate, w_branch, w_gate,
        scratch=[pltpu.VMEM((R + 2, PITCH, DI), F32)],
    )
    row_shape = ((1, DI), F32)
    gin, g_conv, g_cb, g_scan, g_bias, g_rate, g_skip, g_gain, g_shift, gout = call(
        unpack_kernel,
        [
            ((D, 2 * DI), F32), ((3, 3, DI), F32), row_shape, ((HEADS + 2 * NS, 4, DI), F32),
            ((4, HEADS), F32), ((4, HEADS), F32), ((4, DI), F32), row_shape, row_shape, ((DI, D), F32),
        ],
        total, flops=10**7,
    )
    return (
        out.reshape(R, C * D), d_tokens.reshape(R, C * D), gin, g_conv, g_cb.reshape(DI),
        jnp.transpose(g_scan, (1, 2, 0)), g_bias,
        g_rate, g_skip, g_gain.reshape(DI), g_shift.reshape(DI), gout,
    )


def solution(mesh):
    in_specs = (P("row", "col"), P(), P(), P(), P(), P(), P(), P(), P(), P(), P(), P("row", "col"))
    out_specs = (P("row", "col"), P("row", "col"), P(), P(), P(), P(), P(), P(), P(), P(), P(), P())
    return jax.shard_map(local, mesh=mesh, in_specs=in_specs, out_specs=out_specs, check_vma=False)
```

```python
from functools import partial

import jax
import jax.numpy as jnp
from jax import lax
from jax.experimental import pallas as pl
from jax.experimental.pallas import tpu as pltpu
from jax.sharding import PartitionSpec as P

D = 96
DI = 192
NS = 16
HEADS = 3
R = 16
C = 8
T = R * C
PITCH = 24
BIAS = slice(9, 10)
GAIN = slice(10, 11)
SHIFT = slice(11, 12)
SKIP = slice(12, 13)
STEP_BIAS = slice(13, 14)
RATE = slice(14, 15)

F32 = jnp.float32
BF = jnp.bfloat16
FAR = -1e30


def dot(a, b, ca=1, cb=0):
    return lax.dot_general(a, b, (((ca,), (cb,)), ((), ())), preferred_element_type=F32)


def halves(x):
    if x.dtype == BF:
        return [x]
    high = x.astype(BF)
    return [high, (x - high.astype(F32)).astype(BF)]


def fine(a, b, ca=1, cb=0):
    a, b = (halves(a), halves(b))
    out = dot(a[0], b[0], ca, cb)
    for i, j in ((0, 1), (1, 0)):
        if i < len(a) and j < len(b):
            out = out + dot(a[i], b[j], ca, cb)
    return out


def iota(shape, dim):
    return lax.broadcasted_iota(jnp.int32, shape, dim)


def mask(k):
    t, s = (iota((T, T), 0), iota((T, T), 1))
    rt, ct, rs, cs = (t >> 3, t & 7, s >> 3, s & 7)
    if k == 0:
        return (rt == rs) & (cs <= ct)
    if k == 1:
        return (rt == rs) & (cs >= ct)
    if k == 2:
        return (ct == cs) & (rs <= rt)
    return (ct == cs) & (rs >= rt)


def same_line(vertical):
    t, s = (iota((T, T), 0), iota((T, T), 1))
    return (t & 7) == (s & 7) if vertical else (t >> 3) == (s >> 3)


def pick_lanes(parts):
    lane = iota((T, T), 1) // 3
    out = parts[3]
    for k in range(3):
        out = jnp.where(lane == k, parts[k], out)
    return out


def as_f32(m):
    return jnp.where(m, 1.0, 0.0).astype(F32)


def ones(m):
    return as_f32(m).astype(BF)


def states_of(k):
    return 256 if k < 2 else 128


def line_and_entry(j, k):
    if k < 2:
        return (j >> 4, j & 15)
    return ((j >> 3) & 7, 2 * (j & 7) + (j >> 6))


def on_line(k):
    t, j = (iota((T, states_of(k)), 0), iota((T, states_of(k)), 1))
    return line_and_entry(j, k)[0] == (t >> 3 if k < 2 else t & 7)


def spread_states(bc, k):
    i, j = (iota((T, states_of(k)), 0), iota((T, states_of(k)), 1))
    wide = fine(bc, ones(i == 16 * k + line_and_entry(j, k)[1]))
    return jnp.where(on_line(k), wide, 0.0)


def gather_states(wide, k):
    j, i = (iota((states_of(k), T), 0), iota((states_of(k), T), 1))
    entry = line_and_entry(j, k)[1]
    return fine(jnp.where(on_line(k), wide, 0.0), ones(i == 16 * k + entry))


def by_head(values, k):
    lane = iota((T, DI), 1)
    a, b, c = (values[:, 3 * k + h : 3 * k + h + 1] for h in range(HEADS))
    return jnp.where(lane < 64, a, jnp.where(lane < 128, b, c))


def head_sum(wide, k):
    c, j = (iota((DI, T), 0), iota((DI, T), 1))
    return fine(wide, ones(j == 3 * k + c // 64))


def per_head(f):
    lane = iota((T, DI), 1)
    a, b, c = (f(h) for h in range(HEADS))
    return jnp.where(lane < 64, a, jnp.where(lane < 128, b, c))


def write_message(ref, wide_ref, states, totals):
    for d in range(2):
        s = states[d]
        for h in range(HEADS):
            wide_ref[:, d * 3 + h, :] = jnp.concatenate(
                [s[:64, 64 * h : 64 * h + 64], s[64:, 64 * h : 64 * h + 64]], axis=1
            )
    j, t = (iota((64, T), 0), iota((64, T), 1))
    i, o = (iota((T, T), 0), iota((T, T), 1))
    totals = fine(ones(t == (j >> 3)), fine(totals, ones(i == o + 6)))
    high = totals.astype(BF).astype(F32)
    wide_ref[:, 6, :] = high
    wide_ref[:, 7, :] = totals - high
    ref[...] = wide_ref[...].reshape(512, 128).astype(BF)


def open_message(ref, wide_ref):
    wide_ref[...] = ref[...].astype(F32).reshape(64, 8, 128)


def read_message(ref, d):
    x = [ref[:, d * 3 + h, :] for h in range(HEADS)]
    top = jnp.concatenate([v[:, :64] for v in x], axis=1)
    bottom = jnp.concatenate([v[:, 64:] for v in x], axis=1)
    return jnp.concatenate([top, bottom], axis=0)


def chain_kernel(backward, got_ref, out_ref):
    m = 512 // lax.axis_size("row")
    n = 512 // m
    got = got_ref[...].astype(F32).reshape(n, m // 8, 8, 128)
    shape = (m // 8, 8, 128)
    sub, lane = (iota(shape, 1), iota(shape, 2))
    ahead = sub < 3 if not backward else sub >= 3

    def factor(i):
        row = jnp.broadcast_to(got[i, :, 6:7, :] + got[i, :, 7:8, :], shape)
        return jnp.sum(jnp.where(lane == sub, row, 0.0), axis=2, keepdims=True)

    factors = [factor(i) for i in range(n)]
    up = [jnp.zeros(shape, F32)]
    for i in range(n - 1):
        up.append(factors[i] * up[i] + got[i])
    down = [jnp.zeros(shape, F32)]
    for i in range(n - 1, 0, -1):
        down.append(factors[i] * down[-1] + got[i])
    down = down[::-1]
    full = jnp.concatenate([jnp.where(ahead, u, v) for u, v in zip(up, down)], axis=0)
    out_ref[...] = full.reshape(512, 128).astype(BF)


def state_in(k, rows, columns):
    return rows[k][...] if k < 2 else read_message(columns, k - 2)


def sigmoid(x):
    return jax.nn.sigmoid(x)


def softplus(x):
    return jnp.maximum(x, 0.0) + jnp.log1p(jnp.exp(-jnp.abs(x)))


def fill_rim(pad_ref, above, own, below, left, right):
    pad_ref[0:1, 8:16, :] = above.reshape(1, C, -1)
    pad_ref[1 : R + 1, 8:16, :] = own.reshape(R, C, -1)
    pad_ref[R + 1 : R + 2, 8:16, :] = below.reshape(1, C, -1)
    for r in range(R + 2):
        pad_ref[r, 7:8, :] = left[r : r + 1]
        pad_ref[r, 16:17, :] = right[r : r + 1]


def edge_factor(me, blocks, j):
    return jnp.clip(j, 0, blocks - 1), jnp.where((j >= 0) & (j < blocks), 1.0, 0.0)


def fill_blocks(me, got_ref, pad_ref, f):
    for i in range(3):
        at, inside = edge_factor(me, got_ref.shape[0], me + i - 1)
        pad_ref[:, 8 * i : 8 * i + 8, :] = f(got_ref[at]).reshape(R + 2, C, -1) * inside


def as_branch(wbr_ref):
    return lambda x: dot(x, wbr_ref[...]).astype(BF).astype(F32)


def first_kernel(
    me_ref, got_ref, wbr_ref, cw_ref, wd_ref, wbc_ref,
    act_ref, bc_ref, step_ref, log_ref, tot_ref, mv_ref, pad_ref, wide_ref,
):
    fill_blocks(me_ref[0], got_ref, pad_ref, as_branch(wbr_ref))
    total = jnp.zeros((R, C, DI), F32)
    for b in range(3):
        shifted = pad_ref[:, 7 + b : 7 + b + C, :]
        for a in range(3):
            total = total + cw_ref[3 * a + b : 3 * a + b + 1, :] * shifted[a : a + R]
    before = total.reshape(T, DI) + cw_ref[BIAS, :]
    act = (before * sigmoid(before)).astype(BF)
    act_ref[...] = act
    raw_d = dot(act, wd_ref[...])
    bc = dot(act, wbc_ref[...])
    step = softplus(raw_d + cw_ref[STEP_BIAS, :T])
    log_step = step * -jnp.exp(cw_ref[RATE, :T])
    log = pick_lanes([fine(ones(mask(k)), log_step) for k in range(4)])
    rows, cols = (fine(ones(same_line(v)), log_step) for v in (False, True))
    tot = pick_lanes([rows, rows, cols, cols])
    bc_ref[...] = bc
    step_ref[...] = step
    log_ref[...] = log
    tot_ref[...] = tot
    weight = jnp.exp(tot - log) * step
    wide = act.astype(F32)
    states = [
        fine(spread_states(bc, k), by_head(weight, k) * wide, 0, 0) for k in (2, 3)
    ]
    write_message(mv_ref, wide_ref, states, jnp.exp(tot))


def row_pair(me, blocks_ref, group):
    lines = []
    for r in range(2):
        at = pl.ds(16 * group, 16)
        for j in range(8):
            lines.append(blocks_ref[me ^ j, at, :].astype(F32)[8 * r : 8 * r + 8])
    return jnp.concatenate(lines, axis=0)


def row_scan_kernel(
    me_ref, got_ref, wbr_ref, cw_ref, wd_ref, wbc_ref,
    s0_ref, s1_ref, later_ref, pad_ref,
):
    nothing = jnp.zeros((R + 2, 8, DI), F32)
    pad_ref[:, 0:8, :] = nothing
    pad_ref[:, 72:80, :] = nothing
    for j in range(8):
        pad_ref[:, 8 + 8 * j : 16 + 8 * j, :] = as_branch(wbr_ref)(got_ref[j]).reshape(R + 2, C, DI)
    low = me_ref[0] * C
    high = low + C
    t, u = (iota((T, T), 0), iota((T, T), 1))
    same = (t >> 6) == (u >> 6)
    t, u = (t & 63, u & 63)
    reach = [
        same & (u > t) & (u < low),
        same & (u < t) & (u >= high),
        same & (u <= t) & (u >= high),
        same & (u >= t) & (u < low),
    ]
    reach = jnp.concatenate([ones(m) for m in reach], axis=0)
    before, after = (t < low, t >= high)
    first = iota((T, T), 1) < 3
    valid_in = jnp.where(first, as_f32(before), as_f32(after))
    valid_out = jnp.where(first, as_f32(after), as_f32(before))
    tj, j = (iota((T, 32), 0), iota((T, 32), 1))
    line = (tj >> 6) == (j >> 4)
    i, ji = (iota((T, 32), 0), iota((T, 32), 1))
    rate = -jnp.exp(cw_ref[RATE, :T])
    for group in range(R // 2):
        total = jnp.zeros((2, 64, DI), F32)
        for b in range(3):
            shifted = pad_ref[2 * group : 2 * group + 4, 7 + b : 71 + b, :]
            for a in range(3):
                total = total + cw_ref[3 * a + b : 3 * a + b + 1, :] * shifted[a : a + 2]
        wide = total.reshape(T, DI) + cw_ref[BIAS, :]
        act = (wide * sigmoid(wide)).astype(BF)
        wide = act.astype(F32)
        step = softplus(dot(act, wd_ref[...]) + cw_ref[STEP_BIAS, :T])
        bc = dot(act, wbc_ref[...])
        x = fine(reach, step * rate)
        w_in = jnp.exp(jnp.where(first, x[:T], x[T : 2 * T])) * step * valid_in
        later = jnp.exp(jnp.where(first, x[2 * T : 3 * T], x[3 * T :])) * valid_out
        later_ref[group * T : group * T + T, :] = jnp.where(
            iota((T, T), 1) < 64, shifted_gate(bc), pltpu.roll(later, 64, 1)
        )
        for k, ref in enumerate((s0_ref, s1_ref)):
            entry = ones(i == 16 * k + (ji & 15))
            spread = jnp.where(line, fine(bc, entry), 0.0)
            ref[32 * group : 32 * group + 32, :] = fine(spread, by_head(w_in, k) * wide, 0, 0)


def row_back(me, blocks_ref, later_ref, out_refs):
    tj, j = (iota((T, 32), 0), iota((T, 32), 1))
    line = (tj >> 6) == (j >> 4)
    for group in range(R // 2):
        g = row_pair(me, blocks_ref, group)
        gate = later_ref[group * T : group * T + T, :]
        later = pltpu.roll(gate, 64, 1)
        for k, ref in enumerate(out_refs):
            entry = ones(tj == 16 * k + (j & 15))
            spread = jnp.where(line, fine(gate, entry), 0.0)
            ref[32 * group : 32 * group + 32, :] = fine(spread, by_head(later, k) * g, 0, 0)


def tables(k, bc, out_gate):
    lane = iota((T, T), 1) >> 4
    return fine(jnp.where(lane == k, out_gate, 0.0), bc, 1, 1)


def decay(k, h, log, log_t):
    i = 3 * k + h
    return jnp.exp(jnp.where(mask(k), log[:, i : i + 1] - log_t[i : i + 1, :], FAR))


def shifted_gate(bc):
    return pltpu.roll(bc, 64, 1)


def local_kernel(act_ref, bc_ref, step_ref, log_ref, y_ref):
    bc = bc_ref[...]
    out_gate = shifted_gate(bc)
    log = log_ref[...]
    log_t, step_t = (log.T, step_ref[...].T)
    weights = [jnp.zeros((T, T), F32)] * HEADS
    for k in range(4):
        scores = tables(k, bc, out_gate)
        for h in range(HEADS):
            i = 3 * k + h
            weights[h] = weights[h] + scores * (
                decay(k, h, log, log_t) * step_t[i : i + 1, :]
            )
    act = act_ref[...]
    y_ref[...] = per_head(lambda h: fine(weights[h], act))


def carry(k, out_gate, exp_log, state):
    return by_head(exp_log, k) * fine(spread_states(out_gate, k), state)


def norm_kernel(
    y_ref, act_ref, bc_ref, log_ref, tot_ref, sv_ref, s0_ref, s1_ref, vec_ref, tok_ref, wg_ref, ow_ref,
    cot_ref,
    out_ref, g_ref, dgate_ref, gated_ref, norms_ref, mv_ref, wide_ref,
):
    open_message(sv_ref, wide_ref)
    bc = bc_ref[...]
    out_gate = shifted_gate(bc)
    exp_log = jnp.exp(log_ref[...])
    gain = vec_ref[GAIN, :]
    summed = y_ref[...] + vec_ref[SKIP, :] * act_ref[...].astype(F32)
    for k in range(4):
        state = state_in(k, (s0_ref, s1_ref), wide_ref)
        summed = summed + carry(k, out_gate, exp_log, state)
    gate = dot(tok_ref[...], wg_ref[...]).astype(BF).astype(F32)
    sig = sigmoid(gate)
    center = summed - jnp.mean(summed, axis=1, keepdims=True)
    inv = lax.rsqrt(jnp.mean(center * center, axis=1, keepdims=True) + 1e-5)
    unit = center * inv
    normed = unit * gain + vec_ref[SHIFT, :]
    gated = (normed * gate * sig).astype(BF)
    gated_ref[...] = gated
    out_ref[...] = dot(gated, ow_ref[...]).astype(BF)
    grad = dot(cot_ref[...], ow_ref[...], 1, 1)
    dnormed = grad * gate * sig
    dgate_ref[...] = (grad * normed * (sig * (1.0 + gate * (1.0 - sig)))).astype(BF)
    norms_ref[0:1, :] = jnp.sum(dnormed * unit, axis=0, keepdims=True)
    norms_ref[1:2, :] = jnp.sum(dnormed, axis=0, keepdims=True)
    dunit = dnormed * gain
    g = inv * (
        dunit
        - jnp.mean(dunit, axis=1, keepdims=True)
        - unit * jnp.mean(dunit * unit, axis=1, keepdims=True)
    )
    g = g.astype(BF)
    g_ref[...] = g
    g = g.astype(F32)
    states = [
        fine(spread_states(out_gate, k), by_head(exp_log, k) * g, 0, 0) for k in (2, 3)
    ]
    write_message(mv_ref, wide_ref, states, jnp.exp(tot_ref[...]))


def back_kernel(
    act_ref, bc_ref, step_ref, log_ref, g_ref, sv_ref, s0_ref, s1_ref,
    back_ref, wide_ref,
):
    open_message(sv_ref, wide_ref)
    bc = bc_ref[...]
    out_gate = shifted_gate(bc)
    log = log_ref[...]
    step = step_ref[...]
    log_t, step_t = (log.T, step.T)
    exp_log = jnp.exp(log)
    act = act_ref[...]
    g = g_ref[...]
    gw = g.astype(F32)
    lane = iota((T, DI), 1) // 64
    lane16 = iota((T, T), 1) >> 4
    lane1 = iota((T, T), 1)
    pair = [dot(jnp.where(lane == h, g, jnp.zeros_like(g)), act, 1, 1) for h in range(HEADS)]
    weights = [jnp.zeros((T, T), F32)] * HEADS
    d_in = jnp.zeros((T, T), F32)
    d_out = jnp.zeros((T, T), F32)
    row_sums = jnp.zeros((T, T), F32)
    step_rows = []
    for k in range(4):
        scores = tables(k, bc, out_gate)
        d_scores = jnp.zeros((T, T), F32)
        for h in range(HEADS):
            i = 3 * k + h
            dec = decay(k, h, log, log_t)
            dec_step = dec * step_t[i : i + 1, :]
            weights[h] = weights[h] + scores * dec_step
            d_scores = d_scores + pair[h] * dec_step
            d_step = pair[h] * dec * scores
            step_rows.append(jnp.sum(d_step, axis=0, keepdims=True))
            rows = jnp.sum(d_step * step_t[i : i + 1, :], axis=1, keepdims=True)
            row_sums = jnp.where(lane1 == i, rows, row_sums)
        d_out = d_out + fine(d_scores, jnp.where(lane16 == k, bc, 0.0))
        d_in = d_in + fine(d_scores, jnp.where(lane16 == k, out_gate, 0.0), 0, 0)
        state = state_in(k, (s0_ref, s1_ref), wide_ref)
        expg = by_head(exp_log, k) * gw
        carried = fine(spread_states(out_gate, k), state)
        row_sums = row_sums + head_sum(carried * expg, k)
        d_out = d_out + gather_states(fine(expg, state, 1, 1), k)
    d_step = jnp.concatenate(step_rows + [jnp.zeros((T - 12, T), F32)], axis=0).T
    back_ref[:, 0:192] = per_head(lambda h: fine(weights[h], g, 0, 0))
    back_ref[:, 192:256] = jnp.zeros((T, 64), F32)
    back_ref[:, 256:384] = d_in + pltpu.roll(d_out, 64, 1)
    back_ref[:, 384:512] = jnp.where(lane1 < 64, d_step, pltpu.roll(row_sums - step * d_step, 64, 1))


def gate_grads_kernel(
    me_ref, got_ref, tok_ref, dgate_ref, gated_ref, cot_ref, side_ref, shifts_ref, near_ref
):
    fill_blocks(me_ref[0], got_ref, near_ref, lambda x: x.astype(F32))
    for b in range(3):
        near = near_ref[:, 7 + b : 7 + b + C, :]
        for a in range(3):
            i = 3 * a + b
            shifts_ref[D * i : D * i + D, :] = near[a : a + R].reshape(T, D).T.astype(BF)
    side_ref[:D, :] = dot(tok_ref[...], dgate_ref[...], 0, 0)
    side_ref[D:, :] = dot(cot_ref[...], gated_ref[...], 0, 0)


def last_kernel(
    me_ref, pad_ref, shifts_ref, vec_ref, act_ref, bc_ref, step_ref, log_ref, tot_ref, g_ref,
    sv_ref, s0_ref, s1_ref, lv_ref, p0_ref, p1_ref, p2_ref, p3_ref, later_ref, back_ref, wd_ref,
    wbc_ref, side_ref, norms_ref,
    gb_ref, pack_ref, early_ref, late_ref, l0_ref, l1_ref, blocks_ref,
):
    for i, pair_ref in enumerate((p0_ref, p1_ref, p2_ref, p3_ref)):
        blocks_ref[2 * i : 2 * i + 2] = pair_ref[...]
    row_back(me_ref[0], blocks_ref, later_ref, (l0_ref, l1_ref))
    open_message(sv_ref, early_ref)
    open_message(lv_ref, late_ref)
    step, log, tot, bc = (step_ref[...], log_ref[...], tot_ref[...], bc_ref[...])
    act = act_ref[...]
    wide = act.astype(F32)
    g = g_ref[...].astype(F32)
    d_act = back_ref[:, 0:192] + vec_ref[SKIP, :] * g
    d_bc = back_ref[:, 256:384]
    d_mix = back_ref[:, 384:512]
    to_end = jnp.exp(tot - log)
    weight = to_end * step
    through = jnp.exp(tot)
    inner = jnp.zeros((T, T), F32)
    cross = jnp.zeros((T, T), F32)
    for k in range(4):
        later = state_in(k, (l0_ref, l1_ref), late_ref)
        earlier = state_in(k, (s0_ref, s1_ref), early_ref)
        reach = fine(spread_states(bc, k), later)
        wk = by_head(weight, k)
        d_act = d_act + wk * reach
        inner = inner + head_sum(wide * reach, k)
        d_bc = d_bc + gather_states(fine(wk * wide, later, 1, 1), k)
        cross = cross + fine(ones(on_line(k)), head_sum(later * earlier, k))
    d_step = d_mix + to_end * inner
    left = weight * inner
    d_log = pltpu.roll(d_mix, 64, 1)
    parts = []
    for k in range(4):
        after = mask(k ^ 1)
        rest = same_line(k >= 2) & jnp.logical_not(after)
        parts.append(fine(ones(after), d_log) + fine(ones(rest), left))
    d_log_step = pick_lanes(parts) + cross * through
    rate = -jnp.exp(vec_ref[RATE, :T])
    d_rate = jnp.sum(d_log_step * step, axis=0, keepdims=True) * rate
    small = step * (1.0 - 0.5 * step + step * step / 6.0)
    d_raw = (d_step + rate * d_log_step) * jnp.where(step < 0.01, small, 1.0 - jnp.exp(-step))
    live = iota((T, T), 1) < 12
    d_raw = jnp.where(live, d_raw, 0.0)
    d_bias = jnp.sum(d_raw, axis=0, keepdims=True)
    d_raw = d_raw.astype(BF)
    d_bc = d_bc.astype(BF)
    d_act = d_act + dot(d_raw, wd_ref[...], 1, 1) + dot(d_bc, wbc_ref[...], 1, 1)
    near = [pad_ref[:, 7 + b : 7 + b + C, :] for b in range(3)]
    near = [near[i % 3][i // 3 : i // 3 + R].reshape(T, DI) for i in range(9)]
    before = jnp.zeros((T, DI), F32) + vec_ref[BIAS, :]
    for i in range(9):
        before = before + vec_ref[i : i + 1, :] * near[i]
    sig = sigmoid(before)
    gb = (d_act * sig * (1.0 + before * (1.0 - sig))).astype(BF)
    gb_ref[...] = gb
    gbw = gb.astype(F32)
    product = dot(shifts_ref[...], gb)
    gin = jnp.zeros((D, DI), F32)
    conv_rows = [jnp.sum(gbw * near[i], axis=0, keepdims=True) for i in range(9)]
    for i in range(9):
        gin = gin + vec_ref[i : i + 1, :] * product[D * i : D * i + D]
    wide_row = lambda x: jnp.concatenate([x, jnp.zeros((1, DI - T), F32)], axis=1)
    small = jnp.concatenate(
        conv_rows
        + [
            jnp.sum(gbw, axis=0, keepdims=True),
            jnp.sum(g * wide, axis=0, keepdims=True),
            norms_ref[0:1, :],
            norms_ref[1:2, :],
            wide_row(d_bias),
            wide_row(jnp.where(live[:1], d_rate, 0.0)),
            jnp.zeros((1, DI), F32),
        ],
        axis=0,
    )
    both = [
        gin, side_ref[...], small, dot(d_bc, act, 0, 0),
        dot(d_raw, act, 0, 0)[:16],
    ]
    full = jnp.concatenate(both, axis=0)
    rest = small - small.astype(BF).astype(F32)
    pack_ref[0:448, :] = full[:, :128].astype(BF)
    pack_ref[448:672, :] = jnp.concatenate([full[:224, 128:], full[224:, 128:]], axis=1).astype(BF)
    pack_ref[672:688, :] = rest[:, :128].astype(BF)
    pack_ref[688:704, :] = jnp.concatenate(
        [rest[:, 128:], jnp.zeros((16, 64), F32)], axis=1
    ).astype(BF)
    pack_ref[704:1024, :] = jnp.zeros((320, T), BF)


def out_kernel(
    above_ref, own_ref, below_ref, left_ref, right_ref, cw_ref, dgate_ref, wbr_ref, wg_ref,
    out_ref, pad_ref,
):
    around = (above_ref, own_ref, below_ref, left_ref, right_ref)
    fill_rim(pad_ref, *(ref[...].astype(F32) for ref in around))
    total = jnp.zeros((R, C, DI), F32)
    for b in range(3):
        shifted = pad_ref[:, 9 - b : 9 - b + C, :]
        for a in range(3):
            total = total + cw_ref[3 * a + b : 3 * a + b + 1, :] * shifted[2 - a : 2 - a + R]
    d_branch = total.reshape(T, DI).astype(BF)
    out_ref[...] = (
        dot(d_branch, wbr_ref[...], 1, 1) + dot(dgate_ref[...], wg_ref[...], 1, 1)
    ).astype(BF)


def sum_kernel(scale, x_ref, out_ref):
    total = x_ref[0].astype(F32)
    for i in range(1, x_ref.shape[0]):
        total = total + x_ref[i].astype(F32)
    out_ref[...] = jnp.broadcast_to((total * scale).astype(out_ref.dtype), out_ref.shape)


def unpack_kernel(
    x_ref, gin_ref, conv_ref, cb_ref, scan_ref, sb_ref, ld_ref, skip_ref, gain_ref, nb_ref, gout_ref
):
    low, high = (x_ref[0:448, :].astype(F32), x_ref[448:672, :].astype(F32))
    full = jnp.concatenate(
        [low, jnp.concatenate([high[:, :64], high[:, 64:]], axis=0)], axis=1
    )
    rest = jnp.concatenate([x_ref[672:688, :], x_ref[688:704, :64]], axis=1).astype(F32)
    gin_ref[...] = jnp.concatenate([full[:96], full[96:192]], axis=1)
    gout_ref[...] = full[192:288].T
    small = full[288:304] + rest
    for a in range(3):
        conv_ref[a] = small[3 * a : 3 * a + 3]
    cb_ref[...] = small[9:10]
    skip_ref[...] = jnp.broadcast_to(small[10:11], (4, DI))
    gain_ref[...] = small[11:12]
    nb_ref[...] = small[12:13]
    for k in range(4):
        sb_ref[k : k + 1, :] = small[13:14, 3 * k : 3 * k + 3]
        ld_ref[k : k + 1, :] = small[14:15, 3 * k : 3 * k + 3]
    for k in range(4):
        scan_ref[0:3, k, :] = full[432 + 3 * k : 435 + 3 * k]
        scan_ref[3:19, k, :] = full[304 + 16 * k : 320 + 16 * k]
        scan_ref[19:35, k, :] = full[368 + 16 * k : 384 + 16 * k]


def call(kernel, outs, *args, flops=10**8, scratch=(), scalars=0):
    whole = pl.BlockSpec(memory_space=pltpu.VMEM)
    small = pl.BlockSpec(memory_space=pltpu.SMEM)
    return pl.pallas_call(
        kernel,
        out_shape=[jax.ShapeDtypeStruct(s, t) for s, t in outs],
        in_specs=[small] * scalars + [whole] * (len(args) - scalars),
        out_specs=[whole] * len(outs),
        scratch_shapes=list(scratch),
        compiler_params=pltpu.CompilerParams(vmem_limit_bytes=40 * 2**20),
        cost_estimate=pl.CostEstimate(flops=flops, bytes_accessed=10**6, transcendentals=0),
    )(*args)


def neighbours(last, first, axis):
    size = lax.axis_size(axis)
    up = [(i, i + 1) for i in range(size - 1)]
    down = [(j, i) for i, j in up]
    return lax.ppermute(last, axis, up), lax.ppermute(first, axis, down)


def with_rim(x):
    above, below = neighbours(x[T - C :], x[:C], "row")
    grid = x.reshape(R, C, -1)
    side = lambda c: jnp.concatenate([above[c : c + 1], grid[:, c], below[c : c + 1]], axis=0)
    left, right = neighbours(side(C - 1), side(0), "col")
    return above, x, below, left, right


def all_to_all(x, axis):
    return lax.all_to_all(x, axis, 0, 0, tiled=True)


def swapped(x, step):
    return lax.ppermute(x, "col", [(i, i ^ step) for i in range(lax.axis_size("col"))])


def in_pairs(x):
    return jnp.stack([x, swapped(x, 1)])


def along_col(pair):
    return [pair] + [swapped(pair, step) for step in range(2, lax.axis_size("col"), 2)]


def exchange(message, axis, backward, meanwhile=()):
    chunks = (64, 8, 128)
    got, meanwhile = lax.optimization_barrier(
        (all_to_all(message.reshape(chunks), axis).reshape(512, 128), meanwhile)
    )
    (states,) = call(partial(chain_kernel, backward), [((512, 128), BF)], got, flops=10**7)
    return all_to_all(states.reshape(chunks), axis).reshape(512, 128), meanwhile


def reduced(pack, scale, later):
    rows, cols = (lax.axis_size("row"), lax.axis_size("col"))
    chunk = pack.shape[0] // rows
    got = all_to_all(pack.reshape(rows, chunk, 128), "row")
    (part,) = call(partial(sum_kernel, 1.0), [((cols, chunk, 128), BF)], got, flops=10**7)
    part, later = lax.optimization_barrier((part, later))
    got = all_to_all(part, "col")
    (part,) = call(partial(sum_kernel, scale), [((rows, chunk, 128), BF)], got, flops=10**7)
    return all_to_all(part, "row").reshape(pack.shape), later


def local(
    tokens, in_weight, conv_weight, conv_bias, scan_weight, step_bias, log_decay, skip_gain, norm_gain,
    norm_bias, out_weight, cotangent,
):
    own = tokens.reshape(T, D)
    above, below = neighbours(own[T - C :], own[:C], "row")
    band = jnp.concatenate([above, own, below], axis=0)
    got = all_to_all(jnp.broadcast_to(band, (lax.axis_size("col"),) + band.shape), "col")
    place = lax.axis_index("col").reshape(1)
    cot = cotangent.reshape(T, D)
    w_branch, w_gate = (in_weight[:, :DI], in_weight[:, DI:])
    by_channel = jnp.moveaxis(scan_weight, 1, 0)
    w_step = jnp.pad(by_channel[:, :, :HEADS].reshape(DI, 12), ((0, 0), (0, 116)))
    w_bc = jnp.concatenate(
        [
            by_channel[:, :, HEADS : HEADS + NS].reshape(DI, 64),
            by_channel[:, :, HEADS + NS :].reshape(DI, 64),
        ],
        axis=1,
    )
    row = lambda x: x.reshape(1, -1)
    bias = jnp.pad(row(step_bias), ((0, 0), (0, DI - 12)))
    rate = jnp.pad(row(log_decay), ((0, 0), (0, DI - 12)))
    vec = jnp.concatenate(
        [
            conv_weight.reshape(9, DI), row(conv_bias), row(norm_gain), row(norm_bias),
            jnp.sum(skip_gain, axis=0, keepdims=True), bias, rate, jnp.zeros((1, DI), F32),
        ],
        axis=0,
    )
    square = ((T, T), F32)
    wide = ((T, DI), F32)
    low = ((T, DI), BF)
    message = ((512, 128), BF)
    opened = pltpu.VMEM((64, 8, 128), F32)
    states = ((256, DI), F32)
    long = ((8 * T, T), F32)

    act, bc, step, log, tot, mv, padded = call(
        first_kernel,
        [low, square, square, square, square, message, ((R + 2, PITCH, DI), F32)],
        place, got, w_branch, vec, w_step, w_bc, scratch=[opened], scalars=1,
    )
    sv, _ = exchange(mv, "row", False)
    s0, s1, later = call(
        row_scan_kernel, [states, states, long],
        place, got, w_branch, vec, w_step, w_bc,
        scratch=[pltpu.VMEM((R + 2, 80, DI), F32)], scalars=1, flops=10**9,
    )
    (y,) = call(local_kernel, [wide], act, bc, step, log)
    out, g, d_gate, gated, norms, mv = call(
        norm_kernel, [((T, D), BF), low, low, low, ((8, DI), F32), message],
        y, act, bc, log, tot, sv, s0, s1, vec, own, w_gate, out_weight, cot,
        scratch=[opened],
    )
    back = call(
        back_kernel, [((T, 512), F32)], act, bc, step, log, g, sv, s0, s1, scratch=[opened]
    )
    sides = call(
        gate_grads_kernel, [((2 * D, DI), F32), ((9 * D, T), BF)],
        place, got, own, d_gate, gated, cot,
        scratch=[pltpu.VMEM((R + 2, PITCH, D), F32)], scalars=1, flops=10**7,
    )
    lv, (pair, back, sides) = exchange(mv, "row", True, (in_pairs(g), back, sides))
    side, shifts = sides
    lv, blocks = lax.optimization_barrier((lv, along_col(pair)))
    gb, pack = call(
        last_kernel, [low, ((1024, 128), BF)],
        place, padded, shifts, vec, act, bc, step, log, tot, g, sv, s0, s1, lv, *blocks, later,
        *back, w_step, w_bc, side, norms,
        scratch=[opened, opened, pltpu.VMEM((256, DI), F32), pltpu.VMEM((256, DI), F32)]
        + [pltpu.VMEM((8, T, DI), BF)],
        scalars=1,
    )
    scale = float(T * lax.axis_size("row") * lax.axis_size("col")) ** (-0.5)
    total, gb = reduced(pack, scale, gb)
    rim = with_rim(gb)
    (d_tokens,) = call(
        out_kernel, [((T, D), BF)], *rim, vec, d_gate, w_branch, w_gate,
        scratch=[pltpu.VMEM((R + 2, PITCH, DI), F32)],
    )
    row_shape = ((1, DI), F32)
    gin, g_conv, g_cb, g_scan, g_bias, g_rate, g_skip, g_gain, g_shift, gout = call(
        unpack_kernel,
        [
            ((D, 2 * DI), F32), ((3, 3, DI), F32), row_shape, ((HEADS + 2 * NS, 4, DI), F32),
            ((4, HEADS), F32), ((4, HEADS), F32), ((4, DI), F32), row_shape, row_shape, ((DI, D), F32),
        ],
        total, flops=10**7,
    )
    return (
        out.reshape(R, C * D), d_tokens.reshape(R, C * D), gin, g_conv, g_cb.reshape(DI),
        jnp.transpose(g_scan, (1, 2, 0)), g_bias,
        g_rate, g_skip, g_gain.reshape(DI), g_shift.reshape(DI), gout,
    )


def solution(mesh):
    in_specs = (P("row", "col"), P(), P(), P(), P(), P(), P(), P(), P(), P(), P(), P("row", "col"))
    out_specs = (P("row", "col"), P("row", "col"), P(), P(), P(), P(), P(), P(), P(), P(), P(), P())
    return jax.shard_map(local, mesh=mesh, in_specs=in_specs, out_specs=out_specs, check_vma=False)
```
